256 devices in a mesh: clip: 8 (over y_lo, x), tm: 32 (over z, y_hi, core).
Axes of the slice: x: 4, y: 4 (y_hi: 2, y_lo: 2; y = y_hi * 2 + y_lo), z: 8, core: 2. Of those that a mesh axis runs over, the one named last changes fastest.
Arguments:
- frames: bfloat16 [65536, 1024], P(('clip', 'tm')), parts along dimension 0, may hold values from -12 to 12
- conv_weight: float32 [5, 1024], replicated, may hold values from -2.8 to 2.8
- qkv_weight: bfloat16 [1024, 3072], replicated, may hold values from -0.1875 to 0.1875
- out_weight: bfloat16 [1024, 1024], replicated, may hold values from -0.1875 to 0.1875
- cotangent: bfloat16 [65536, 1024], P(('clip', 'tm')), parts along dimension 0, may hold values from -1.5 to 1.5
Outputs:
- mixed: bfloat16 [65536, 1024], P(('clip', 'tm')), parts along dimension 0
- x_grad: bfloat16 [65536, 1024], P(('clip', 'tm')), parts along dimension 0
- qkv_weight_grad: float32 [8192, 3072], P(('clip', 'tm')), parts along dimension 0
- out_weight_grad: float32 [8192, 1024], P(('clip', 'tm')), parts along dimension 0
- conv_weight_grad: float32 [40, 1024], P('clip'), parts along dimension 0
The draws below stay inside these ranges and needn't reach their ends.
There are 8 independent parts, one for each index of `clip`. The reference program is written for one: setup_inputs(seed, part) draws one part's arguments, and reference() takes and returns one part's arrays. A program takes and returns all parts, laid end to end along the dimension named above; an argument that names none is the same for every part. Nothing has to cross between parts.
All inputs are finite; a program needn't handle non-finite values.
Results may differ from the reference program's by a relative error of at most 0.012.
The reference program's roundings to bfloat16 on the way count: a program that leaves them out, or rounds other values in their place, can miss the bound.
Values may be sent and summed in bfloat16 or wider, within the bound.
No kernel may reach another device: no remote copies, remote signals or barrier semaphores. Data moves between devices by JAX's collectives and lax.ppermute only.
A program may use at most 128 MiB of HBM per device.

```python
import jax
import jax.numpy as jnp
from jax import lax

D = 1024
HEADS = 8
HEAD_DIM = 128
TAPS = 5
GAP = 2
STRIDE = 8
TOKENS = 8192


def draw_frames(key, part):
    key = jax.random.fold_in(key, 11)
    normal_draw = jnp.clip(jax.random.normal(key, (TOKENS, D), jnp.float32), -6.0, 6.0)
    return normal_draw.astype(jnp.bfloat16)


def shard_levels(rng, dims, pieces, smallest, high):
    gain, own = 1.0, jax.random.fold_in(rng, 6)
    for dim, blocks in pieces:
        heights = jnp.exp(jax.random.uniform(jax.random.fold_in(own, dim), (blocks,), jnp.float32, smallest / len(pieces), high / len(pieces)))
        gain = gain * jnp.repeat(heights, dims[dim] // blocks).reshape([-1 if axis == dim else 1 for axis in range(len(dims))])
    return gain


def bell_draw(own_key, extent, deviation, most, cuts=(), dtype=jnp.bfloat16):
    entries = deviation * jax.random.normal(own_key, extent, jnp.float32)
    if cuts:
        entries = entries * shard_levels(own_key, extent, cuts, -0.22, 0.18)
    return jnp.clip(entries, -most, most).astype(dtype)


def setup_inputs(seed: int = 0, part: int = 0) -> dict:
    key_list = jax.random.split(jax.random.key(seed), 6)
    part_keys = jax.random.split(jax.random.fold_in(key_list[5], part), 6)
    return {
        "frames": draw_frames(jax.random.fold_in(jax.random.fold_in(key_list[5], part), 71), part),
        "conv_weight": bell_draw(key_list[1], (TAPS, D), 0.7, 2.8, (), jnp.float32),
        "qkv_weight": bell_draw(key_list[2], (D, 3 * D), D ** -0.5, 0.1875),
        "out_weight": bell_draw(key_list[3], (D, D), D ** -0.5, 0.1875),
        "cotangent": bell_draw(part_keys[4], (TOKENS, D), 0.25, 1.5, ((0, 32),)),
    }


def split_heads(matrix):
    return matrix.reshape(matrix.shape[0], HEADS, HEAD_DIM).transpose(1, 0, 2)


def merge_heads(stacked):
    return stacked.transpose(1, 0, 2).reshape(stacked.shape[1], D)


def reference(frames, conv_weight, qkv_weight, out_weight, cotangent):
    conv_reach = GAP * (TAPS // 2)
    score_scale = 1.0 / (HEAD_DIM ** 0.5)
    padded = jnp.pad(frames.astype(jnp.float32), ((conv_reach, conv_reach), (0, 0)))
    total = jnp.zeros((TOKENS, D), jnp.float32)
    for tap_index in range(TAPS):
        total = total + conv_weight[tap_index] * padded[GAP * tap_index:GAP * tap_index + TOKENS]
    conv_out = total.astype(jnp.bfloat16)
    projected = jnp.dot(conv_out, qkv_weight, preferred_element_type=jnp.float32).astype(jnp.bfloat16)
    queries = projected[:, :D]
    panel_keys = projected[::STRIDE, D:2 * D]
    panel_values = projected[::STRIDE, 2 * D:]
    grad_attended = jnp.dot(cotangent, out_weight.T, preferred_element_type=jnp.float32).astype(jnp.bfloat16)

    def one_head(operands):
        query_head, key_head, value_head, grad_head = operands
        scores = jnp.dot(query_head, key_head.T, preferred_element_type=jnp.float32) * score_scale
        highest = jnp.max(scores, axis=-1, keepdims=True)
        raised = jnp.exp(scores - highest)
        probs = raised / jnp.sum(raised, axis=-1, keepdims=True)
        weights = probs.astype(jnp.bfloat16)
        attended = jnp.dot(weights, value_head, preferred_element_type=jnp.float32).astype(jnp.bfloat16)
        dprob = jnp.dot(grad_head, value_head.T, preferred_element_type=jnp.float32)
        delta = jnp.sum(grad_head.astype(jnp.float32) * attended.astype(jnp.float32), axis=-1, keepdims=True)
        grad_scores = (probs * (dprob - delta)).astype(jnp.bfloat16)
        grad_queries = (jnp.dot(grad_scores, key_head, preferred_element_type=jnp.float32) * score_scale).astype(jnp.bfloat16)
        grad_keys = jnp.dot(grad_scores.T, query_head, preferred_element_type=jnp.float32) * score_scale
        grad_values = jnp.dot(weights.T, grad_head, preferred_element_type=jnp.float32)
        return attended, grad_queries, grad_keys, grad_values

    head_att, head_gq, head_gk, head_gv = lax.map(one_head, (split_heads(queries), split_heads(panel_keys), split_heads(panel_values), split_heads(grad_attended)))
    attended = merge_heads(head_att)
    grad_queries = merge_heads(head_gq)
    grad_panel_keys = merge_heads(head_gk).astype(jnp.bfloat16)
    grad_panel_values = merge_heads(head_gv).astype(jnp.bfloat16)
    mixed = jnp.dot(attended, out_weight, preferred_element_type=jnp.float32).astype(jnp.bfloat16)
    grad_keys = jnp.zeros((TOKENS, D), jnp.bfloat16).at[::STRIDE].set(grad_panel_keys)
    grad_values = jnp.zeros((TOKENS, D), jnp.bfloat16).at[::STRIDE].set(grad_panel_values)
    grad_projected = jnp.concatenate([grad_queries, grad_keys, grad_values], axis=1)
    qkv_weight_grad = jnp.dot(conv_out.T, grad_projected, preferred_element_type=jnp.float32)
    out_weight_grad = jnp.dot(attended.T, cotangent, preferred_element_type=jnp.float32)
    grad_conv = jnp.dot(grad_projected, qkv_weight.T, preferred_element_type=jnp.float32).astype(jnp.bfloat16)
    grad_padded = jnp.pad(grad_conv.astype(jnp.float32), ((conv_reach, conv_reach), (0, 0)))
    x_total = jnp.zeros((TOKENS, D), jnp.float32)
    tap_sums = []
    for tap_index in range(TAPS):
        begin = 2 * conv_reach - GAP * tap_index
        x_total = x_total + conv_weight[tap_index] * grad_padded[begin:begin + TOKENS]
        tap_sums.append(jnp.sum(grad_conv.astype(jnp.float32) * padded[GAP * tap_index:GAP * tap_index + TOKENS], axis=0))
    x_grad = x_total.astype(jnp.bfloat16)
    conv_weight_grad = jnp.stack(tap_sums, axis=0)
    return mixed, x_grad, qkv_weight_grad, out_weight_grad, conv_weight_grad
```

```python
import jax
import jax.numpy as jnp
from jax import lax
from jax.experimental import pallas as pl
from jax.experimental.pallas import tpu as pltpu
from jax.sharding import Mesh
from jax.sharding import PartitionSpec as P

D = 1024
HEADS = 8
HEAD_DIM = 128
TAPS = 5
GAP = 2
STRIDE = 8
REACH = GAP * (TAPS // 2)
EDGE = 16
CORES = 2
PLANES = 2
OWN = HEADS // CORES
HALF = OWN * HEAD_DIM
SCALE = 1.0 / HEAD_DIM**0.5
LOG2E = 1.4426950408889634
TALL = ("z", "y", "core")
SWAP = [(0, 1), (1, 0)]

NN = (((1,), (0,)), ((), ()))
NT = (((1,), (1,)), ((), ()))
TN = (((0,), (0,)), ((), ()))


def mm(a, b, dims=NN):
    return lax.dot_general(a, b, dims, preferred_element_type=jnp.float32)


def params(mib):
    return pltpu.CompilerParams(vmem_limit_bytes=mib * 1024 * 1024)


def whole(shape):
    return pl.BlockSpec(shape, lambda *_: (0,) * len(shape))


def conv_kernel(frames, low, high, weight, conv_out, conv_panel, framed, total):
    rows = frames.shape[0]
    framed[:EDGE] = low[...].astype(jnp.float32)
    framed[EDGE : EDGE + rows] = frames[...].astype(jnp.float32)
    framed[EDGE + rows :] = high[...].astype(jnp.float32)
    acc = None
    for tap in range(TAPS):
        start = EDGE - REACH + GAP * tap
        term = weight[tap : tap + 1, :] * framed[start : start + rows, :]
        acc = term if acc is None else acc + term
    conv_out[...] = acc.astype(jnp.bfloat16)
    for chunk in range(D // HEAD_DIM):
        cols = slice(chunk * HEAD_DIM, (chunk + 1) * HEAD_DIM)
        total[chunk] = acc[:, cols]
        picked = total[chunk, pl.ds(0, rows // STRIDE, stride=STRIDE), :]
        conv_panel[:, cols] = picked.astype(jnp.bfloat16)


def conv(frames, low, high, weight):
    rows = frames.shape[0]
    return pl.pallas_call(
        conv_kernel,
        out_shape=(
            jax.ShapeDtypeStruct((rows, D), jnp.bfloat16),
            jax.ShapeDtypeStruct((rows // STRIDE, D), jnp.bfloat16),
        ),
        scratch_shapes=[
            pltpu.VMEM((rows + 2 * EDGE, D), jnp.float32),
            pltpu.VMEM((D // HEAD_DIM, rows, HEAD_DIM), jnp.float32),
        ],
        compiler_params=params(32),
        name="conv",
    )(frames, low, high, weight)


def attention_kernel(
    core, queries, grads, panel_own, panel_other, key_weight, value_weight, att, gq, mine, theirs, acck, accv
):
    del core
    half = panel_own.shape[0]
    weight = jnp.concatenate([key_weight[...], value_weight[...]], axis=1)
    own = mm(panel_own[...], weight).astype(jnp.bfloat16)
    other = mm(panel_other[...], weight).astype(jnp.bfloat16)
    both = jnp.concatenate([own, other], axis=0)
    keys, values = both[:, :HEAD_DIM], both[:, HEAD_DIM:]
    tokens = queries.shape[0]
    step = 256
    for begin in range(0, tokens, step):
        rows = slice(begin, begin + step)
        query, grad = queries[rows, :], grads[rows, :]
        scores = mm(keys, query, NT)
        highest = jnp.max(scores, axis=0, keepdims=True)
        raised = jnp.exp2((scores - highest) * (SCALE * LOG2E))
        probs = raised * (1.0 / jnp.sum(raised, axis=0, keepdims=True))
        weights = probs.astype(jnp.bfloat16)
        attended = mm(values, weights, TN).astype(jnp.bfloat16)
        grad_t = grad.astype(jnp.float32).T
        delta = jnp.sum(grad_t * attended.astype(jnp.float32), axis=0, keepdims=True)
        dprob = mm(values, grad, NT)
        grad_scores = (probs * (dprob - delta)).astype(jnp.bfloat16)
        att[rows, :] = attended.astype(jnp.float32).T.astype(jnp.bfloat16)
        gq[rows, :] = (mm(keys, grad_scores, TN) * SCALE).T.astype(jnp.bfloat16)
        part_k = mm(grad_scores, query)
        part_v = mm(weights, grad)
        if begin == 0:
            acck[...] = part_k
            accv[...] = part_v
        else:
            acck[...] += part_k
            accv[...] += part_v
    depth, piece = mine.shape[0], mine.shape[2]
    for lane in range(CORES):
        for z in range(depth):
            row = lane * half + z * PLANES * piece
            for out, at in ((mine, row), (theirs, row + piece)):
                out[z, lane, :, :HEAD_DIM] = (acck[at : at + piece, :] * SCALE).astype(jnp.bfloat16)
                out[z, lane, :, HEAD_DIM:] = accv[at : at + piece, :].astype(jnp.bfloat16)


def attention(core, queries, grads, panel_own, panel_other, qkv_weight, depth):
    tokens = queries.shape[0]
    half = panel_own.shape[0]
    piece = half // depth // PLANES
    head = pl.BlockSpec((tokens, HEAD_DIM), lambda h, core: (0, h))
    panel = whole((half, D))
    out = pl.BlockSpec((depth, CORES, piece, 2 * HEAD_DIM), lambda h, core: (0, 0, 0, h))
    part = jax.ShapeDtypeStruct((depth, CORES, piece, 2 * HALF), jnp.bfloat16)
    return pl.pallas_call(
        attention_kernel,
        grid_spec=pltpu.PrefetchScalarGridSpec(
            num_scalar_prefetch=1,
            grid=(OWN,),
            in_specs=[
                head,
                head,
                panel,
                panel,
                pl.BlockSpec((D, HEAD_DIM), lambda h, core: (0, HEADS + OWN * core[0] + h)),
                pl.BlockSpec((D, HEAD_DIM), lambda h, core: (0, 2 * HEADS + OWN * core[0] + h)),
            ],
            out_specs=[head, head, out, out],
            scratch_shapes=[
                pltpu.VMEM((2 * half, HEAD_DIM), jnp.float32),
                pltpu.VMEM((2 * half, HEAD_DIM), jnp.float32),
            ],
        ),
        out_shape=(
            jax.ShapeDtypeStruct((tokens, HALF), jnp.bfloat16),
            jax.ShapeDtypeStruct((tokens, HALF), jnp.bfloat16),
            part,
            part,
        ),
        compiler_params=params(48),
        name="attention",
    )(core, queries, grads, panel_own, panel_other, qkv_weight, qkv_weight)


def tail_kernel(base, panel, key_weight, value_weight, frames, low, high, grad_out, taps, framed, total):
    rows = frames.shape[0]
    extra = mm(panel[:, :D], key_weight[...], NT) + mm(panel[:, D:], value_weight[...], NT)
    framed[:EDGE] = low[...].astype(jnp.float32)
    framed[EDGE : EDGE + rows] = frames[...].astype(jnp.float32)
    framed[EDGE + rows :] = high[...].astype(jnp.float32)
    for chunk in range(D // HEAD_DIM):
        cols = slice(chunk * HEAD_DIM, (chunk + 1) * HEAD_DIM)
        total[chunk] = base[:, cols]
        at = (chunk, pl.ds(0, rows // STRIDE, stride=STRIDE), slice(None))
        total[at] = total[at] + extra[:, cols]
        grad = total[chunk].astype(jnp.bfloat16)
        grad_out[:, cols] = grad
        grad = grad.astype(jnp.float32)
        for tap in range(TAPS):
            start = EDGE - REACH + GAP * tap
            term = grad * framed[start : start + rows, cols]
            taps[tap : tap + 1, cols] = jnp.sum(term, axis=0, keepdims=True)
    taps[TAPS:, :] = jnp.zeros((taps.shape[0] - TAPS, D), jnp.float32)


def tail(base, panel, qkv_weight, frames, low, high):
    rows = frames.shape[0]
    return pl.pallas_call(
        tail_kernel,
        grid=(1,),
        in_specs=[
            whole(base.shape),
            whole(panel.shape),
            pl.BlockSpec((D, D), lambda i: (0, 1)),
            pl.BlockSpec((D, D), lambda i: (0, 2)),
            whole(frames.shape),
            whole(low.shape),
            whole(high.shape),
        ],
        out_specs=[whole((rows, D)), whole((8, D))],
        out_shape=(
            jax.ShapeDtypeStruct((rows, D), jnp.bfloat16),
            jax.ShapeDtypeStruct((8, D), jnp.float32),
        ),
        scratch_shapes=[
            pltpu.VMEM((rows + 2 * EDGE, D), jnp.float32),
            pltpu.VMEM((D // HEAD_DIM, rows, HEAD_DIM), jnp.float32),
        ],
        compiler_params=params(40),
        name="tail",
    )(base, panel, qkv_weight, qkv_weight, frames, low, high)


def back_kernel(grad, low, high, weight, out, framed):
    rows = grad.shape[0]
    framed[:EDGE] = low[...].astype(jnp.float32)
    framed[EDGE : EDGE + rows] = grad[...].astype(jnp.float32)
    framed[EDGE + rows :] = high[...].astype(jnp.float32)
    acc = None
    for tap in range(TAPS):
        start = EDGE + REACH - GAP * tap
        term = weight[tap : tap + 1, :] * framed[start : start + rows, :]
        acc = term if acc is None else acc + term
    out[...] = acc.astype(jnp.bfloat16)


def back(grad, low, high, weight):
    rows = grad.shape[0]
    return pl.pallas_call(
        back_kernel,
        out_shape=jax.ShapeDtypeStruct((rows, D), jnp.bfloat16),
        scratch_shapes=[pltpu.VMEM((rows + 2 * EDGE, D), jnp.float32)],
        compiler_params=params(32),
        name="back",
    )(grad, low, high, weight)


def swap(block, axis):
    return lax.ppermute(block, axis, SWAP)


def edges(block):
    count = lax.axis_size(TALL)
    up = [(i, i + 1) for i in range(count - 1)]
    down = [(i + 1, i) for i in range(count - 1)]
    return lax.ppermute(block[-EDGE:], TALL, up), lax.ppermute(block[:EDGE], TALL, down)


def in_order(first, own, other, axis):
    return jnp.where(
        first, jnp.concatenate([own, other], axis=axis), jnp.concatenate([other, own], axis=axis)
    )


def shards(frames, conv_weight, qkv_weight, out_weight, cotangent):
    rows = frames.shape[0]
    depth = lax.axis_size("z")
    core = lax.axis_index("core")
    first = core == 0
    plane = lax.axis_index("y")

    low, high = edges(frames)
    cot_all = jnp.concatenate([cotangent, swap(cotangent, "core")], axis=0)
    conv_out, conv_panel = conv(frames, low, high, conv_weight)
    chunk = jnp.concatenate([conv_panel, swap(conv_panel, "y")], axis=0)
    panel_own = lax.all_gather(chunk, "z", axis=0, tiled=True)
    conv_all = jnp.concatenate([conv_out, swap(conv_out, "core")], axis=0)

    query_weight = lax.dynamic_slice_in_dim(qkv_weight, core * HALF, HALF, axis=1)
    out_rows = lax.dynamic_slice_in_dim(out_weight, core * HALF, HALF, axis=0)
    queries = mm(conv_all, query_weight).astype(jnp.bfloat16)
    grads = mm(cot_all, out_rows, NT).astype(jnp.bfloat16)

    panel_other = swap(panel_own, "core")
    att, gq, mine, theirs = attention(
        core.astype(jnp.int32)[None], queries, grads, panel_own, panel_other, qkv_weight, depth
    )

    summed = mine.astype(jnp.float32) + swap(theirs, "y").astype(jnp.float32)
    pieces = summed.astype(jnp.bfloat16).reshape(-1, 2 * HALF)
    panel_grads = lax.psum_scatter(pieces, "z", scatter_dimension=0, tiled=True)
    share = panel_grads.shape[0] // CORES

    att_other = swap(att, "core")
    att_other = jnp.concatenate([att_other[rows:], att_other[:rows]], axis=0)
    gq_other = swap(gq[rows:], "core")
    att_full = in_order(first, att, att_other, 1)
    gq_full = in_order(first, gq[:rows], gq_other, 1)
    mixed = mm(att_full[:rows], out_weight).astype(jnp.bfloat16)
    base = mm(gq_full, qkv_weight[:, :D], NT)

    cot_cols = lax.dynamic_slice_in_dim(cot_all, core * HALF, HALF, axis=1)
    sums = jnp.concatenate([mm(conv_all, gq, TN), mm(att_full, cot_cols, TN)], axis=1).astype(jnp.bfloat16)
    sums = sums.reshape(depth, PLANES, D // depth // PLANES, 2 * HALF)
    sums_mine = lax.dynamic_index_in_dim(sums, plane, 1, keepdims=False)
    sums_theirs = lax.dynamic_index_in_dim(sums, 1 - plane, 1, keepdims=False)

    other_heads = swap(panel_grads[share:], "core")

    def by_kind(block):
        return block.reshape(block.shape[0], OWN, 2, HEAD_DIM).transpose(0, 2, 1, 3)

    panel_full = in_order(first, by_kind(panel_grads[:share]), by_kind(other_heads), 2).reshape(share, 2 * D)
    grad_conv, taps = tail(base, panel_full, qkv_weight, frames, low, high)
    x_grad = back(grad_conv, *edges(grad_conv), conv_weight)

    gathered = lax.all_gather(panel_grads, "z", axis=0, tiled=True)
    place = lax.axis_index("z") * (D // depth)

    def plane_rows(panel):
        cols = lax.dynamic_slice_in_dim(panel, place, D // depth, axis=1)
        return cols.reshape(depth, PLANES, share, D // depth)[:, 0]

    panel_cols = jnp.stack([plane_rows(panel_own), plane_rows(panel_other)], axis=1).reshape(-1, D // depth)
    kv_sums = mm(panel_cols, gathered, TN).reshape(PLANES, -1, 2 * HALF)
    kv_mine = lax.dynamic_index_in_dim(kv_sums, plane, 0, keepdims=False)
    kv_theirs = lax.dynamic_index_in_dim(kv_sums, 1 - plane, 0, keepdims=False)
    kv_mine = kv_mine + swap(kv_theirs, "y")

    sums_mine = sums_mine.astype(jnp.float32) + swap(sums_theirs, "y").astype(jnp.float32)
    qo_mine = lax.psum_scatter(
        sums_mine.astype(jnp.bfloat16).reshape(-1, 2 * HALF), "z", scatter_dimension=0, tiled=True
    )

    def exchanged(block):
        block = block.reshape(CORES, -1, 2 * HALF)
        keep = lax.dynamic_index_in_dim(block, core, 0, keepdims=False)
        give = lax.dynamic_index_in_dim(block, 1 - core, 0, keepdims=False)
        return keep, swap(give, "core")

    qo_own, qo_other = exchanged(qo_mine)
    kv_own, kv_other = exchanged(kv_mine)
    kv_grad = in_order(first, by_kind(kv_own), by_kind(kv_other), 2).reshape(-1, 2 * D)
    query_grad = in_order(first, qo_own[:, :HALF], qo_other[:, :HALF], 1).astype(jnp.float32)
    out_weight_grad = in_order(first, qo_own[:, HALF:], qo_other[:, HALF:], 1).astype(jnp.float32)
    qkv_weight_grad = jnp.concatenate([query_grad, kv_grad], axis=1)

    taps = taps + swap(taps, "core")
    taps = taps + swap(taps, "y")
    distance = 1
    while distance < depth:
        taps = taps + lax.ppermute(taps, "z", [(i, i ^ distance) for i in range(depth)])
        distance *= 2
    conv_weight_grad = taps[:TAPS]
    return (mixed, x_grad, qkv_weight_grad, out_weight_grad, conv_weight_grad)


def solution(mesh):
    clips, tall = mesh.devices.shape
    grid = Mesh(
        mesh.devices.reshape(clips, tall // (PLANES * CORES), PLANES, CORES), ("clip", "z", "y", "core")
    )
    rows = P(("clip",) + TALL, None)
    in_specs = (rows, P(), P(), P(), rows)
    out_specs = (rows, rows, rows, rows, P("clip", None))
    return jax.shard_map(shards, mesh=grid, in_specs=in_specs, out_specs=out_specs, check_vma=False)
```

```python
import jax
import jax.numpy as jnp
from jax import lax
from jax.experimental import pallas as pl
from jax.experimental.pallas import tpu as pltpu
from jax.sharding import Mesh
from jax.sharding import PartitionSpec as P

D = 1024
HEADS = 8
HEAD_DIM = 128
TAPS = 5
GAP = 2
STRIDE = 8
REACH = GAP * (TAPS // 2)
EDGE = 16
CORES = 2
PLANES = 2
OWN = HEADS // CORES
HALF = OWN * HEAD_DIM
SCALE = 1.0 / HEAD_DIM**0.5
LOG2E = 1.4426950408889634
TALL = ("z", "y", "core")
SWAP = [(0, 1), (1, 0)]

NN = (((1,), (0,)), ((), ()))
NT = (((1,), (1,)), ((), ()))
TN = (((0,), (0,)), ((), ()))


def mm(a, b, dims=NN):
    return lax.dot_general(a, b, dims, preferred_element_type=jnp.float32)


def params(mib):
    return pltpu.CompilerParams(vmem_limit_bytes=mib * 1024 * 1024)


def whole(shape):
    return pl.BlockSpec(shape, lambda *_: (0,) * len(shape))


def conv_kernel(frames, low, high, weight, conv_out, conv_panel, framed, total):
    rows = frames.shape[0]
    framed[:EDGE] = low[...].astype(jnp.float32)
    framed[EDGE : EDGE + rows] = frames[...].astype(jnp.float32)
    framed[EDGE + rows :] = high[...].astype(jnp.float32)
    acc = None
    for tap in range(TAPS):
        start = EDGE - REACH + GAP * tap
        term = weight[tap : tap + 1, :] * framed[start : start + rows, :]
        acc = term if acc is None else acc + term
    conv_out[...] = acc.astype(jnp.bfloat16)
    for chunk in range(D // HEAD_DIM):
        cols = slice(chunk * HEAD_DIM, (chunk + 1) * HEAD_DIM)
        total[chunk] = acc[:, cols]
        picked = total[chunk, pl.ds(0, rows // STRIDE, stride=STRIDE), :].astype(jnp.bfloat16)
        for copy in range(conv_panel.shape[0]):
            conv_panel[copy, :, cols] = picked


def conv(frames, low, high, weight, depth):
    rows = frames.shape[0]
    return pl.pallas_call(
        conv_kernel,
        out_shape=(
            jax.ShapeDtypeStruct((rows, D), jnp.bfloat16),
            jax.ShapeDtypeStruct((depth, rows // STRIDE, D), jnp.bfloat16),
        ),
        scratch_shapes=[
            pltpu.VMEM((rows + 2 * EDGE, D), jnp.float32),
            pltpu.VMEM((D // HEAD_DIM, rows, HEAD_DIM), jnp.float32),
        ],
        compiler_params=params(32),
        name="conv",
    )(frames, low, high, weight)


def project_kernel(place, conv_own, conv_other, cot_own, cot_other, query_weight, out_weight, queries, grads):
    del place
    rows = conv_own.shape[0]
    for at, conv_block, cot_block in ((0, conv_own, cot_own), (rows, conv_other, cot_other)):
        queries[at : at + rows, :] = mm(conv_block[...], query_weight[...]).astype(jnp.bfloat16)
        grads[at : at + rows, :] = mm(cot_block[...], out_weight[...], NT).astype(jnp.bfloat16)


def project(place, conv_own, conv_other, cot_own, cot_other, qkv_weight, out_weight):
    rows = conv_own.shape[0]
    block = whole((rows, D))
    out = jax.ShapeDtypeStruct((2 * rows, HALF), jnp.bfloat16)
    return pl.pallas_call(
        project_kernel,
        grid_spec=pltpu.PrefetchScalarGridSpec(
            num_scalar_prefetch=1,
            grid=(1,),
            in_specs=[
                block,
                block,
                block,
                block,
                pl.BlockSpec((D, HALF), lambda i, place: (0, place[0])),
                pl.BlockSpec((HALF, D), lambda i, place: (place[0], 0)),
            ],
            out_specs=[whole((2 * rows, HALF))] * 2,
        ),
        out_shape=(out, out),
        compiler_params=params(32),
        cost_estimate=pl.CostEstimate(
            flops=8 * rows * D * HALF, bytes_accessed=12 * rows * D + 4 * D * HALF, transcendentals=0
        ),
        name="project",
    )(place, conv_own, conv_other, cot_own, cot_other, qkv_weight, out_weight)


def attention_kernel(
    place, queries, grads, p00, p10, p01, p11, key_weight, value_weight,
    att, gq, early, late, sums, acck, accv, keys, values, panel_t,
):
    head = pl.program_id(0)
    panels = (p00, p10, p01, p11)
    size = p00.shape[0]

    @pl.when(head == 0)
    def _():
        for index, panel in enumerate(panels):
            panel_t[:, index * size : (index + 1) * size] = panel[...].T

    weight = jnp.concatenate([key_weight[...], value_weight[...]], axis=1)
    for index, panel in enumerate(panels):
        both = mm(panel[...], weight).astype(jnp.bfloat16)
        keys[index * size : (index + 1) * size, :] = both[:, :HEAD_DIM]
        values[index * size : (index + 1) * size, :] = both[:, HEAD_DIM:]
    tokens = queries.shape[0]
    step = 256
    for begin in range(0, tokens, step):
        rows = slice(begin, begin + step)
        query, grad = queries[rows, :], grads[rows, :]
        scores = mm(keys[...], query, NT)
        highest = jnp.max(scores, axis=0, keepdims=True)
        raised = jnp.exp2((scores - highest) * (SCALE * LOG2E))
        probs = raised * (1.0 / jnp.sum(raised, axis=0, keepdims=True))
        weights = probs.astype(jnp.bfloat16)
        attended = mm(values[...], weights, TN).astype(jnp.bfloat16)
        grad_t = grad.astype(jnp.float32).T
        delta = jnp.sum(grad_t * attended.astype(jnp.float32), axis=0, keepdims=True)
        dprob = mm(values[...], grad, NT)
        grad_scores = (probs * (dprob - delta)).astype(jnp.bfloat16)
        att[rows, :] = attended.astype(jnp.float32).T.astype(jnp.bfloat16)
        gq[rows, :] = (mm(keys[...], grad_scores, TN) * SCALE).T.astype(jnp.bfloat16)
        part_k = mm(grad_scores, query)
        part_v = mm(weights, grad)
        if begin == 0:
            acck[...] = part_k
            accv[...] = part_v
        else:
            acck[...] += part_k
            accv[...] += part_v
    part = jnp.concatenate([acck[...] * SCALE, accv[...]], axis=1).astype(jnp.bfloat16)
    sums[...] = mm(panel_t[...], part).astype(jnp.bfloat16)

    depth, piece = early.shape[0], early.shape[3]

    def store(out):
        for ahead in range(depth):
            z = lax.rem(place[1] + ahead, depth)
            for index in range(len(panels)):
                at = pl.ds(pl.multiple_of(index * size + z * piece, piece), piece)
                out[ahead, index % PLANES, index // PLANES, :, :HEAD_DIM] = (acck[at, :] * SCALE).astype(
                    jnp.bfloat16
                )
                out[ahead, index % PLANES, index // PLANES, :, HEAD_DIM:] = accv[at, :].astype(jnp.bfloat16)

    @pl.when(head < OWN // 2)
    def _():
        store(early)

    @pl.when(head >= OWN // 2)
    def _():
        store(late)


def attention(place, queries, grads, panels, qkv_weight, depth):
    tokens = queries.shape[0]
    size = panels[0].shape[0]
    piece = size // depth
    total = PLANES * CORES * size
    wide = 2 * HEAD_DIM
    head = pl.BlockSpec((tokens, HEAD_DIM), lambda h, place: (0, h))
    shape = (depth, PLANES, CORES, piece, wide)
    part = jax.ShapeDtypeStruct(shape[:-1] + (HALF,), jnp.bfloat16)
    return pl.pallas_call(
        attention_kernel,
        grid_spec=pltpu.PrefetchScalarGridSpec(
            num_scalar_prefetch=1,
            grid=(OWN,),
            in_specs=[head, head]
            + [whole((size, D))] * 4
            + [
                pl.BlockSpec((D, HEAD_DIM), lambda h, place: (0, HEADS + OWN * place[0] + h)),
                pl.BlockSpec((D, HEAD_DIM), lambda h, place: (0, 2 * HEADS + OWN * place[0] + h)),
            ],
            out_specs=[
                head,
                head,
                pl.BlockSpec(shape, lambda h, place: (0, 0, 0, 0, jnp.minimum(h, OWN // 2 - 1))),
                pl.BlockSpec(shape, lambda h, place: (0, 0, 0, 0, jnp.maximum(h - OWN // 2, 0))),
                pl.BlockSpec((D, wide), lambda h, place: (0, h)),
            ],
            scratch_shapes=[
                pltpu.VMEM((total, HEAD_DIM), jnp.float32),
                pltpu.VMEM((total, HEAD_DIM), jnp.float32),
                pltpu.VMEM((total, HEAD_DIM), jnp.bfloat16),
                pltpu.VMEM((total, HEAD_DIM), jnp.bfloat16),
                pltpu.VMEM((D, total), jnp.bfloat16),
            ],
        ),
        out_shape=(
            jax.ShapeDtypeStruct((tokens, HALF), jnp.bfloat16),
            jax.ShapeDtypeStruct((tokens, HALF), jnp.bfloat16),
            part,
            part,
            jax.ShapeDtypeStruct((D, 2 * D), jnp.bfloat16),
        ),
        compiler_params=params(50),
        cost_estimate=pl.CostEstimate(flops=8_000_000_000, bytes_accessed=16_000_000, transcendentals=2_000_000),
        name="attention",
    )(place, queries, grads, *panels, qkv_weight, qkv_weight)


def middle_kernel(
    place, att, att_other, gq, gq_other, conv_own, conv_other, cot_own, cot_other, out_weight, query_weight, held,
    mixed, base, sums,
):
    del held
    core = place[0]
    rows = conv_own.shape[0]
    own = pl.ds(pl.multiple_of(core * HALF, HALF), HALF)
    away = pl.ds(pl.multiple_of((1 - core) * HALF, HALF), HALF)
    queries = mm(conv_own[...], gq[:rows, :], TN) + mm(conv_other[...], gq[rows:, :], TN)
    sums[:, :HALF] = queries.astype(jnp.bfloat16)
    part = mm(att[:rows, :], cot_own[:, own], TN) + mm(att[rows:, :], cot_other[:, own], TN)
    sums[own, HALF:] = part.astype(jnp.bfloat16)
    part = mm(att_other[rows:, :], cot_own[:, own], TN) + mm(att_other[:rows, :], cot_other[:, own], TN)
    sums[away, HALF:] = part.astype(jnp.bfloat16)
    blend = mm(att[:rows, :], out_weight[own, :]) + mm(att_other[rows:, :], out_weight[away, :])
    mixed[...] = blend.astype(jnp.bfloat16)
    base[...] = mm(gq[:rows, :], query_weight[:, own], NT) + mm(gq_other[...], query_weight[:, away], NT)


def middle(place, att, att_other, gq, gq_other, conv_own, conv_other, cot_own, cot_other, out_weight, qkv_weight, held):
    rows = conv_own.shape[0]
    ins = (att, att_other, gq, gq_other, conv_own, conv_other, cot_own, cot_other, out_weight)
    return pl.pallas_call(
        middle_kernel,
        grid_spec=pltpu.PrefetchScalarGridSpec(
            num_scalar_prefetch=1,
            grid=(1,),
            in_specs=[whole(item.shape) for item in ins]
            + [pl.BlockSpec((D, D), lambda i, place: (0, 0)), pl.BlockSpec(memory_space=pl.ANY)],
            out_specs=[
                whole((rows, D)),
                whole((rows, D)),
                pl.BlockSpec((D, D), lambda i, place: (0, 1)),
            ],
        ),
        out_shape=(
            jax.ShapeDtypeStruct((rows, D), jnp.bfloat16),
            jax.ShapeDtypeStruct((rows, D), jnp.float32),
            jax.ShapeDtypeStruct(held.shape, held.dtype),
        ),
        input_output_aliases={len(ins) + 2: 2},
        compiler_params=params(50),
        cost_estimate=pl.CostEstimate(flops=4_000_000_000, bytes_accessed=12_000_000, transcendentals=0),
        name="middle",
    )(place, *ins, qkv_weight, held)


def tail_kernel(base, panel, key_weight, value_weight, frames, low, high, grad_out, taps, framed, total):
    rows = frames.shape[0]
    extra = mm(panel[:, :D], key_weight[...], NT) + mm(panel[:, D:], value_weight[...], NT)
    framed[:EDGE] = low[...].astype(jnp.float32)
    framed[EDGE : EDGE + rows] = frames[...].astype(jnp.float32)
    framed[EDGE + rows :] = high[...].astype(jnp.float32)
    for chunk in range(D // HEAD_DIM):
        cols = slice(chunk * HEAD_DIM, (chunk + 1) * HEAD_DIM)
        total[chunk] = base[:, cols]
        at = (chunk, pl.ds(0, rows // STRIDE, stride=STRIDE), slice(None))
        total[at] = total[at] + extra[:, cols]
        grad = total[chunk].astype(jnp.bfloat16)
        grad_out[:, cols] = grad
        grad = grad.astype(jnp.float32)
        for tap in range(TAPS):
            start = EDGE - REACH + GAP * tap
            term = grad * framed[start : start + rows, cols]
            taps[tap : tap + 1, cols] = jnp.sum(term, axis=0, keepdims=True)
    taps[TAPS:, :] = jnp.zeros((taps.shape[0] - TAPS, D), jnp.float32)


def tail(base, panel, qkv_weight, frames, low, high):
    rows = frames.shape[0]
    return pl.pallas_call(
        tail_kernel,
        grid=(1,),
        in_specs=[
            whole(base.shape),
            whole(panel.shape),
            pl.BlockSpec((D, D), lambda i: (0, 1)),
            pl.BlockSpec((D, D), lambda i: (0, 2)),
            whole(frames.shape),
            whole(low.shape),
            whole(high.shape),
        ],
        out_specs=[whole((rows, D)), whole((8, D))],
        out_shape=(
            jax.ShapeDtypeStruct((rows, D), jnp.bfloat16),
            jax.ShapeDtypeStruct((8, D), jnp.float32),
        ),
        scratch_shapes=[
            pltpu.VMEM((rows + 2 * EDGE, D), jnp.float32),
            pltpu.VMEM((D // HEAD_DIM, rows, HEAD_DIM), jnp.float32),
        ],
        compiler_params=params(40),
        name="tail",
    )(base, panel, qkv_weight, qkv_weight, frames, low, high)


def back_kernel(grad, low, high, weight, out, framed):
    rows = grad.shape[0]
    framed[:EDGE] = low[...].astype(jnp.float32)
    framed[EDGE : EDGE + rows] = grad[...].astype(jnp.float32)
    framed[EDGE + rows :] = high[...].astype(jnp.float32)
    acc = None
    for tap in range(TAPS):
        start = EDGE + REACH - GAP * tap
        term = weight[tap : tap + 1, :] * framed[start : start + rows, :]
        acc = term if acc is None else acc + term
    out[...] = acc.astype(jnp.bfloat16)


def back(grad, low, high, weight):
    rows = grad.shape[0]
    return pl.pallas_call(
        back_kernel,
        out_shape=jax.ShapeDtypeStruct((rows, D), jnp.bfloat16),
        scratch_shapes=[pltpu.VMEM((rows + 2 * EDGE, D), jnp.float32)],
        compiler_params=params(32),
        name="back",
    )(grad, low, high, weight)


def swap(block, axis):
    return lax.ppermute(block, axis, SWAP)


def edges(block):
    count = lax.axis_size(TALL)
    up = [(i, i + 1) for i in range(count - 1)]
    down = [(i + 1, i) for i in range(count - 1)]
    return lax.ppermute(block[-EDGE:], TALL, up), lax.ppermute(block[:EDGE], TALL, down)


def in_order(first, own, other, axis):
    return jnp.where(
        first, jnp.concatenate([own, other], axis=axis), jnp.concatenate([other, own], axis=axis)
    )


def ring_sum(part, depth):
    ahead = [(i, (i + 1) % depth) for i in range(depth)]
    behind = [(i, (i - 1) % depth) for i in range(depth)]
    far = depth // 2
    up, down = part[far], part[far + 1]
    for step in range(1, far + 1):
        up = lax.ppermute(up, "z", ahead)
        if step < far:
            up = plus(up, part[far - step])
            down = lax.ppermute(down, "z", behind)
            if step < far - 1:
                down = plus(down, part[far + 1 + step])
    return part[0].astype(jnp.float32) + up.astype(jnp.float32) + down.astype(jnp.float32)


def plus(one, two):
    return (one.astype(jnp.float32) + two.astype(jnp.float32)).astype(jnp.bfloat16)


def shards(frames, conv_weight, qkv_weight, out_weight, cotangent):
    rows = frames.shape[0]
    depth = lax.axis_size("z")
    core = lax.axis_index("core")
    plane = lax.axis_index("y")
    first = core == 0
    place = jnp.stack([core, lax.axis_index("z")]).astype(jnp.int32)

    low, high = edges(frames)
    cot_other = swap(cotangent, "core")
    conv_own, copies = conv(frames, low, high, conv_weight, depth)
    p00 = lax.all_to_all(copies.reshape(-1, D), "z", 0, 0, tiled=True)
    conv_other = swap(conv_own, "core")
    queries, grads = project(place, conv_own, conv_other, cotangent, cot_other, qkv_weight, out_weight)
    p10 = swap(p00, "y")
    p01 = swap(p00, "core")
    p11 = swap(p10, "core")
    att, gq, early, late, held = attention(place, queries, grads, (p00, p10, p01, p11), qkv_weight, depth)

    def finish(part):
        total = ring_sum(part, depth).astype(jnp.bfloat16)
        total = total.reshape((PLANES, CORES) + total.shape[-2:])
        return total[:, 0], swap(total[:, 1], "core")

    att_other = swap(att, "core")
    gq_other = swap(gq[rows:], "core")
    mixed, base, sums = middle(
        place, att, att_other, gq, gq_other, conv_own, conv_other, cotangent, cot_other, out_weight, qkv_weight, held
    )
    scattered = lax.psum_scatter(sums, "z", scatter_dimension=0, tiled=True)

    early_own, early_other = finish(early)
    late_own, late_other = finish(late)
    panel = jnp.concatenate([early_own, late_own, early_other, late_other], axis=-1)
    panel = plus(panel[0], swap(panel[1], "y"))

    def by_kind(block):
        return block.reshape(block.shape[0], OWN, 2, HEAD_DIM).transpose(0, 2, 1, 3)

    panel_full = in_order(first, by_kind(panel[:, : 2 * HALF]), by_kind(panel[:, 2 * HALF :]), 2).reshape(-1, 2 * D)
    grad_conv, taps = tail(base, panel_full, qkv_weight, frames, low, high)
    x_grad = back(grad_conv, *edges(grad_conv), conv_weight)

    taps = taps + swap(taps, "core")
    taps = taps + swap(taps, "y")
    distance = 1
    while distance < depth:
        taps = taps + lax.ppermute(taps, "z", [(i, i ^ distance) for i in range(depth)])
        distance *= 2
    conv_weight_grad = taps[:TAPS]

    scattered = scattered.reshape(PLANES, -1, 2 * D)
    keep = lax.dynamic_index_in_dim(scattered, plane, 0, keepdims=False)
    give = lax.dynamic_index_in_dim(scattered, 1 - plane, 0, keepdims=False)
    summed = keep.astype(jnp.float32) + swap(give, "y").astype(jnp.float32)
    summed = summed.reshape(CORES, -1, 2 * D)
    own = lax.dynamic_index_in_dim(summed, core, 0, keepdims=False)
    other = swap(lax.dynamic_index_in_dim(summed, 1 - core, 0, keepdims=False), "core")

    def columns(begin, count):
        return in_order(first, own[:, begin : begin + count], other[:, begin : begin + count], 1)

    kv_grad = in_order(first, by_kind(own[:, :D]), by_kind(other[:, :D]), 2).reshape(-1, 2 * D)
    qkv_weight_grad = jnp.concatenate([columns(D, HALF), kv_grad], axis=1)
    out_weight_grad = columns(D + HALF, HALF)
    return (mixed, x_grad, qkv_weight_grad, out_weight_grad, conv_weight_grad)


def solution(mesh):
    clips, tall = mesh.devices.shape
    grid = Mesh(
        mesh.devices.reshape(clips, tall // (PLANES * CORES), PLANES, CORES), ("clip", "z", "y", "core")
    )
    rows = P(("clip",) + TALL, None)
    in_specs = (rows, P(), P(), P(), rows)
    out_specs = (rows, rows, rows, rows, P("clip", None))
    return jax.shard_map(shards, mesh=grid, in_specs=in_specs, out_specs=out_specs, check_vma=False)
```

```python
import functools

import jax
import jax.numpy as jnp
from jax import lax
from jax.experimental import pallas as pl
from jax.experimental.pallas import tpu as pltpu
from jax.sharding import Mesh
from jax.sharding import PartitionSpec as P

D = 1024
HEADS = 8
HEAD_DIM = 128
TAPS = 5
GAP = 2
STRIDE = 8
REACH = GAP * (TAPS // 2)
EDGE = 16
CORES = 2
PLANES = 2
OWN = HEADS // CORES
HALF = OWN * HEAD_DIM
SCALE = 1.0 / HEAD_DIM**0.5
LOG2E = 1.4426950408889634
TALL = ("z", "y", "core")
SWAP = [(0, 1), (1, 0)]

NN = (((1,), (0,)), ((), ()))
NT = (((1,), (1,)), ((), ()))
TN = (((0,), (0,)), ((), ()))


def mm(a, b, dims=NN):
    return lax.dot_general(a, b, dims, preferred_element_type=jnp.float32)


def params(mib):
    return pltpu.CompilerParams(vmem_limit_bytes=mib * 1024 * 1024)


def whole(shape):
    return pl.BlockSpec(shape, lambda *_: (0,) * len(shape))


def conv_kernel(frames, low, high, weight, conv_out, conv_panel, framed, total):
    rows = frames.shape[0]
    framed[:EDGE] = low[...].astype(jnp.float32)
    framed[EDGE : EDGE + rows] = frames[...].astype(jnp.float32)
    framed[EDGE + rows :] = high[...].astype(jnp.float32)
    acc = None
    for tap in range(TAPS):
        start = EDGE - REACH + GAP * tap
        term = weight[tap : tap + 1, :] * framed[start : start + rows, :]
        acc = term if acc is None else acc + term
    conv_out[...] = acc.astype(jnp.bfloat16)
    for chunk in range(D // HEAD_DIM):
        cols = slice(chunk * HEAD_DIM, (chunk + 1) * HEAD_DIM)
        total[chunk] = acc[:, cols]
        picked = total[chunk, pl.ds(0, rows // STRIDE, stride=STRIDE), :]
        conv_panel[:, cols] = picked.astype(jnp.bfloat16)


def conv(frames, low, high, weight):
    rows = frames.shape[0]
    return pl.pallas_call(
        conv_kernel,
        out_shape=(
            jax.ShapeDtypeStruct((rows, D), jnp.bfloat16),
            jax.ShapeDtypeStruct((rows // STRIDE, D), jnp.bfloat16),
        ),
        scratch_shapes=[
            pltpu.VMEM((rows + 2 * EDGE, D), jnp.float32),
            pltpu.VMEM((D // HEAD_DIM, rows, HEAD_DIM), jnp.float32),
        ],
        compiler_params=params(60),
        name="conv",
    )(frames, low, high, weight)


def project_kernel(place, conv_own, conv_other, cot_own, cot_other, query_weight, out_weight, queries, grads):
    del place
    rows = conv_own.shape[0]
    for at, conv_block, cot_block in ((0, conv_own, cot_own), (rows, conv_other, cot_other)):
        queries[at : at + rows, :] = mm(conv_block[...], query_weight[...]).astype(jnp.bfloat16)
        grads[at : at + rows, :] = mm(cot_block[...], out_weight[...], NT).astype(jnp.bfloat16)


def project(place, conv_own, conv_other, cot_own, cot_other, qkv_weight, out_weight):
    rows = conv_own.shape[0]
    block = whole((rows, D))
    out = jax.ShapeDtypeStruct((2 * rows, HALF), jnp.bfloat16)
    return pl.pallas_call(
        project_kernel,
        grid_spec=pltpu.PrefetchScalarGridSpec(
            num_scalar_prefetch=1,
            grid=(1,),
            in_specs=[
                block,
                block,
                block,
                block,
                pl.BlockSpec((D, HALF), lambda i, place: (0, place[0])),
                pl.BlockSpec((HALF, D), lambda i, place: (place[0], 0)),
            ],
            out_specs=[whole((2 * rows, HALF))] * 2,
        ),
        out_shape=(out, out),
        compiler_params=params(32),
        cost_estimate=pl.CostEstimate(
            flops=8 * rows * D * HALF, bytes_accessed=12 * rows * D + 4 * D * HALF, transcendentals=0
        ),
        name="project",
    )(place, conv_own, conv_other, cot_own, cot_other, qkv_weight, out_weight)


def batches(depth):
    far = depth // 2
    pieces = [(0, 0)] + [(step, core) for step in range(1, far) for core in range(CORES)] + [(far, 0)]
    cut = 1 + CORES * (far // 2)
    return pieces[:cut], pieces[cut:]


def attention_kernel(depth, place, queries, grads, *refs):
    panels, rest = refs[:8], refs[8:]
    key_weight, value_weight, att, gq, early, late, panel, part, keys, values, acck, accv = rest
    head = pl.program_id(0)

    @pl.when(head == 0)
    def _():
        at = 0
        for block in panels:
            panel[at : at + block.shape[0], :] = block[...]
            at += block.shape[0]

    weight = jnp.concatenate([key_weight[...], value_weight[...]], axis=1)
    both = mm(panel[...], weight).astype(jnp.bfloat16)
    keys[...] = both[:, :HEAD_DIM]
    values[...] = both[:, HEAD_DIM:]
    query, grad = queries[...], grads[...]
    scores = mm(keys[...], query, NT)
    highest = jnp.max(scores, axis=0, keepdims=True)
    raised = jnp.exp2((scores - highest) * (SCALE * LOG2E))
    probs = raised * (1.0 / jnp.sum(raised, axis=0, keepdims=True))
    weights = probs.astype(jnp.bfloat16)
    attended = mm(values[...], weights, TN).astype(jnp.bfloat16)
    grad_t = grad.astype(jnp.float32).T
    delta = jnp.sum(grad_t * attended.astype(jnp.float32), axis=0, keepdims=True)
    dprob = mm(values[...], grad, NT)
    grad_scores = (probs * (dprob - delta)).astype(jnp.bfloat16)
    att[...] = attended.astype(jnp.float32).T.astype(jnp.bfloat16)
    gq[...] = (mm(keys[...], grad_scores, TN) * SCALE).T.astype(jnp.bfloat16)
    acck[...] = mm(grad_scores, query) * SCALE
    accv[...] = mm(weights, grad)
    part[:, :HEAD_DIM] = acck[...].astype(jnp.bfloat16)
    part[:, HEAD_DIM:] = accv[...].astype(jnp.bfloat16)

    piece = early.shape[3]
    sign = 2 * place[0] - 1

    def store(out):
        at = 0
        for lane in range(CORES):
            for plane in range(PLANES):
                for batch in batches(depth):
                    for step, core in batch:
                        steps = step * (1 - 2 * lane)
                        ahead = lax.rem(depth + sign * steps, depth)
                        where = (ahead, plane, core ^ lane, slice(None))
                        out[where + (slice(0, HEAD_DIM),)] = part[at : at + piece, :HEAD_DIM]
                        out[where + (slice(HEAD_DIM, 2 * HEAD_DIM),)] = part[at : at + piece, HEAD_DIM:]
                        at += piece

    @pl.when(head < OWN // 2)
    def _():
        store(early)

    @pl.when(head >= OWN // 2)
    def _():
        store(late)


def attention(place, queries, grads, panels, qkv_weight, depth):
    tokens = queries.shape[0]
    total = sum(block.shape[0] for block in panels)
    piece = total // depth // PLANES // CORES
    wide = 2 * HEAD_DIM
    head = pl.BlockSpec((tokens, HEAD_DIM), lambda h, place: (0, h))
    shape = (depth, PLANES, CORES, piece, wide)
    parts = jax.ShapeDtypeStruct(shape[:-1] + (HALF,), jnp.bfloat16)
    return pl.pallas_call(
        functools.partial(attention_kernel, depth),
        grid_spec=pltpu.PrefetchScalarGridSpec(
            num_scalar_prefetch=1,
            grid=(OWN,),
            in_specs=[head, head]
            + [whole(block.shape) for block in panels]
            + [
                pl.BlockSpec((D, HEAD_DIM), lambda h, place: (0, HEADS + OWN * place[0] + h)),
                pl.BlockSpec((D, HEAD_DIM), lambda h, place: (0, 2 * HEADS + OWN * place[0] + h)),
            ],
            out_specs=[
                head,
                head,
                pl.BlockSpec(shape, lambda h, place: (0, 0, 0, 0, jnp.minimum(h, OWN // 2 - 1))),
                pl.BlockSpec(shape, lambda h, place: (0, 0, 0, 0, jnp.maximum(h - OWN // 2, 0))),
                whole((total, D)),
                pl.BlockSpec((total, wide), lambda h, place: (0, h)),
            ],
            scratch_shapes=[
                pltpu.VMEM((total, HEAD_DIM), jnp.bfloat16),
                pltpu.VMEM((total, HEAD_DIM), jnp.bfloat16),
                pltpu.VMEM((total, HEAD_DIM), jnp.float32),
                pltpu.VMEM((total, HEAD_DIM), jnp.float32),
            ],
        ),
        out_shape=(
            jax.ShapeDtypeStruct((tokens, HALF), jnp.bfloat16),
            jax.ShapeDtypeStruct((tokens, HALF), jnp.bfloat16),
            parts,
            parts,
            jax.ShapeDtypeStruct((total, D), jnp.bfloat16),
            jax.ShapeDtypeStruct((total, 2 * HALF), jnp.bfloat16),
        ),
        compiler_params=params(40),
        cost_estimate=pl.CostEstimate(flops=8_000_000_000, bytes_accessed=16_000_000, transcendentals=2_000_000),
        name="attention",
    )(place, queries, grads, *panels, qkv_weight, qkv_weight)


def weights_kernel(place, att, att_other, gq, conv_own, conv_other, cot_own, cot_other, panel, part, sums):
    core = place[0]
    rows = conv_own.shape[0]
    own = pl.ds(pl.multiple_of(core * HALF, HALF), HALF)
    away = pl.ds(pl.multiple_of((1 - core) * HALF, HALF), HALF)

    @pl.when(pl.program_id(0) == 0)
    def _():
        sums[...] = mm(panel[...], part[...], TN).astype(jnp.bfloat16)

    @pl.when(pl.program_id(0) == 1)
    def _():
        queries = mm(conv_own[...], gq[:rows, :], TN) + mm(conv_other[...], gq[rows:, :], TN)
        sums[:, :HALF] = queries.astype(jnp.bfloat16)
        mine = mm(att[:rows, :], cot_own[:, own], TN) + mm(att[rows:, :], cot_other[:, own], TN)
        sums[own, HALF:] = mine.astype(jnp.bfloat16)
        other = mm(att_other[rows:, :], cot_own[:, own], TN) + mm(att_other[:rows, :], cot_other[:, own], TN)
        sums[away, HALF:] = other.astype(jnp.bfloat16)


def weights(place, *ins):
    return pl.pallas_call(
        weights_kernel,
        grid_spec=pltpu.PrefetchScalarGridSpec(
            num_scalar_prefetch=1,
            grid=(2,),
            in_specs=[whole(item.shape) for item in ins],
            out_specs=pl.BlockSpec((D, D), lambda i, place: (0, i)),
        ),
        out_shape=jax.ShapeDtypeStruct((D, 2 * D), jnp.bfloat16),
        compiler_params=params(40),
        cost_estimate=pl.CostEstimate(flops=4_000_000_000, bytes_accessed=12_000_000, transcendentals=0),
        name="weights",
    )(place, *ins)


def mixing_kernel(place, att, att_other, gq, gq_other, out_weight, query_weight, mixed, base):
    core = place[0]
    rows = mixed.shape[0]
    own = pl.ds(pl.multiple_of(core * HALF, HALF), HALF)
    away = pl.ds(pl.multiple_of((1 - core) * HALF, HALF), HALF)
    blend = mm(att[:rows, :], out_weight[own, :]) + mm(att_other[rows:, :], out_weight[away, :])
    mixed[...] = blend.astype(jnp.bfloat16)
    base[...] = mm(gq[:rows, :], query_weight[:, own], NT) + mm(gq_other[...], query_weight[:, away], NT)


def mixing(place, att, att_other, gq, gq_other, out_weight, qkv_weight):
    rows = gq_other.shape[0]
    ins = (att, att_other, gq, gq_other, out_weight)
    return pl.pallas_call(
        mixing_kernel,
        grid_spec=pltpu.PrefetchScalarGridSpec(
            num_scalar_prefetch=1,
            grid=(1,),
            in_specs=[whole(item.shape) for item in ins] + [pl.BlockSpec((D, D), lambda i, place: (0, 0))],
            out_specs=[whole((rows, D)), whole((rows, D))],
        ),
        out_shape=(
            jax.ShapeDtypeStruct((rows, D), jnp.bfloat16),
            jax.ShapeDtypeStruct((rows, D), jnp.float32),
        ),
        compiler_params=params(40),
        cost_estimate=pl.CostEstimate(flops=1_000_000_000, bytes_accessed=8_000_000, transcendentals=0),
        name="mixing",
    )(place, *ins, qkv_weight)


def tail_kernel(base, panel, key_weight, value_weight, frames, low, high, grad_out, taps, framed, total):
    rows = frames.shape[0]
    extra = mm(panel[:, :D], key_weight[...], NT) + mm(panel[:, D:], value_weight[...], NT)
    framed[:EDGE] = low[...].astype(jnp.float32)
    framed[EDGE : EDGE + rows] = frames[...].astype(jnp.float32)
    framed[EDGE + rows :] = high[...].astype(jnp.float32)
    for chunk in range(D // HEAD_DIM):
        cols = slice(chunk * HEAD_DIM, (chunk + 1) * HEAD_DIM)
        total[chunk] = base[:, cols]
        at = (chunk, pl.ds(0, rows // STRIDE, stride=STRIDE), slice(None))
        total[at] = total[at] + extra[:, cols]
        grad = total[chunk].astype(jnp.bfloat16)
        grad_out[:, cols] = grad
        grad = grad.astype(jnp.float32)
        for tap in range(TAPS):
            start = EDGE - REACH + GAP * tap
            term = grad * framed[start : start + rows, cols]
            taps[tap : tap + 1, cols] = jnp.sum(term, axis=0, keepdims=True)
    taps[TAPS:, :] = jnp.zeros((taps.shape[0] - TAPS, D), jnp.float32)


def tail(base, panel, qkv_weight, frames, low, high):
    rows = frames.shape[0]
    return pl.pallas_call(
        tail_kernel,
        grid=(1,),
        in_specs=[
            whole(base.shape),
            whole(panel.shape),
            pl.BlockSpec((D, D), lambda i: (0, 1)),
            pl.BlockSpec((D, D), lambda i: (0, 2)),
            whole(frames.shape),
            whole(low.shape),
            whole(high.shape),
        ],
        out_specs=[whole((rows, D)), whole((8, D))],
        out_shape=(
            jax.ShapeDtypeStruct((rows, D), jnp.bfloat16),
            jax.ShapeDtypeStruct((8, D), jnp.float32),
        ),
        scratch_shapes=[
            pltpu.VMEM((rows + 2 * EDGE, D), jnp.float32),
            pltpu.VMEM((D // HEAD_DIM, rows, HEAD_DIM), jnp.float32),
        ],
        compiler_params=params(60),
        name="tail",
    )(base, panel, qkv_weight, qkv_weight, frames, low, high)


def back_kernel(grad, low, high, weight, out, framed):
    rows = grad.shape[0]
    framed[:EDGE] = low[...].astype(jnp.float32)
    framed[EDGE : EDGE + rows] = grad[...].astype(jnp.float32)
    framed[EDGE + rows :] = high[...].astype(jnp.float32)
    acc = None
    for tap in range(TAPS):
        start = EDGE + REACH - GAP * tap
        term = weight[tap : tap + 1, :] * framed[start : start + rows, :]
        acc = term if acc is None else acc + term
    out[...] = acc.astype(jnp.bfloat16)


def back(grad, low, high, weight):
    rows = grad.shape[0]
    return pl.pallas_call(
        back_kernel,
        out_shape=jax.ShapeDtypeStruct((rows, D), jnp.bfloat16),
        scratch_shapes=[pltpu.VMEM((rows + 2 * EDGE, D), jnp.float32)],
        compiler_params=params(60),
        name="back",
    )(grad, low, high, weight)


def swap(block, axis):
    return lax.ppermute(block, axis, SWAP)


def edges(block):
    count = lax.axis_size(TALL)
    up = [(i, i + 1) for i in range(count - 1)]
    down = [(i + 1, i) for i in range(count - 1)]
    return lax.ppermute(block[-EDGE:], TALL, up), lax.ppermute(block[:EDGE], TALL, down)


def in_order(first, own, other, axis):
    return jnp.where(
        first, jnp.concatenate([own, other], axis=axis), jnp.concatenate([other, own], axis=axis)
    )


def ring_sum(part, depth):
    ahead = [(i, (i + 1) % depth) for i in range(depth)]
    behind = [(i, (i - 1) % depth) for i in range(depth)]
    far = depth // 2
    up, down = part[far], part[far + 1]
    for step in range(1, far + 1):
        up = lax.ppermute(up, "z", ahead)
        if step < far:
            up = plus(up, part[far - step])
            down = lax.ppermute(down, "z", behind)
            if step < far - 1:
                down = plus(down, part[far + 1 + step])
    return part[0].astype(jnp.float32) + up.astype(jnp.float32) + down.astype(jnp.float32)


def gather(own, depth):
    far = depth // 2
    pair = jnp.concatenate([own, swap(own, "core")], axis=0)
    pieces = [own]
    for step in range(1, far):
        routes = [(CORES * z, CORES * ((z + step) % depth)) for z in range(depth)]
        routes += [(CORES * z + 1, CORES * ((z - step) % depth) + 1) for z in range(depth)]
        pieces.append(lax.ppermute(pair, ("z", "core"), routes))
    pieces.append(lax.ppermute(own, "z", [(z, (z + far) % depth) for z in range(depth)]))
    cut = 1 + far // 2
    near = jnp.concatenate(pieces[:cut], axis=0)
    rest = jnp.concatenate(pieces[cut:], axis=0)
    mine = [near, rest, swap(near, "y"), swap(rest, "y")]
    return mine + [swap(block, "core") for block in mine]


def plus(one, two):
    return (one.astype(jnp.float32) + two.astype(jnp.float32)).astype(jnp.bfloat16)


def shards(frames, conv_weight, qkv_weight, out_weight, cotangent):
    rows = frames.shape[0]
    depth = lax.axis_size("z")
    core = lax.axis_index("core")
    plane = lax.axis_index("y")
    first = core == 0
    place = jnp.stack([core, lax.axis_index("z")]).astype(jnp.int32)

    low, high = edges(frames)
    cot_other = swap(cotangent, "core")
    conv_own, conv_panel = conv(frames, low, high, conv_weight)
    conv_other = swap(conv_own, "core")
    queries, grads = project(place, conv_own, conv_other, cotangent, cot_other, qkv_weight, out_weight)
    panels = gather(conv_panel, depth)
    att, gq, early, late, panel, part = attention(place, queries, grads, panels, qkv_weight, depth)

    def finish(part):
        total = ring_sum(part, depth).astype(jnp.bfloat16)
        total = total.reshape((PLANES, CORES) + total.shape[-2:])
        return total[:, 0], swap(total[:, 1], "core")

    att_other = swap(att, "core")
    gq_other = swap(gq[rows:], "core")
    sums = weights(place, att, att_other, gq, conv_own, conv_other, cotangent, cot_other, panel, part)
    mixed, base = mixing(place, att, att_other, gq, gq_other, out_weight, qkv_weight)
    scattered = lax.psum_scatter(sums, "z", scatter_dimension=0, tiled=True)

    early_own, early_other = finish(early)
    late_own, late_other = finish(late)
    panel_grads = jnp.concatenate([early_own, late_own, early_other, late_other], axis=-1)
    panel_grads = plus(panel_grads[0], swap(panel_grads[1], "y"))

    def by_kind(block):
        return block.reshape(block.shape[0], OWN, 2, HEAD_DIM).transpose(0, 2, 1, 3)

    panel_full = in_order(first, by_kind(panel_grads[:, : 2 * HALF]), by_kind(panel_grads[:, 2 * HALF :]), 2).reshape(-1, 2 * D)
    grad_conv, taps = tail(base, panel_full, qkv_weight, frames, low, high)
    x_grad = back(grad_conv, *edges(grad_conv), conv_weight)

    taps = taps + swap(taps, "core")
    taps = taps + swap(taps, "y")
    distance = 1
    while distance < depth:
        taps = taps + lax.ppermute(taps, "z", [(i, i ^ distance) for i in range(depth)])
        distance *= 2
    conv_weight_grad = taps[:TAPS]

    scattered = scattered.reshape(PLANES, -1, 2 * D)
    keep = lax.dynamic_index_in_dim(scattered, plane, 0, keepdims=False)
    give = lax.dynamic_index_in_dim(scattered, 1 - plane, 0, keepdims=False)
    summed = keep.astype(jnp.float32) + swap(give, "y").astype(jnp.float32)
    summed = summed.reshape(CORES, -1, 2 * D)
    own = lax.dynamic_index_in_dim(summed, core, 0, keepdims=False)
    other = swap(lax.dynamic_index_in_dim(summed, 1 - core, 0, keepdims=False), "core")

    def columns(begin, count):
        return in_order(first, own[:, begin : begin + count], other[:, begin : begin + count], 1)

    kv_grad = in_order(first, by_kind(own[:, :D]), by_kind(other[:, :D]), 2).reshape(-1, 2 * D)
    qkv_weight_grad = jnp.concatenate([columns(D, HALF), kv_grad], axis=1)
    out_weight_grad = columns(D + HALF, HALF)
    return (mixed, x_grad, qkv_weight_grad, out_weight_grad, conv_weight_grad)


def solution(mesh):
    clips, tall = mesh.devices.shape
    grid = Mesh(
        mesh.devices.reshape(clips, tall // (PLANES * CORES), PLANES, CORES), ("clip", "z", "y", "core")
    )
    rows = P(("clip",) + TALL, None)
    in_specs = (rows, P(), P(), P(), rows)
    out_specs = (rows, rows, rows, rows, P("clip", None))
    return jax.shard_map(shards, mesh=grid, in_specs=in_specs, out_specs=out_specs, check_vma=False)
```

```python
import functools

import jax
import jax.numpy as jnp
from jax import lax
from jax.experimental import pallas as pl
from jax.experimental.pallas import tpu as pltpu
from jax.sharding import Mesh
from jax.sharding import PartitionSpec as P

D = 1024
HEADS = 8
HEAD_DIM = 128
TAPS = 5
GAP = 2
STRIDE = 8
REACH = GAP * (TAPS // 2)
EDGE = 16
CORES = 2
PLANES = 2
OWN = HEADS // CORES
HALF = OWN * HEAD_DIM
SCALE = 1.0 / HEAD_DIM**0.5
LOG2E = 1.4426950408889634
TALL = ("z", "y", "core")
SWAP = [(0, 1), (1, 0)]

NN = (((1,), (0,)), ((), ()))
NT = (((1,), (1,)), ((), ()))
TN = (((0,), (0,)), ((), ()))


def mm(a, b, dims=NN):
    return lax.dot_general(a, b, dims, preferred_element_type=jnp.float32)


def params(mib):
    return pltpu.CompilerParams(vmem_limit_bytes=mib * 1024 * 1024)


HBM = pl.BlockSpec(memory_space=pltpu.HBM)


def fetch(pairs, sems):
    copies = [pltpu.make_async_copy(source, target, sems.at[at]) for at, (source, target) in enumerate(pairs)]
    for copy in copies:
        copy.start()
    return copies


def whole(shape):
    return pl.BlockSpec(shape, lambda *_: (0,) * len(shape))


def conv_kernel(frames, low, high, weight, conv_out, conv_panel, framed, total):
    rows = frames.shape[0]
    framed[:EDGE] = low[...].astype(jnp.float32)
    framed[EDGE : EDGE + rows] = frames[...].astype(jnp.float32)
    framed[EDGE + rows :] = high[...].astype(jnp.float32)
    acc = None
    for tap in range(TAPS):
        start = EDGE - REACH + GAP * tap
        term = weight[tap : tap + 1, :] * framed[start : start + rows, :]
        acc = term if acc is None else acc + term
    conv_out[...] = acc.astype(jnp.bfloat16)
    for chunk in range(D // HEAD_DIM):
        cols = slice(chunk * HEAD_DIM, (chunk + 1) * HEAD_DIM)
        total[chunk] = acc[:, cols]
        picked = total[chunk, pl.ds(0, rows // STRIDE, stride=STRIDE), :]
        conv_panel[:, cols] = picked.astype(jnp.bfloat16)


def conv(frames, low, high, weight):
    rows = frames.shape[0]
    return pl.pallas_call(
        conv_kernel,
        out_shape=(
            jax.ShapeDtypeStruct((rows, D), jnp.bfloat16),
            jax.ShapeDtypeStruct((rows // STRIDE, D), jnp.bfloat16),
        ),
        scratch_shapes=[
            pltpu.VMEM((rows + 2 * EDGE, D), jnp.float32),
            pltpu.VMEM((D // HEAD_DIM, rows, HEAD_DIM), jnp.float32),
        ],
        compiler_params=params(16),
        name="conv",
    )(frames, low, high, weight)


def project_kernel(
    conv_own, conv_other, cot_own, cot_other, qkv_weight, out_weight, queries, grads, cot_rows, wide, tall, sems
):
    rows = conv_own.shape[0]
    core = lax.axis_index("core")
    start = pl.multiple_of(core * HALF, HALF)
    copies = fetch(
        (
            (qkv_weight.at[:, pl.ds(start, HALF)], wide),
            (out_weight.at[pl.ds(start, HALF), :], tall),
            (cot_own, cot_rows),
        ),
        sems,
    )
    copies[0].wait()
    queries[:rows, :] = mm(conv_own[...], wide[...]).astype(jnp.bfloat16)
    queries[rows:, :] = mm(conv_other[...], wide[...]).astype(jnp.bfloat16)
    copies[1].wait()
    grads[rows:, :] = mm(cot_other[...], tall[...], NT).astype(jnp.bfloat16)
    copies[2].wait()
    grads[:rows, :] = mm(cot_rows[...], tall[...], NT).astype(jnp.bfloat16)


def project(conv_own, conv_other, cot_own, cot_other, qkv_weight, out_weight):
    rows = conv_own.shape[0]
    vmem = pl.BlockSpec(memory_space=pltpu.VMEM)
    out = jax.ShapeDtypeStruct((2 * rows, HALF), jnp.bfloat16)
    return pl.pallas_call(
        project_kernel,
        in_specs=[vmem, vmem, HBM, vmem, HBM, HBM],
        out_shape=(out, out),
        scratch_shapes=[
            pltpu.VMEM((rows, D), jnp.bfloat16),
            pltpu.VMEM((D, HALF), jnp.bfloat16),
            pltpu.VMEM((HALF, D), jnp.bfloat16),
            pltpu.SemaphoreType.DMA((3,)),
        ],
        compiler_params=params(50),
        cost_estimate=pl.CostEstimate(flops=2_000_000_000, bytes_accessed=6_000_000, transcendentals=0),
        name="project",
    )(conv_own, conv_other, cot_own, cot_other, qkv_weight, out_weight)


def batches(depth):
    far = depth // 2
    near = [(0, 0), (far, 0)]
    rest = []
    for step in range(1, far):
        (near if step < far // 2 else rest).extend((step, core) for core in range(CORES))
    return near, rest


def attention_kernel(depth, place, queries, grads, *refs):
    panels, rest = refs[:8], refs[8:]
    key_weight, value_weight, att, gq, early, late, panel, part, keys, values, sems = rest
    head = pl.program_id(0)

    @pl.when(head == 0)
    def _():
        at, pairs = 0, []
        for block in panels:
            pairs.append((block, panel.at[at : at + block.shape[0]]))
            at += block.shape[0]
        for copy in fetch(pairs, sems):
            copy.wait()

    weight = jnp.concatenate([key_weight[...], value_weight[...]], axis=1)
    both = mm(panel[...], weight).astype(jnp.bfloat16)
    keys[...] = both[:, :HEAD_DIM]
    values[...] = both[:, HEAD_DIM:]
    query, grad = queries[...], grads[...]
    scores = mm(keys[...], query, NT)
    highest = jnp.max(scores, axis=0, keepdims=True)
    raised = jnp.exp2((scores - highest) * (SCALE * LOG2E))
    probs = raised * (1.0 / jnp.sum(raised, axis=0, keepdims=True))
    weights = probs.astype(jnp.bfloat16)
    attended = mm(values[...], weights, TN).astype(jnp.bfloat16)
    grad_t = grad.astype(jnp.float32).T
    delta = jnp.sum(grad_t * attended.astype(jnp.float32), axis=0, keepdims=True)
    dprob = mm(values[...], grad, NT)
    grad_scores = (probs * (dprob - delta)).astype(jnp.bfloat16)
    att[...] = attended.astype(jnp.float32).T.astype(jnp.bfloat16)
    gq[...] = (mm(keys[...], grad_scores, TN) * SCALE).T.astype(jnp.bfloat16)
    part[:, :HEAD_DIM] = (mm(grad_scores, query) * SCALE).astype(jnp.bfloat16)
    part[:, HEAD_DIM:] = mm(weights, grad).astype(jnp.bfloat16)

    piece = early.shape[3]
    sign = 2 * place[0] - 1

    def store(out):
        at = 0
        for lane in range(CORES):
            for plane in range(PLANES):
                for batch in batches(depth):
                    for step, core in batch:
                        steps = step * (1 - 2 * lane)
                        ahead = lax.rem(depth + sign * steps, depth)
                        out[ahead, plane, core ^ lane] = part[at : at + piece, :]
                        at += piece

    @pl.when(head < OWN // 2)
    def _():
        store(early)

    @pl.when(head >= OWN // 2)
    def _():
        store(late)


def attention(place, queries, grads, panels, qkv_weight, depth):
    tokens = queries.shape[0]
    total = sum(block.shape[0] for block in panels)
    piece = total // depth // PLANES // CORES
    wide = 2 * HEAD_DIM
    head = pl.BlockSpec((tokens, HEAD_DIM), lambda h, place: (0, h))
    shape = (depth, PLANES, CORES, piece, wide)
    parts = jax.ShapeDtypeStruct(shape[:-1] + (HALF,), jnp.bfloat16)
    return pl.pallas_call(
        functools.partial(attention_kernel, depth),
        grid_spec=pltpu.PrefetchScalarGridSpec(
            num_scalar_prefetch=1,
            grid=(OWN,),
            in_specs=[head, head]
            + [HBM] * len(panels)
            + [
                pl.BlockSpec((D, HEAD_DIM), lambda h, place: (0, HEADS + OWN * place[0] + h)),
                pl.BlockSpec((D, HEAD_DIM), lambda h, place: (0, 2 * HEADS + OWN * place[0] + h)),
            ],
            out_specs=[
                head,
                head,
                pl.BlockSpec(shape, lambda h, place: (0, 0, 0, 0, jnp.minimum(h, OWN // 2 - 1))),
                pl.BlockSpec(shape, lambda h, place: (0, 0, 0, 0, jnp.maximum(h - OWN // 2, 0))),
                whole((total, D)),
                pl.BlockSpec((total, wide), lambda h, place: (0, h)),
            ],
            scratch_shapes=[
                pltpu.VMEM((total, HEAD_DIM), jnp.bfloat16),
                pltpu.VMEM((total, HEAD_DIM), jnp.bfloat16),
                pltpu.SemaphoreType.DMA((len(panels),)),
            ],
        ),
        out_shape=(
            jax.ShapeDtypeStruct((tokens, HALF), jnp.bfloat16),
            jax.ShapeDtypeStruct((tokens, HALF), jnp.bfloat16),
            parts,
            parts,
            jax.ShapeDtypeStruct((total, D), jnp.bfloat16),
            jax.ShapeDtypeStruct((total, 2 * HALF), jnp.bfloat16),
        ),
        compiler_params=params(40),
        cost_estimate=pl.CostEstimate(flops=8_000_000_000, bytes_accessed=16_000_000, transcendentals=2_000_000),
        name="attention",
    )(place, queries, grads, *panels, qkv_weight, qkv_weight)


def weights_kernel(place, att, att_other, gq, conv_own, conv_other, cot_own, cot_other, panel, part, sums):
    core = place[0]
    rows = conv_own.shape[0]
    own = pl.ds(pl.multiple_of(core * HALF, HALF), HALF)
    away = pl.ds(pl.multiple_of((1 - core) * HALF, HALF), HALF)

    @pl.when(pl.program_id(0) == 0)
    def _():
        sums[...] = mm(panel[...], part[...], TN).astype(jnp.bfloat16)

    @pl.when(pl.program_id(0) == 1)
    def _():
        queries = mm(conv_own[...], gq[:rows, :], TN) + mm(conv_other[...], gq[rows:, :], TN)
        sums[:, :HALF] = queries.astype(jnp.bfloat16)
        mine = mm(att[:rows, :], cot_own[:, own], TN) + mm(att[rows:, :], cot_other[:, own], TN)
        sums[own, HALF:] = mine.astype(jnp.bfloat16)
        other = mm(att_other[rows:, :], cot_own[:, own], TN) + mm(att_other[:rows, :], cot_other[:, own], TN)
        sums[away, HALF:] = other.astype(jnp.bfloat16)


def weights(place, *ins):
    return pl.pallas_call(
        weights_kernel,
        grid_spec=pltpu.PrefetchScalarGridSpec(
            num_scalar_prefetch=1,
            grid=(2,),
            in_specs=[whole(item.shape) for item in ins],
            out_specs=pl.BlockSpec((D, D), lambda i, place: (0, i)),
        ),
        out_shape=jax.ShapeDtypeStruct((D, 2 * D), jnp.bfloat16),
        compiler_params=params(40),
        cost_estimate=pl.CostEstimate(flops=4_000_000_000, bytes_accessed=12_000_000, transcendentals=0),
        name="weights",
    )(place, *ins)


def mixing_kernel(att, att_other, gq, gq_other, out_weight, qkv_weight, mixed, base, first, second, sems):
    core = lax.axis_index("core")
    rows = mixed.shape[0]
    own = pl.ds(pl.multiple_of(core * HALF, HALF), HALF)
    away = pl.ds(pl.multiple_of((1 - core) * HALF, HALF), HALF)
    copies = fetch(((out_weight, first), (qkv_weight.at[:, pl.ds(0, D)], second)), sems)
    copies[0].wait()
    blend = mm(att[:rows, :], first[own, :]) + mm(att_other[rows:, :], first[away, :])
    mixed[...] = blend.astype(jnp.bfloat16)
    copies[1].wait()
    base[...] = mm(gq[:rows, :], second[:, own], NT) + mm(gq_other[...], second[:, away], NT)


def mixing(att, att_other, gq, gq_other, out_weight, qkv_weight):
    rows = gq_other.shape[0]
    vmem = pl.BlockSpec(memory_space=pltpu.VMEM)
    return pl.pallas_call(
        mixing_kernel,
        in_specs=[vmem] * 4 + [HBM] * 2,
        out_shape=(
            jax.ShapeDtypeStruct((rows, D), jnp.bfloat16),
            jax.ShapeDtypeStruct((rows, D), jnp.float32),
        ),
        scratch_shapes=[
            pltpu.VMEM((D, D), jnp.bfloat16),
            pltpu.VMEM((D, D), jnp.bfloat16),
            pltpu.SemaphoreType.DMA((2,)),
        ],
        compiler_params=params(50),
        cost_estimate=pl.CostEstimate(flops=1_000_000_000, bytes_accessed=8_000_000, transcendentals=0),
        name="mixing",
    )(att, att_other, gq, gq_other, out_weight, qkv_weight)


def by_kind(block):
    pieces = [block[:, at : at + HEAD_DIM] for at in range(0, block.shape[1], HEAD_DIM)]
    return jnp.concatenate(pieces[0::2], axis=1), jnp.concatenate(pieces[1::2], axis=1)


def halves():
    core = lax.axis_index("core")
    return [pl.ds(pl.multiple_of(at * HALF, HALF), HALF) for at in (core, 1 - core)]


def tail_kernel(
    base, panel_own, panel_other, qkv_weight, frames, low, high, grad_out, taps, framed, total, weight, sems
):
    rows = frames.shape[0]
    copies = fetch([(qkv_weight.at[:, pl.ds(D * at, D)], weight.at[at - 1]) for at in (1, 2)], sems)
    framed[:EDGE] = low[...].astype(jnp.float32)
    framed[EDGE : EDGE + rows] = frames[...].astype(jnp.float32)
    framed[EDGE + rows :] = high[...].astype(jnp.float32)
    panel = plus(panel_own[...], panel_other[...])
    kinds = [by_kind(panel[:, :D]), by_kind(panel[:, D:])]
    extra = None
    for kind in range(2):
        copies[kind].wait()
        for block, cols in zip(kinds, halves()):
            term = mm(block[kind], weight[kind, :, cols], NT)
            extra = term if extra is None else extra + term
    for chunk in range(D // HEAD_DIM):
        cols = slice(chunk * HEAD_DIM, (chunk + 1) * HEAD_DIM)
        total[chunk] = base[:, cols]
        at = (chunk, pl.ds(0, rows // STRIDE, stride=STRIDE), slice(None))
        total[at] = total[at] + extra[:, cols]
        grad = total[chunk].astype(jnp.bfloat16)
        grad_out[:, cols] = grad
        grad = grad.astype(jnp.float32)
        for tap in range(TAPS):
            start = EDGE - REACH + GAP * tap
            term = grad * framed[start : start + rows, cols]
            taps[tap : tap + 1, cols] = jnp.sum(term, axis=0, keepdims=True)
    taps[TAPS:, :] = jnp.zeros((taps.shape[0] - TAPS, D), jnp.float32)


def tail(base, panel_own, panel_other, qkv_weight, frames, low, high):
    rows = frames.shape[0]
    vmem = pl.BlockSpec(memory_space=pltpu.VMEM)
    return pl.pallas_call(
        tail_kernel,
        in_specs=[vmem, vmem, vmem, HBM, vmem, vmem, vmem],
        out_shape=(
            jax.ShapeDtypeStruct((rows, D), jnp.bfloat16),
            jax.ShapeDtypeStruct((8, D), jnp.float32),
        ),
        scratch_shapes=[
            pltpu.VMEM((rows + 2 * EDGE, D), jnp.float32),
            pltpu.VMEM((D // HEAD_DIM, rows, HEAD_DIM), jnp.float32),
            pltpu.VMEM((2, D, D), jnp.bfloat16),
            pltpu.SemaphoreType.DMA((2,)),
        ],
        compiler_params=params(50),
        cost_estimate=pl.CostEstimate(flops=10_000_000_000, bytes_accessed=8_000_000, transcendentals=0),
        name="tail",
    )(base, panel_own, panel_other, qkv_weight, frames, low, high)


def finish_kernel(own, other, qkv_grad, out_grad):
    for block, cols in zip((own, other), halves()):
        keys, values = by_kind(block[:, :D])
        qkv_grad[:, cols] = block[:, D : D + HALF]
        qkv_grad[:, pl.ds(cols.start + D, HALF)] = keys
        qkv_grad[:, pl.ds(cols.start + 2 * D, HALF)] = values
        out_grad[:, cols] = block[:, D + HALF :]


def finish(own, other):
    rows = own.shape[0]
    return pl.pallas_call(
        finish_kernel,
        out_shape=(
            jax.ShapeDtypeStruct((rows, 3 * D), jnp.float32),
            jax.ShapeDtypeStruct((rows, D), jnp.float32),
        ),
        compiler_params=params(16),
        cost_estimate=pl.CostEstimate(flops=15_000_000_000, bytes_accessed=1_000_000, transcendentals=0),
        name="finish",
    )(own, other)


def back_kernel(grad, low, high, weight, out, framed):
    rows = grad.shape[0]
    framed[:EDGE] = low[...].astype(jnp.float32)
    framed[EDGE : EDGE + rows] = grad[...].astype(jnp.float32)
    framed[EDGE + rows :] = high[...].astype(jnp.float32)
    acc = None
    for tap in range(TAPS):
        start = EDGE + REACH - GAP * tap
        term = weight[tap : tap + 1, :] * framed[start : start + rows, :]
        acc = term if acc is None else acc + term
    out[...] = acc.astype(jnp.bfloat16)


def back(grad, low, high, weight):
    rows = grad.shape[0]
    return pl.pallas_call(
        back_kernel,
        out_shape=jax.ShapeDtypeStruct((rows, D), jnp.bfloat16),
        scratch_shapes=[pltpu.VMEM((rows + 2 * EDGE, D), jnp.float32)],
        compiler_params=params(16),
        name="back",
    )(grad, low, high, weight)


def swap(block, axis):
    return lax.ppermute(block, axis, SWAP)


def edges(block):
    count = lax.axis_size(TALL)
    up = [(i, i + 1) for i in range(count - 1)]
    down = [(i + 1, i) for i in range(count - 1)]
    return lax.ppermute(block[-EDGE:], TALL, up), lax.ppermute(block[:EDGE], TALL, down)


def ring_sums(parts, depth, beside):
    ahead = [(i, (i + 1) % depth) for i in range(depth)]
    behind = [(i, (i - 1) % depth) for i in range(depth)]
    far = depth // 2
    ups, downs = [part[far] for part in parts], [part[far + 1] for part in parts]
    done = []
    for step in range(1, far + 1):
        sent = ups[0]
        ups = [lax.ppermute(up, "z", ahead) for up in ups]
        if step < far:
            downs = [lax.ppermute(down, "z", behind) for down in downs]
        if step <= len(beside):
            result = beside[step - 1](sent)
            parts, result = lax.optimization_barrier((parts, result))
            done.append(result)
        if step < far:
            ups = [plus(up, part[far - step]) for up, part in zip(ups, parts)]
        if step < far - 1:
            downs = [plus(down, part[far + 1 + step]) for down, part in zip(downs, parts)]
    totals = [
        part[0].astype(jnp.float32) + up.astype(jnp.float32) + down.astype(jnp.float32)
        for part, up, down in zip(parts, ups, downs)
    ]
    return totals, done


def gather(own, depth, token):
    far = depth // 2
    near = [own, lax.ppermute(own, "z", [(z, (z + far) % depth) for z in range(depth)])]
    rest = []
    pair = jnp.concatenate([own, swap(own, "core")], axis=0)
    for step in range(1, far):
        routes = [(CORES * z, CORES * ((z + step) % depth)) for z in range(depth)]
        routes += [(CORES * z + 1, CORES * ((z - step) % depth) + 1) for z in range(depth)]
        (near if step < far // 2 else rest).append(lax.ppermute(pair, ("z", "core"), routes))
    near = jnp.concatenate(near, axis=0)
    rest = jnp.concatenate(rest, axis=0)
    near, rest, token = lax.optimization_barrier((near, rest, token))
    mine = [near, rest, swap(near, "y"), swap(rest, "y")]
    return mine + [swap(block, "core") for block in mine], token


def plus(one, two):
    return (one.astype(jnp.float32) + two.astype(jnp.float32)).astype(jnp.bfloat16)


def shards(frames, conv_weight, qkv_weight, out_weight, cotangent):
    rows = frames.shape[0]
    depth = lax.axis_size("z")
    core = lax.axis_index("core")
    plane = lax.axis_index("y")
    place = jnp.stack([core, lax.axis_index("z")]).astype(jnp.int32)

    low, high = edges(frames)
    cot_other = swap(cotangent, "core")
    conv_own, conv_panel = conv(frames, low, high, conv_weight)
    conv_other = swap(conv_own, "core")
    queries, grads = project(conv_own, conv_other, cotangent, cot_other, qkv_weight, out_weight)
    panels, queries = gather(conv_panel, depth, queries)
    att, gq, early, late, panel, part = attention(place, queries, grads, panels, qkv_weight, depth)

    att_other = swap(att, "core")
    gq_other = swap(gq[rows:], "core")

    totals, (sums, (mixed, base)) = ring_sums(
        (early, late),
        depth,
        (
            lambda sent: weights(place, att, att_other, gq, conv_own, conv_other, cotangent, cot_other, panel, part),
            lambda sent: mixing(
                att, att_other, gq, lax.optimization_barrier((gq_other, sent))[0], out_weight, qkv_weight
            ),
        ),
    )
    scattered = lax.psum_scatter(sums, "z", scatter_dimension=0, tiled=True)

    def for_cores(total):
        total = total.astype(jnp.bfloat16).reshape((PLANES, CORES) + total.shape[-2:])
        return total[:, 0], swap(total[:, 1], "core")

    (early_own, early_other), (late_own, late_other) = for_cores(totals[0]), for_cores(totals[1])
    panel_grads = jnp.concatenate([early_own, late_own, early_other, late_other], axis=-1)
    panel_away = swap(panel_grads[1], "y")
    grad_conv, taps = tail(base, panel_grads[0], panel_away, qkv_weight, frames, low, high)
    x_grad = back(grad_conv, *edges(grad_conv), conv_weight)

    taps = taps + swap(taps, "core")
    taps = taps + swap(taps, "y")
    distance = 1
    while distance < depth:
        taps = taps + lax.ppermute(taps, "z", [(i, i ^ distance) for i in range(depth)])
        distance *= 2
    conv_weight_grad = taps[:TAPS]

    scattered = scattered.reshape(PLANES, -1, 2 * D)
    keep = lax.dynamic_index_in_dim(scattered, plane, 0, keepdims=False)
    give = lax.dynamic_index_in_dim(scattered, 1 - plane, 0, keepdims=False)
    summed = keep.astype(jnp.float32) + swap(give, "y").astype(jnp.float32)
    summed = summed.reshape(CORES, -1, 2 * D)
    own = lax.dynamic_index_in_dim(summed, core, 0, keepdims=False)
    other = swap(lax.dynamic_index_in_dim(summed, 1 - core, 0, keepdims=False), "core")

    qkv_weight_grad, out_weight_grad = finish(own, other)
    return (mixed, x_grad, qkv_weight_grad, out_weight_grad, conv_weight_grad)


def solution(mesh):
    clips, tall = mesh.devices.shape
    grid = Mesh(
        mesh.devices.reshape(clips, tall // (PLANES * CORES), PLANES, CORES), ("clip", "z", "y", "core")
    )
    rows = P(("clip",) + TALL, None)
    in_specs = (rows, P(), P(), P(), rows)
    out_specs = (rows, rows, rows, rows, P("clip", None))
    return jax.shard_map(shards, mesh=grid, in_specs=in_specs, out_specs=out_specs, check_vma=False)
```

```python
import functools

import jax
import jax.numpy as jnp
from jax import lax
from jax.experimental import pallas as pl
from jax.experimental.pallas import tpu as pltpu
from jax.sharding import Mesh
from jax.sharding import PartitionSpec as P

D = 1024
HEADS = 8
HEAD_DIM = 128
TAPS = 5
GAP = 2
STRIDE = 8
REACH = GAP * (TAPS // 2)
EDGE = 16
CORES = 2
PLANES = 2
OWN = HEADS // CORES
HALF = OWN * HEAD_DIM
SCALE = 1.0 / HEAD_DIM**0.5
LOG2E = 1.4426950408889634
TALL = ("z", "y", "core")
SWAP = [(0, 1), (1, 0)]

NN = (((1,), (0,)), ((), ()))
NT = (((1,), (1,)), ((), ()))
TN = (((0,), (0,)), ((), ()))


def mm(a, b, dims=NN):
    return lax.dot_general(a, b, dims, preferred_element_type=jnp.float32)


def params(mib):
    return pltpu.CompilerParams(vmem_limit_bytes=mib * 1024 * 1024)


HBM = pl.BlockSpec(memory_space=pltpu.HBM)


def fetch(pairs, sems):
    copies = [pltpu.make_async_copy(source, target, sems.at[at]) for at, (source, target) in enumerate(pairs)]
    for copy in copies:
        copy.start()
    return copies


def whole(shape):
    return pl.BlockSpec(shape, lambda *_: (0,) * len(shape))


def conv_kernel(frames, low, high, weight, conv_out, conv_panel, framed, total):
    rows = frames.shape[0]
    framed[:EDGE] = low[...].astype(jnp.float32)
    framed[EDGE : EDGE + rows] = frames[...].astype(jnp.float32)
    framed[EDGE + rows :] = high[...].astype(jnp.float32)
    acc = None
    for tap in range(TAPS):
        start = EDGE - REACH + GAP * tap
        term = weight[tap : tap + 1, :] * framed[start : start + rows, :]
        acc = term if acc is None else acc + term
    conv_out[...] = acc.astype(jnp.bfloat16)
    for chunk in range(D // HEAD_DIM):
        cols = slice(chunk * HEAD_DIM, (chunk + 1) * HEAD_DIM)
        total[chunk] = acc[:, cols]
        picked = total[chunk, pl.ds(0, rows // STRIDE, stride=STRIDE), :]
        conv_panel[:, cols] = picked.astype(jnp.bfloat16)


def conv(frames, low, high, weight):
    rows = frames.shape[0]
    return pl.pallas_call(
        conv_kernel,
        out_shape=(
            jax.ShapeDtypeStruct((rows, D), jnp.bfloat16),
            jax.ShapeDtypeStruct((rows // STRIDE, D), jnp.bfloat16),
        ),
        scratch_shapes=[
            pltpu.VMEM((rows + 2 * EDGE, D), jnp.float32),
            pltpu.VMEM((D // HEAD_DIM, rows, HEAD_DIM), jnp.float32),
        ],
        compiler_params=params(16),
        name="conv",
    )(frames, low, high, weight)


def project_kernel(
    conv_own, conv_other, cot_own, cot_other, qkv_weight, out_weight, queries, grads, cot_rows, wide, tall, sems
):
    rows = conv_own.shape[0]
    core = lax.axis_index("core")
    start = pl.multiple_of(core * HALF, HALF)
    copies = fetch(
        (
            (qkv_weight.at[:, pl.ds(start, HALF)], wide),
            (out_weight.at[pl.ds(start, HALF), :], tall),
            (cot_own, cot_rows),
        ),
        sems,
    )
    copies[0].wait()
    queries[:rows, :] = mm(conv_own[...], wide[...]).astype(jnp.bfloat16)
    queries[rows:, :] = mm(conv_other[...], wide[...]).astype(jnp.bfloat16)
    copies[1].wait()
    grads[rows:, :] = mm(cot_other[...], tall[...], NT).astype(jnp.bfloat16)
    copies[2].wait()
    grads[:rows, :] = mm(cot_rows[...], tall[...], NT).astype(jnp.bfloat16)


def project(conv_own, conv_other, cot_own, cot_other, qkv_weight, out_weight):
    rows = conv_own.shape[0]
    vmem = pl.BlockSpec(memory_space=pltpu.VMEM)
    out = jax.ShapeDtypeStruct((2 * rows, HALF), jnp.bfloat16)
    return pl.pallas_call(
        project_kernel,
        in_specs=[vmem, vmem, HBM, vmem, HBM, HBM],
        out_shape=(out, out),
        scratch_shapes=[
            pltpu.VMEM((rows, D), jnp.bfloat16),
            pltpu.VMEM((D, HALF), jnp.bfloat16),
            pltpu.VMEM((HALF, D), jnp.bfloat16),
            pltpu.SemaphoreType.DMA((3,)),
        ],
        compiler_params=params(50),
        cost_estimate=pl.CostEstimate(flops=2_000_000_000, bytes_accessed=6_000_000, transcendentals=0),
        name="project",
    )(conv_own, conv_other, cot_own, cot_other, qkv_weight, out_weight)


def batches(depth):
    far = depth // 2
    near = [(0, 0), (far, 0)]
    rest = []
    for step in range(1, far):
        (near if step < far // 2 else rest).extend((step, core) for core in range(CORES))
    return near, rest


def attention_kernel(depth, queries, grads, *refs):
    panels, rest = refs[:8], refs[8:]
    qkv_weight, att, gq, early, late, panel, part, keys, values, weight, sems, weight_sems = rest
    head = pl.program_id(0)
    core = lax.axis_index("core")

    def columns(at, kind):
        start = pl.multiple_of((kind * HEADS + core * OWN + at) * HEAD_DIM, HEAD_DIM)
        return pltpu.make_async_copy(
            qkv_weight.at[:, pl.ds(start, HEAD_DIM)],
            weight.at[at, :, pl.ds((kind - 1) * HEAD_DIM, HEAD_DIM)],
            weight_sems.at[at, kind - 1],
        )

    @pl.when(head == 0)
    def _():
        at, pairs = 0, []
        for block in panels:
            pairs.append((block, panel.at[at : at + block.shape[0]]))
            at += block.shape[0]
        copies = fetch(pairs, sems)
        for at in range(OWN):
            for kind in (1, 2):
                columns(at, kind).start()
        for copy in copies:
            copy.wait()

    for kind in (1, 2):
        columns(head, kind).wait()
    both = mm(panel[...], weight[head]).astype(jnp.bfloat16)
    keys[...] = both[:, :HEAD_DIM]
    values[...] = both[:, HEAD_DIM:]
    query, grad = queries[...], grads[...]
    scores = mm(keys[...], query, NT)
    highest = jnp.max(scores, axis=0, keepdims=True)
    raised = jnp.exp2((scores - highest) * (SCALE * LOG2E))
    probs = raised * (1.0 / jnp.sum(raised, axis=0, keepdims=True))
    weights = probs.astype(jnp.bfloat16)
    attended = mm(values[...], weights, TN).astype(jnp.bfloat16)
    grad_t = grad.astype(jnp.float32).T
    delta = jnp.sum(grad_t * attended.astype(jnp.float32), axis=0, keepdims=True)
    dprob = mm(values[...], grad, NT)
    grad_scores = (probs * (dprob - delta)).astype(jnp.bfloat16)
    att[...] = attended.astype(jnp.float32).T.astype(jnp.bfloat16)
    gq[...] = (mm(keys[...], grad_scores, TN) * SCALE).T.astype(jnp.bfloat16)
    part[:, :HEAD_DIM] = (mm(grad_scores, query) * SCALE).astype(jnp.bfloat16)
    part[:, HEAD_DIM:] = mm(weights, grad).astype(jnp.bfloat16)

    piece = early.shape[3]
    sign = 2 * core - 1

    def store(out):
        at = 0
        for lane in range(CORES):
            for plane in range(PLANES):
                for batch in batches(depth):
                    for step, sender in batch:
                        steps = step * (1 - 2 * lane)
                        ahead = lax.rem(depth + sign * steps, depth)
                        out[ahead, plane, sender ^ lane] = part[at : at + piece, :]
                        at += piece

    @pl.when(head < OWN // 2)
    def _():
        store(early)

    @pl.when(head >= OWN // 2)
    def _():
        store(late)


def attention(queries, grads, panels, qkv_weight, depth):
    tokens = queries.shape[0]
    total = sum(block.shape[0] for block in panels)
    piece = total // depth // PLANES // CORES
    wide = 2 * HEAD_DIM
    head = pl.BlockSpec((tokens, HEAD_DIM), lambda h: (0, h))
    shape = (depth, PLANES, CORES, piece, wide)
    parts = jax.ShapeDtypeStruct(shape[:-1] + (HALF,), jnp.bfloat16)
    return pl.pallas_call(
        functools.partial(attention_kernel, depth),
        grid=(OWN,),
        in_specs=[head, head] + [HBM] * len(panels) + [HBM],
        out_specs=[
            head,
            head,
            pl.BlockSpec(shape, lambda h: (0, 0, 0, 0, jnp.minimum(h, OWN // 2 - 1))),
            pl.BlockSpec(shape, lambda h: (0, 0, 0, 0, jnp.maximum(h - OWN // 2, 0))),
            whole((total, D)),
            pl.BlockSpec((total, wide), lambda h: (0, h)),
        ],
        scratch_shapes=[
            pltpu.VMEM((total, HEAD_DIM), jnp.bfloat16),
            pltpu.VMEM((total, HEAD_DIM), jnp.bfloat16),
            pltpu.VMEM((OWN, D, wide), jnp.bfloat16),
            pltpu.SemaphoreType.DMA((len(panels),)),
            pltpu.SemaphoreType.DMA((OWN, 2)),
        ],
        out_shape=(
            jax.ShapeDtypeStruct((tokens, HALF), jnp.bfloat16),
            jax.ShapeDtypeStruct((tokens, HALF), jnp.bfloat16),
            parts,
            parts,
            jax.ShapeDtypeStruct((total, D), jnp.bfloat16),
            jax.ShapeDtypeStruct((total, 2 * HALF), jnp.bfloat16),
        ),
        compiler_params=params(44),
        cost_estimate=pl.CostEstimate(flops=8_000_000_000, bytes_accessed=16_000_000, transcendentals=2_000_000),
        name="attention",
    )(queries, grads, *panels, qkv_weight)


def weights_kernel(depth, att, att_other, gq, conv_own, conv_other, cot_own, cot_other, panel, part, sums):
    core, plane = lax.axis_index("core"), lax.axis_index("y")
    rows = conv_own.shape[0]
    own, away = halves()
    size = D // depth // PLANES // CORES

    def store(value, first, cols):
        for at in range(0, value.shape[0], size):
            block = first + at // size
            other_core, other_plane = lax.rem(block + core, CORES), lax.rem(block // CORES + plane, PLANES)
            to = (block // (PLANES * CORES) * PLANES + other_plane) * CORES + other_core
            sums[pl.ds(pl.multiple_of(to * size, size), size), cols] = value[at : at + size].astype(jnp.bfloat16)

    @pl.when(pl.program_id(0) == 0)
    def _():
        store(mm(panel[...], part[...], TN), 0, slice(None))

    @pl.when(pl.program_id(0) == 1)
    def _():
        queries = mm(conv_own[...], gq[:rows, :], TN) + mm(conv_other[...], gq[rows:, :], TN)
        store(queries, 0, slice(0, HALF))
        mine = mm(att[:rows, :], cot_own[:, own], TN) + mm(att[rows:, :], cot_other[:, own], TN)
        store(mine, core * (HALF // size), slice(HALF, D))
        other = mm(att_other[rows:, :], cot_own[:, own], TN) + mm(att_other[:rows, :], cot_other[:, own], TN)
        store(other, (1 - core) * (HALF // size), slice(HALF, D))


def weights(depth, *ins):
    return pl.pallas_call(
        functools.partial(weights_kernel, depth),
        grid=(2,),
        in_specs=[whole(item.shape) for item in ins],
        out_specs=pl.BlockSpec((D, D), lambda i: (0, i)),
        out_shape=jax.ShapeDtypeStruct((D, 2 * D), jnp.bfloat16),
        compiler_params=params(47),
        cost_estimate=pl.CostEstimate(flops=4_000_000_000, bytes_accessed=12_000_000, transcendentals=0),
        name="weights",
    )(*ins)


def mixing_kernel(att, att_other, gq, gq_other, out_weight, qkv_weight, mixed, base, first, second, sems):
    core = lax.axis_index("core")
    rows = mixed.shape[0]
    own = pl.ds(pl.multiple_of(core * HALF, HALF), HALF)
    away = pl.ds(pl.multiple_of((1 - core) * HALF, HALF), HALF)
    copies = fetch(((out_weight, first), (qkv_weight.at[:, pl.ds(0, D)], second)), sems)
    copies[0].wait()
    blend = mm(att[:rows, :], first[own, :]) + mm(att_other[rows:, :], first[away, :])
    mixed[...] = blend.astype(jnp.bfloat16)
    copies[1].wait()
    base[...] = mm(gq[:rows, :], second[:, own], NT) + mm(gq_other[...], second[:, away], NT)


def mixing(att, att_other, gq, gq_other, out_weight, qkv_weight):
    rows = gq_other.shape[0]
    vmem = pl.BlockSpec(memory_space=pltpu.VMEM)
    return pl.pallas_call(
        mixing_kernel,
        in_specs=[vmem] * 4 + [HBM] * 2,
        out_shape=(
            jax.ShapeDtypeStruct((rows, D), jnp.bfloat16),
            jax.ShapeDtypeStruct((rows, D), jnp.float32),
        ),
        scratch_shapes=[
            pltpu.VMEM((D, D), jnp.bfloat16),
            pltpu.VMEM((D, D), jnp.bfloat16),
            pltpu.SemaphoreType.DMA((2,)),
        ],
        compiler_params=params(50),
        cost_estimate=pl.CostEstimate(flops=1_000_000_000, bytes_accessed=8_000_000, transcendentals=0),
        name="mixing",
    )(att, att_other, gq, gq_other, out_weight, qkv_weight)


def by_kind(block):
    pieces = [block[:, at : at + HEAD_DIM] for at in range(0, block.shape[1], HEAD_DIM)]
    return jnp.concatenate(pieces[0::2], axis=1), jnp.concatenate(pieces[1::2], axis=1)


def halves():
    core = lax.axis_index("core")
    return [pl.ds(pl.multiple_of(at * HALF, HALF), HALF) for at in (core, 1 - core)]


def tail_kernel(
    base, panel_own, panel_other, qkv_weight, frames, low, high, grad_out, taps, framed, total, weight, sems
):
    rows = frames.shape[0]
    copies = fetch([(qkv_weight.at[:, pl.ds(D * at, D)], weight.at[at - 1]) for at in (1, 2)], sems)
    framed[:EDGE] = low[...].astype(jnp.float32)
    framed[EDGE : EDGE + rows] = frames[...].astype(jnp.float32)
    framed[EDGE + rows :] = high[...].astype(jnp.float32)
    panel = plus(panel_own[...], panel_other[...])
    kinds = [by_kind(panel[:, :D]), by_kind(panel[:, D:])]
    extra = None
    for kind in range(2):
        copies[kind].wait()
        for block, cols in zip(kinds, halves()):
            term = mm(block[kind], weight[kind, :, cols], NT)
            extra = term if extra is None else extra + term
    for chunk in range(D // HEAD_DIM):
        cols = slice(chunk * HEAD_DIM, (chunk + 1) * HEAD_DIM)
        total[chunk] = base[:, cols]
        at = (chunk, pl.ds(0, rows // STRIDE, stride=STRIDE), slice(None))
        total[at] = total[at] + extra[:, cols]
        grad = total[chunk].astype(jnp.bfloat16)
        grad_out[:, cols] = grad
        grad = grad.astype(jnp.float32)
        for tap in range(TAPS):
            start = EDGE - REACH + GAP * tap
            term = grad * framed[start : start + rows, cols]
            taps[tap : tap + 1, cols] = jnp.sum(term, axis=0, keepdims=True)
    taps[TAPS:, :] = jnp.zeros((taps.shape[0] - TAPS, D), jnp.float32)


def tail(base, panel_own, panel_other, qkv_weight, frames, low, high):
    rows = frames.shape[0]
    vmem = pl.BlockSpec(memory_space=pltpu.VMEM)
    return pl.pallas_call(
        tail_kernel,
        in_specs=[vmem, vmem, vmem, HBM, vmem, vmem, vmem],
        out_shape=(
            jax.ShapeDtypeStruct((rows, D), jnp.bfloat16),
            jax.ShapeDtypeStruct((8, D), jnp.float32),
        ),
        scratch_shapes=[
            pltpu.VMEM((rows + 2 * EDGE, D), jnp.float32),
            pltpu.VMEM((D // HEAD_DIM, rows, HEAD_DIM), jnp.float32),
            pltpu.VMEM((2, D, D), jnp.bfloat16),
            pltpu.SemaphoreType.DMA((2,)),
        ],
        compiler_params=params(50),
        cost_estimate=pl.CostEstimate(flops=20_000_000_000, bytes_accessed=8_000_000, transcendentals=0),
        name="tail",
    )(base, panel_own, panel_other, qkv_weight, frames, low, high)


def finish_kernel(own, other, qkv_grad, out_grad):
    for block, cols in zip((own, other), halves()):
        keys, values = by_kind(block[:, :D])
        qkv_grad[:, cols] = block[:, D : D + HALF]
        qkv_grad[:, pl.ds(cols.start + D, HALF)] = keys
        qkv_grad[:, pl.ds(cols.start + 2 * D, HALF)] = values
        out_grad[:, cols] = block[:, D + HALF :]


def finish(own, other):
    rows = own.shape[0]
    return pl.pallas_call(
        finish_kernel,
        out_shape=(
            jax.ShapeDtypeStruct((rows, 3 * D), jnp.float32),
            jax.ShapeDtypeStruct((rows, D), jnp.float32),
        ),
        compiler_params=params(16),
        cost_estimate=pl.CostEstimate(flops=3_000_000_000, bytes_accessed=1_000_000, transcendentals=0),
        name="finish",
    )(own, other)


def back_kernel(grad, low, high, weight, out, framed):
    rows = grad.shape[0]
    framed[:EDGE] = low[...].astype(jnp.float32)
    framed[EDGE : EDGE + rows] = grad[...].astype(jnp.float32)
    framed[EDGE + rows :] = high[...].astype(jnp.float32)
    acc = None
    for tap in range(TAPS):
        start = EDGE + REACH - GAP * tap
        term = weight[tap : tap + 1, :] * framed[start : start + rows, :]
        acc = term if acc is None else acc + term
    out[...] = acc.astype(jnp.bfloat16)


def back(grad, low, high, weight):
    rows = grad.shape[0]
    return pl.pallas_call(
        back_kernel,
        out_shape=jax.ShapeDtypeStruct((rows, D), jnp.bfloat16),
        scratch_shapes=[pltpu.VMEM((rows + 2 * EDGE, D), jnp.float32)],
        compiler_params=params(16),
        name="back",
    )(grad, low, high, weight)


def swap(block, axis):
    return lax.ppermute(block, axis, SWAP)


def edges(block):
    count = lax.axis_size(TALL)
    up = [(i, i + 1) for i in range(count - 1)]
    down = [(i + 1, i) for i in range(count - 1)]
    return lax.ppermute(block[-EDGE:], TALL, up), lax.ppermute(block[:EDGE], TALL, down)


def ring_sums(parts, depth, beside):
    ahead = [(i, (i + 1) % depth) for i in range(depth)]
    behind = [(i, (i - 1) % depth) for i in range(depth)]
    far = depth // 2
    ups, downs = [part[far] for part in parts], [part[far + 1] for part in parts]
    done = []
    for step in range(1, far + 1):
        sent = ups[0]
        ups = [lax.ppermute(up, "z", ahead) for up in ups]
        if step < far:
            downs = [lax.ppermute(down, "z", behind) for down in downs]
        if step <= len(beside):
            result = beside[step - 1](sent)
            parts, result = lax.optimization_barrier((parts, result))
            done.append(result)
        if step < far:
            ups = [plus(up, part[far - step]) for up, part in zip(ups, parts)]
        if step < far - 1:
            downs = [plus(down, part[far + 1 + step]) for down, part in zip(downs, parts)]
    totals = [
        part[0].astype(jnp.float32) + up.astype(jnp.float32) + down.astype(jnp.float32)
        for part, up, down in zip(parts, ups, downs)
    ]
    return totals, done


def gather(own, depth, token):
    far = depth // 2
    near = [own, lax.ppermute(own, "z", [(z, (z + far) % depth) for z in range(depth)])]
    rest = []
    pair = jnp.concatenate([own, swap(own, "core")], axis=0)
    for step in range(1, far):
        routes = [(CORES * z, CORES * ((z + step) % depth)) for z in range(depth)]
        routes += [(CORES * z + 1, CORES * ((z - step) % depth) + 1) for z in range(depth)]
        (near if step < far // 2 else rest).append(lax.ppermute(pair, ("z", "core"), routes))
    near = jnp.concatenate(near, axis=0)
    rest = jnp.concatenate(rest, axis=0)
    near, rest, token = lax.optimization_barrier((near, rest, token))
    mine = [near, rest, swap(near, "y"), swap(rest, "y")]
    return mine + [swap(block, "core") for block in mine], token


def plus(one, two):
    return (one.astype(jnp.float32) + two.astype(jnp.float32)).astype(jnp.bfloat16)


def shards(frames, conv_weight, qkv_weight, out_weight, cotangent):
    rows = frames.shape[0]
    depth = lax.axis_size("z")

    low, high = edges(frames)
    cot_other = swap(cotangent, "core")
    conv_own, conv_panel = conv(frames, low, high, conv_weight)
    conv_other = swap(conv_own, "core")
    queries, grads = project(conv_own, conv_other, cotangent, cot_other, qkv_weight, out_weight)
    panels, queries = gather(conv_panel, depth, queries)
    att, gq, early, late, panel, part = attention(queries, grads, panels, qkv_weight, depth)

    att_other = swap(att, "core")
    gq_other = swap(gq[rows:], "core")

    totals, (sums, (mixed, base)) = ring_sums(
        (early, late),
        depth,
        (
            lambda sent: weights(depth, att, att_other, gq, conv_own, conv_other, cotangent, cot_other, panel, part),
            lambda sent: mixing(
                att, att_other, gq, lax.optimization_barrier((gq_other, sent))[0], out_weight, qkv_weight
            ),
        ),
    )
    scattered = lax.psum_scatter(sums, "z", scatter_dimension=0, tiled=True)

    def for_cores(total):
        total = total.astype(jnp.bfloat16).reshape((PLANES, CORES) + total.shape[-2:])
        return total[:, 0], swap(total[:, 1], "core")

    (early_own, early_other), (late_own, late_other) = for_cores(totals[0]), for_cores(totals[1])
    panel_grads = jnp.concatenate([early_own, late_own, early_other, late_other], axis=-1)
    panel_away = swap(panel_grads[1], "y")
    grad_conv, taps = tail(base, panel_grads[0], panel_away, qkv_weight, frames, low, high)
    x_grad = back(grad_conv, *edges(grad_conv), conv_weight)

    taps = taps + swap(taps, "core")
    taps = taps + swap(taps, "y")
    scattered, x_grad, taps = lax.optimization_barrier((scattered, x_grad, taps))
    distance = 1
    while distance < depth:
        taps = taps + lax.ppermute(taps, "z", [(i, i ^ distance) for i in range(depth)])
        distance *= 2
    conv_weight_grad = taps[:TAPS]

    half = scattered.shape[0] // PLANES
    summed = scattered[:half].astype(jnp.float32) + swap(scattered[half:], "y").astype(jnp.float32)
    own, other = summed[: half // CORES], swap(summed[half // CORES :], "core")
    qkv_weight_grad, out_weight_grad = finish(own, other)
    return (mixed, x_grad, qkv_weight_grad, out_weight_grad, conv_weight_grad)


def solution(mesh):
    clips, tall = mesh.devices.shape
    grid = Mesh(
        mesh.devices.reshape(clips, tall // (PLANES * CORES), PLANES, CORES), ("clip", "z", "y", "core")
    )
    rows = P(("clip",) + TALL, None)
    in_specs = (rows, P(), P(), P(), rows)
    out_specs = (rows, rows, rows, rows, P("clip", None))
    return jax.shard_map(shards, mesh=grid, in_specs=in_specs, out_specs=out_specs, check_vma=False)
```

```python
import functools

import jax
import jax.numpy as jnp
from jax import lax
from jax.experimental import pallas as pl
from jax.experimental.pallas import tpu as pltpu
from jax.sharding import Mesh
from jax.sharding import PartitionSpec as P

D = 1024
HEADS = 8
HEAD_DIM = 128
TAPS = 5
GAP = 2
STRIDE = 8
REACH = GAP * (TAPS // 2)
EDGE = 16
CORES = 2
PLANES = 2
OWN = HEADS // CORES
HALF = OWN * HEAD_DIM
SCALE = 1.0 / HEAD_DIM**0.5
LOG2E = 1.4426950408889634
TALL = ("z", "y", "core")
SWAP = [(0, 1), (1, 0)]

NN = (((1,), (0,)), ((), ()))
NT = (((1,), (1,)), ((), ()))
TN = (((0,), (0,)), ((), ()))


def mm(a, b, dims=NN):
    return lax.dot_general(a, b, dims, preferred_element_type=jnp.float32)


def params(mib):
    return pltpu.CompilerParams(vmem_limit_bytes=mib * 1024 * 1024)


HBM = pl.BlockSpec(memory_space=pltpu.HBM)


def fetch(pairs, sems):
    copies = [pltpu.make_async_copy(source, target, sems.at[at]) for at, (source, target) in enumerate(pairs)]
    for copy in copies:
        copy.start()
    return copies


def stacked(blocks, target):
    at, pairs = 0, []
    for block in blocks:
        pairs.append((block, target.at[at : at + block.shape[0]]))
        at += block.shape[0]
    return pairs


def whole(shape):
    return pl.BlockSpec(shape, lambda *_: (0,) * len(shape))


def conv_kernel(frames, low, high, weight, conv_out, conv_panel, framed, total):
    rows = frames.shape[0]
    framed[:EDGE] = low[...].astype(jnp.float32)
    framed[EDGE : EDGE + rows] = frames[...].astype(jnp.float32)
    framed[EDGE + rows :] = high[...].astype(jnp.float32)
    acc = None
    for tap in range(TAPS):
        start = EDGE - REACH + GAP * tap
        term = weight[tap : tap + 1, :] * framed[start : start + rows, :]
        acc = term if acc is None else acc + term
    conv_out[...] = acc.astype(jnp.bfloat16)
    for chunk in range(D // HEAD_DIM):
        cols = slice(chunk * HEAD_DIM, (chunk + 1) * HEAD_DIM)
        total[chunk] = acc[:, cols]
        picked = total[chunk, pl.ds(0, rows // STRIDE, stride=STRIDE), :]
        conv_panel[:, cols] = picked.astype(jnp.bfloat16)


def conv(frames, low, high, weight):
    rows = frames.shape[0]
    return pl.pallas_call(
        conv_kernel,
        out_shape=(
            jax.ShapeDtypeStruct((rows, D), jnp.bfloat16),
            jax.ShapeDtypeStruct((rows // STRIDE, D), jnp.bfloat16),
        ),
        scratch_shapes=[
            pltpu.VMEM((rows + 2 * EDGE, D), jnp.float32),
            pltpu.VMEM((D // HEAD_DIM, rows, HEAD_DIM), jnp.float32),
        ],
        compiler_params=params(16),
        name="conv",
    )(frames, low, high, weight)


def project_kernel(
    conv_own, conv_other, cot_own, cot_other, qkv_weight, out_weight, queries, grads, cot_rows, wide, tall, sems
):
    rows = conv_own.shape[0]
    core = lax.axis_index("core")
    start = pl.multiple_of(core * HALF, HALF)
    copies = fetch(
        (
            (qkv_weight.at[:, pl.ds(start, HALF)], wide),
            (out_weight.at[pl.ds(start, HALF), :], tall),
            (cot_own, cot_rows),
        ),
        sems,
    )
    copies[0].wait()
    queries[:rows, :] = mm(conv_own[...], wide[...]).astype(jnp.bfloat16)
    queries[rows:, :] = mm(conv_other[...], wide[...]).astype(jnp.bfloat16)
    copies[1].wait()
    grads[rows:, :] = mm(cot_other[...], tall[...], NT).astype(jnp.bfloat16)
    copies[2].wait()
    grads[:rows, :] = mm(cot_rows[...], tall[...], NT).astype(jnp.bfloat16)


def project(conv_own, conv_other, cot_own, cot_other, qkv_weight, out_weight):
    rows = conv_own.shape[0]
    vmem = pl.BlockSpec(memory_space=pltpu.VMEM)
    out = jax.ShapeDtypeStruct((2 * rows, HALF), jnp.bfloat16)
    return pl.pallas_call(
        project_kernel,
        in_specs=[vmem, vmem, HBM, vmem, HBM, HBM],
        out_shape=(out, out),
        scratch_shapes=[
            pltpu.VMEM((rows, D), jnp.bfloat16),
            pltpu.VMEM((D, HALF), jnp.bfloat16),
            pltpu.VMEM((HALF, D), jnp.bfloat16),
            pltpu.SemaphoreType.DMA((3,)),
        ],
        compiler_params=params(50),
        cost_estimate=pl.CostEstimate(flops=2_000_000_000, bytes_accessed=6_000_000, transcendentals=0),
        name="project",
    )(conv_own, conv_other, cot_own, cot_other, qkv_weight, out_weight)


def batches(depth):
    far = depth // 2
    near, rest = [(0, 0)], []
    for step in range(1, far):
        (near if step <= far // 2 else rest).extend((step, core) for core in range(CORES))
    rest.append((far, 0))
    return near, rest


def attention_kernel(depth, queries, grads, *refs):
    panels, rest = refs[:8], refs[8:]
    qkv_weight, att, gq, early, late, part, keys, values, panel, weight, sems, weight_sems = rest
    head = pl.program_id(0)
    core = lax.axis_index("core")

    def columns(at, kind):
        start = pl.multiple_of((kind * HEADS + core * OWN + at) * HEAD_DIM, HEAD_DIM)
        return pltpu.make_async_copy(
            qkv_weight.at[:, pl.ds(start, HEAD_DIM)],
            weight.at[at, :, pl.ds((kind - 1) * HEAD_DIM, HEAD_DIM)],
            weight_sems.at[at, kind - 1],
        )

    @pl.when(head == 0)
    def _():
        copies = fetch(stacked(panels, panel), sems)
        for at in range(OWN):
            for kind in (1, 2):
                columns(at, kind).start()
        for copy in copies:
            copy.wait()

    for kind in (1, 2):
        columns(head, kind).wait()
    both = mm(panel[...], weight[head]).astype(jnp.bfloat16)
    keys[...] = both[:, :HEAD_DIM]
    values[...] = both[:, HEAD_DIM:]
    query, grad = queries[...], grads[...]
    scores = mm(keys[...], query, NT)
    highest = jnp.max(scores, axis=0, keepdims=True)
    raised = jnp.exp2((scores - highest) * (SCALE * LOG2E))
    probs = raised * (1.0 / jnp.sum(raised, axis=0, keepdims=True))
    weights = probs.astype(jnp.bfloat16)
    attended = mm(values[...], weights, TN).astype(jnp.bfloat16)
    grad_t = grad.astype(jnp.float32).T
    delta = jnp.sum(grad_t * attended.astype(jnp.float32), axis=0, keepdims=True)
    dprob = mm(values[...], grad, NT)
    grad_scores = (probs * (dprob - delta)).astype(jnp.bfloat16)
    att[...] = attended.astype(jnp.float32).T.astype(jnp.bfloat16)
    gq[...] = (mm(keys[...], grad_scores, TN) * SCALE).T.astype(jnp.bfloat16)
    part[:, :HEAD_DIM] = (mm(grad_scores, query) * SCALE).astype(jnp.bfloat16)
    part[:, HEAD_DIM:] = mm(weights, grad).astype(jnp.bfloat16)

    piece = early.shape[3]
    sign = 2 * core - 1

    def store(out):
        at = 0
        for lane in range(CORES):
            for plane in range(PLANES):
                for batch in batches(depth):
                    for step, sender in batch:
                        steps = step * (1 - 2 * lane)
                        ahead = lax.rem(depth + sign * steps, depth)
                        out[ahead, plane, sender ^ lane] = part[at : at + piece, :]
                        at += piece

    @pl.when(head < OWN // 2)
    def _():
        store(early)

    @pl.when(head >= OWN // 2)
    def _():
        store(late)


def attention(queries, grads, panels, qkv_weight, depth):
    tokens = queries.shape[0]
    total = sum(block.shape[0] for block in panels)
    piece = total // depth // PLANES // CORES
    wide = 2 * HEAD_DIM
    head = pl.BlockSpec((tokens, HEAD_DIM), lambda h: (0, h))
    shape = (depth, PLANES, CORES, piece, wide)
    parts = jax.ShapeDtypeStruct(shape[:-1] + (HALF,), jnp.bfloat16)
    return pl.pallas_call(
        functools.partial(attention_kernel, depth),
        grid=(OWN,),
        in_specs=[head, head] + [HBM] * len(panels) + [HBM],
        out_specs=[
            head,
            head,
            pl.BlockSpec(shape, lambda h: (0, 0, 0, 0, jnp.minimum(h, OWN // 2 - 1))),
            pl.BlockSpec(shape, lambda h: (0, 0, 0, 0, jnp.maximum(h - OWN // 2, 0))),
            pl.BlockSpec((total, wide), lambda h: (0, h)),
        ],
        scratch_shapes=[
            pltpu.VMEM((total, HEAD_DIM), jnp.bfloat16),
            pltpu.VMEM((total, HEAD_DIM), jnp.bfloat16),
            pltpu.VMEM((total, D), jnp.bfloat16),
            pltpu.VMEM((OWN, D, wide), jnp.bfloat16),
            pltpu.SemaphoreType.DMA((len(panels),)),
            pltpu.SemaphoreType.DMA((OWN, 2)),
        ],
        out_shape=(
            jax.ShapeDtypeStruct((tokens, HALF), jnp.bfloat16),
            jax.ShapeDtypeStruct((tokens, HALF), jnp.bfloat16),
            parts,
            parts,
            jax.ShapeDtypeStruct((total, 2 * HALF), jnp.bfloat16),
        ),
        compiler_params=params(44),
        cost_estimate=pl.CostEstimate(flops=8_000_000_000, bytes_accessed=16_000_000, transcendentals=2_000_000),
        name="attention",
    )(queries, grads, *panels, qkv_weight)


def weights_kernel(depth, att, att_other, gq, conv_own, conv_other, cot_own, cot_other, part, *refs):
    panels, (sums, panel, sems) = refs[:8], refs[8:]
    core, plane = lax.axis_index("core"), lax.axis_index("y")
    rows = conv_own.shape[0]
    own, away = halves()
    size = D // depth // PLANES // CORES

    def store(value, first, cols):
        for at in range(0, value.shape[0], size):
            block = first + at // size
            other_core, other_plane = lax.rem(block + core, CORES), lax.rem(block // CORES + plane, PLANES)
            to = (block // (PLANES * CORES) * PLANES + other_plane) * CORES + other_core
            sums[pl.ds(pl.multiple_of(to * size, size), size), cols] = value[at : at + size].astype(jnp.bfloat16)

    @pl.when(pl.program_id(0) == 0)
    def _():
        for copy in fetch(stacked(panels, panel), sems):
            copy.wait()
        store(mm(panel[...], part[...], TN), 0, slice(None))

    @pl.when(pl.program_id(0) == 1)
    def _():
        queries = mm(conv_own[...], gq[:rows, :], TN) + mm(conv_other[...], gq[rows:, :], TN)
        store(queries, 0, slice(0, HALF))
        mine = mm(att[:rows, :], cot_own[:, own], TN) + mm(att[rows:, :], cot_other[:, own], TN)
        store(mine, core * (HALF // size), slice(HALF, D))
        other = mm(att_other[rows:, :], cot_own[:, own], TN) + mm(att_other[:rows, :], cot_other[:, own], TN)
        store(other, (1 - core) * (HALF // size), slice(HALF, D))


def weights(depth, panels, *ins):
    total = sum(block.shape[0] for block in panels)
    return pl.pallas_call(
        functools.partial(weights_kernel, depth),
        grid=(2,),
        in_specs=[whole(item.shape) for item in ins] + [HBM] * len(panels),
        out_specs=pl.BlockSpec((D, D), lambda i: (0, i)),
        scratch_shapes=[pltpu.VMEM((total, D), jnp.bfloat16), pltpu.SemaphoreType.DMA((len(panels),))],
        out_shape=jax.ShapeDtypeStruct((D, 2 * D), jnp.bfloat16),
        compiler_params=params(45),
        cost_estimate=pl.CostEstimate(flops=4_000_000_000, bytes_accessed=12_000_000, transcendentals=0),
        name="weights",
    )(*ins, *panels)


def mixing_kernel(att, att_other, gq, gq_other, out_weight, qkv_weight, mixed, base, first, second, sems):
    core = lax.axis_index("core")
    rows = mixed.shape[0]
    own = pl.ds(pl.multiple_of(core * HALF, HALF), HALF)
    away = pl.ds(pl.multiple_of((1 - core) * HALF, HALF), HALF)
    copies = fetch(((out_weight, first), (qkv_weight.at[:, pl.ds(0, D)], second)), sems)
    copies[0].wait()
    blend = mm(att[:rows, :], first[own, :]) + mm(att_other[rows:, :], first[away, :])
    mixed[...] = blend.astype(jnp.bfloat16)
    copies[1].wait()
    base[...] = mm(gq[:rows, :], second[:, own], NT) + mm(gq_other[...], second[:, away], NT)


def mixing(att, att_other, gq, gq_other, out_weight, qkv_weight):
    rows = gq_other.shape[0]
    vmem = pl.BlockSpec(memory_space=pltpu.VMEM)
    return pl.pallas_call(
        mixing_kernel,
        in_specs=[vmem] * 4 + [HBM] * 2,
        out_shape=(
            jax.ShapeDtypeStruct((rows, D), jnp.bfloat16),
            jax.ShapeDtypeStruct((rows, D), jnp.float32),
        ),
        scratch_shapes=[
            pltpu.VMEM((D, D), jnp.bfloat16),
            pltpu.VMEM((D, D), jnp.bfloat16),
            pltpu.SemaphoreType.DMA((2,)),
        ],
        compiler_params=params(50),
        cost_estimate=pl.CostEstimate(flops=1_000_000_000, bytes_accessed=8_000_000, transcendentals=0),
        name="mixing",
    )(att, att_other, gq, gq_other, out_weight, qkv_weight)


def by_kind(block):
    pieces = [block[:, at : at + HEAD_DIM] for at in range(0, block.shape[1], HEAD_DIM)]
    return jnp.concatenate(pieces[0::2], axis=1), jnp.concatenate(pieces[1::2], axis=1)


def halves():
    core = lax.axis_index("core")
    return [pl.ds(pl.multiple_of(at * HALF, HALF), HALF) for at in (core, 1 - core)]


def tail_kernel(
    base, panel_own, panel_other, qkv_weight, frames, low, high, grad_out, taps, framed, total, weight, sems
):
    rows = frames.shape[0]
    copies = fetch([(qkv_weight.at[:, pl.ds(D * at, D)], weight.at[at - 1]) for at in (1, 2)], sems)
    framed[:EDGE] = low[...].astype(jnp.float32)
    framed[EDGE : EDGE + rows] = frames[...].astype(jnp.float32)
    framed[EDGE + rows :] = high[...].astype(jnp.float32)
    panel = plus(panel_own[...], panel_other[...])
    kinds = [by_kind(panel[:, :D]), by_kind(panel[:, D:])]
    extra = None
    for kind in range(2):
        copies[kind].wait()
        for block, cols in zip(kinds, halves()):
            term = mm(block[kind], weight[kind, :, cols], NT)
            extra = term if extra is None else extra + term
    for chunk in range(D // HEAD_DIM):
        cols = slice(chunk * HEAD_DIM, (chunk + 1) * HEAD_DIM)
        total[chunk] = base[:, cols]
        at = (chunk, pl.ds(0, rows // STRIDE, stride=STRIDE), slice(None))
        total[at] = total[at] + extra[:, cols]
        grad = total[chunk].astype(jnp.bfloat16)
        grad_out[:, cols] = grad
        grad = grad.astype(jnp.float32)
        for tap in range(TAPS):
            start = EDGE - REACH + GAP * tap
            term = grad * framed[start : start + rows, cols]
            taps[tap : tap + 1, cols] = jnp.sum(term, axis=0, keepdims=True)
    taps[TAPS:, :] = jnp.zeros((taps.shape[0] - TAPS, D), jnp.float32)


def tail(base, panel_own, panel_other, qkv_weight, frames, low, high):
    rows = frames.shape[0]
    vmem = pl.BlockSpec(memory_space=pltpu.VMEM)
    return pl.pallas_call(
        tail_kernel,
        in_specs=[vmem, vmem, vmem, HBM, vmem, vmem, vmem],
        out_shape=(
            jax.ShapeDtypeStruct((rows, D), jnp.bfloat16),
            jax.ShapeDtypeStruct((8, D), jnp.float32),
        ),
        scratch_shapes=[
            pltpu.VMEM((rows + 2 * EDGE, D), jnp.float32),
            pltpu.VMEM((D // HEAD_DIM, rows, HEAD_DIM), jnp.float32),
            pltpu.VMEM((2, D, D), jnp.bfloat16),
            pltpu.SemaphoreType.DMA((2,)),
        ],
        compiler_params=params(50),
        cost_estimate=pl.CostEstimate(flops=20_000_000_000, bytes_accessed=8_000_000, transcendentals=0),
        name="tail",
    )(base, panel_own, panel_other, qkv_weight, frames, low, high)


def finish_kernel(own, other, qkv_grad, out_grad):
    for block, cols in zip((own, other), halves()):
        keys, values = by_kind(block[:, :D])
        qkv_grad[:, cols] = block[:, D : D + HALF]
        qkv_grad[:, pl.ds(cols.start + D, HALF)] = keys
        qkv_grad[:, pl.ds(cols.start + 2 * D, HALF)] = values
        out_grad[:, cols] = block[:, D + HALF :]


def finish(own, other):
    rows = own.shape[0]
    return pl.pallas_call(
        finish_kernel,
        out_shape=(
            jax.ShapeDtypeStruct((rows, 3 * D), jnp.float32),
            jax.ShapeDtypeStruct((rows, D), jnp.float32),
        ),
        compiler_params=params(16),
        cost_estimate=pl.CostEstimate(flops=3_000_000_000, bytes_accessed=1_000_000, transcendentals=0),
        name="finish",
    )(own, other)


def back_kernel(grad, low, high, weight, out, framed):
    rows = grad.shape[0]
    framed[:EDGE] = low[...].astype(jnp.float32)
    framed[EDGE : EDGE + rows] = grad[...].astype(jnp.float32)
    framed[EDGE + rows :] = high[...].astype(jnp.float32)
    acc = None
    for tap in range(TAPS):
        start = EDGE + REACH - GAP * tap
        term = weight[tap : tap + 1, :] * framed[start : start + rows, :]
        acc = term if acc is None else acc + term
    out[...] = acc.astype(jnp.bfloat16)


def back(grad, low, high, weight):
    rows = grad.shape[0]
    return pl.pallas_call(
        back_kernel,
        out_shape=jax.ShapeDtypeStruct((rows, D), jnp.bfloat16),
        scratch_shapes=[pltpu.VMEM((rows + 2 * EDGE, D), jnp.float32)],
        compiler_params=params(16),
        name="back",
    )(grad, low, high, weight)


def swap(block, axis):
    return lax.ppermute(block, axis, SWAP)


def edges(block):
    count = lax.axis_size(TALL)
    up = [(i, i + 1) for i in range(count - 1)]
    down = [(i + 1, i) for i in range(count - 1)]
    return lax.ppermute(block[-EDGE:], TALL, up), lax.ppermute(block[:EDGE], TALL, down)


def ring_sums(parts, depth, beside):
    ahead = [(i, (i + 1) % depth) for i in range(depth)]
    behind = [(i, (i - 1) % depth) for i in range(depth)]
    far = depth // 2
    ups, downs = [part[far] for part in parts], [part[far + 1] for part in parts]
    done = []
    for step in range(1, far + 1):
        sent = ups[0]
        ups = [lax.ppermute(up, "z", ahead) for up in ups]
        if step < far:
            downs = [lax.ppermute(down, "z", behind) for down in downs]
        if step <= len(beside):
            result = beside[step - 1](sent)
            parts, result = lax.optimization_barrier((parts, result))
            done.append(result)
        if step < far:
            ups = [plus(up, part[far - step]) for up, part in zip(ups, parts)]
        if step < far - 1:
            downs = [plus(down, part[far + 1 + step]) for down, part in zip(downs, parts)]
    totals = [
        part[0].astype(jnp.float32) + up.astype(jnp.float32) + down.astype(jnp.float32)
        for part, up, down in zip(parts, ups, downs)
    ]
    return totals, done


def gather(own, depth, token):
    far = depth // 2
    routes = [(CORES * z, CORES * ((z + 1) % depth)) for z in range(depth)]
    routes += [(CORES * z + 1, CORES * ((z - 1) % depth) + 1) for z in range(depth)]
    near, rest = [own], []
    held = jnp.concatenate([own, swap(own, "core")], axis=0)
    for step in range(1, far + 1):
        held = lax.ppermute(held if step < far else held[: own.shape[0]], ("z", "core"), routes)
        (near if step <= far // 2 else rest).append(held)
    near = jnp.concatenate(near, axis=0)
    rest = jnp.concatenate(rest, axis=0)
    near_away, token = lax.optimization_barrier((swap(near, "y"), token))
    mine = [near, rest, near_away, swap(rest, "y")]
    return mine + [swap(block, "core") for block in mine], token


def plus(one, two):
    return (one.astype(jnp.float32) + two.astype(jnp.float32)).astype(jnp.bfloat16)


def shards(frames, conv_weight, qkv_weight, out_weight, cotangent):
    rows = frames.shape[0]
    depth = lax.axis_size("z")

    low, high = edges(frames)
    cot_other = swap(cotangent, "core")
    conv_own, conv_panel = conv(frames, low, high, conv_weight)
    conv_other = swap(conv_own, "core")
    queries, grads = project(conv_own, conv_other, cotangent, cot_other, qkv_weight, out_weight)
    panels, queries = gather(conv_panel, depth, queries)
    att, gq, early, late, part = attention(queries, grads, panels, qkv_weight, depth)

    att_other = swap(att, "core")
    gq_other = swap(gq[rows:], "core")

    totals, (sums, (mixed, base)) = ring_sums(
        (early, late),
        depth,
        (
            lambda sent: weights(
                depth, panels, att, att_other, gq, conv_own, conv_other, cotangent, cot_other, part
            ),
            lambda sent: mixing(
                att, att_other, gq, lax.optimization_barrier((gq_other, sent))[0], out_weight, qkv_weight
            ),
        ),
    )
    scattered = lax.psum_scatter(sums, "z", scatter_dimension=0, tiled=True)

    def for_cores(total):
        total = total.astype(jnp.bfloat16).reshape((PLANES, CORES) + total.shape[-2:])
        return total[:, 0], swap(total[:, 1], "core")

    (early_own, early_other), (late_own, late_other) = for_cores(totals[0]), for_cores(totals[1])
    panel_grads = jnp.concatenate([early_own, late_own, early_other, late_other], axis=-1)
    panel_away = swap(panel_grads[1], "y")
    grad_conv, taps = tail(base, panel_grads[0], panel_away, qkv_weight, frames, low, high)
    x_grad = back(grad_conv, *edges(grad_conv), conv_weight)

    taps = taps + swap(taps, "core")
    taps = taps + swap(taps, "y")
    scattered, x_grad, taps = lax.optimization_barrier((scattered, x_grad, taps))
    distance = 1
    while distance < depth:
        taps = taps + lax.ppermute(taps, "z", [(i, i ^ distance) for i in range(depth)])
        distance *= 2
    conv_weight_grad = taps[:TAPS]

    half = scattered.shape[0] // PLANES
    summed = scattered[:half].astype(jnp.float32) + swap(scattered[half:], "y").astype(jnp.float32)
    own, other = summed[: half // CORES], swap(summed[half // CORES :], "core")
    qkv_weight_grad, out_weight_grad = finish(own, other)
    return (mixed, x_grad, qkv_weight_grad, out_weight_grad, conv_weight_grad)


def solution(mesh):
    clips, tall = mesh.devices.shape
    grid = Mesh(
        mesh.devices.reshape(clips, tall // (PLANES * CORES), PLANES, CORES), ("clip", "z", "y", "core")
    )
    rows = P(("clip",) + TALL, None)
    in_specs = (rows, P(), P(), P(), rows)
    out_specs = (rows, rows, rows, rows, P("clip", None))
    return jax.shard_map(shards, mesh=grid, in_specs=in_specs, out_specs=out_specs, check_vma=False)
```

```python
import functools

import jax
import jax.numpy as jnp
from jax import lax
from jax.experimental import pallas as pl
from jax.experimental.pallas import tpu as pltpu
from jax.sharding import Mesh
from jax.sharding import PartitionSpec as P

D = 1024
HEADS = 8
HEAD_DIM = 128
TAPS = 5
GAP = 2
STRIDE = 8
REACH = GAP * (TAPS // 2)
EDGE = 16
CORES = 2
PLANES = 2
OWN = HEADS // CORES
HALF = OWN * HEAD_DIM
SCALE = 1.0 / HEAD_DIM**0.5
LOG2E = 1.4426950408889634
TALL = ("z", "y", "core")
SWAP = [(0, 1), (1, 0)]

NN = (((1,), (0,)), ((), ()))
NT = (((1,), (1,)), ((), ()))
TN = (((0,), (0,)), ((), ()))


def mm(a, b, dims=NN):
    return lax.dot_general(a, b, dims, preferred_element_type=jnp.float32)


def params(mib):
    return pltpu.CompilerParams(vmem_limit_bytes=mib * 1024 * 1024)


HBM = pl.BlockSpec(memory_space=pltpu.HBM)


def fetch(pairs, sems):
    copies = [pltpu.make_async_copy(source, target, sems.at[at]) for at, (source, target) in enumerate(pairs)]
    for copy in copies:
        copy.start()
    return copies


def stacked(blocks, target):
    at, pairs = 0, []
    for block in blocks:
        pairs.append((block, target.at[at : at + block.shape[0]]))
        at += block.shape[0]
    return pairs


def whole(shape):
    return pl.BlockSpec(shape, lambda *_: (0,) * len(shape))


def conv_kernel(frames, low, high, weight, conv_out, conv_panel, framed, total):
    rows = frames.shape[0]
    framed[:EDGE] = low[...].astype(jnp.float32)
    framed[EDGE : EDGE + rows] = frames[...].astype(jnp.float32)
    framed[EDGE + rows :] = high[...].astype(jnp.float32)
    acc = None
    for tap in range(TAPS):
        start = EDGE - REACH + GAP * tap
        term = weight[tap : tap + 1, :] * framed[start : start + rows, :]
        acc = term if acc is None else acc + term
    conv_out[...] = acc.astype(jnp.bfloat16)
    for chunk in range(D // HEAD_DIM):
        cols = slice(chunk * HEAD_DIM, (chunk + 1) * HEAD_DIM)
        total[chunk] = acc[:, cols]
        picked = total[chunk, pl.ds(0, rows // STRIDE, stride=STRIDE), :]
        conv_panel[:, cols] = picked.astype(jnp.bfloat16)


def conv(frames, low, high, weight):
    rows = frames.shape[0]
    return pl.pallas_call(
        conv_kernel,
        out_shape=(
            jax.ShapeDtypeStruct((rows, D), jnp.bfloat16),
            jax.ShapeDtypeStruct((rows // STRIDE, D), jnp.bfloat16),
        ),
        scratch_shapes=[
            pltpu.VMEM((rows + 2 * EDGE, D), jnp.float32),
            pltpu.VMEM((D // HEAD_DIM, rows, HEAD_DIM), jnp.float32),
        ],
        compiler_params=params(16),
        name="conv",
    )(frames, low, high, weight)


def project_kernel(
    conv_own, conv_other, cot_own, cot_other, qkv_weight, out_weight, queries, grads, cot_rows, wide, tall, sems
):
    rows = conv_own.shape[0]
    core = lax.axis_index("core")
    start = pl.multiple_of(core * HALF, HALF)
    copies = fetch(
        (
            (qkv_weight.at[:, pl.ds(start, HALF)], wide),
            (out_weight.at[pl.ds(start, HALF), :], tall),
            (cot_own, cot_rows),
        ),
        sems,
    )
    copies[0].wait()
    queries[:rows, :] = mm(conv_own[...], wide[...]).astype(jnp.bfloat16)
    queries[rows:, :] = mm(conv_other[...], wide[...]).astype(jnp.bfloat16)
    copies[1].wait()
    grads[rows:, :] = mm(cot_other[...], tall[...], NT).astype(jnp.bfloat16)
    copies[2].wait()
    grads[:rows, :] = mm(cot_rows[...], tall[...], NT).astype(jnp.bfloat16)


def project(conv_own, conv_other, cot_own, cot_other, qkv_weight, out_weight):
    rows = conv_own.shape[0]
    vmem = pl.BlockSpec(memory_space=pltpu.VMEM)
    out = jax.ShapeDtypeStruct((2 * rows, HALF), jnp.bfloat16)
    return pl.pallas_call(
        project_kernel,
        in_specs=[vmem, vmem, HBM, vmem, HBM, HBM],
        out_shape=(out, out),
        scratch_shapes=[
            pltpu.VMEM((rows, D), jnp.bfloat16),
            pltpu.VMEM((D, HALF), jnp.bfloat16),
            pltpu.VMEM((HALF, D), jnp.bfloat16),
            pltpu.SemaphoreType.DMA((3,)),
        ],
        compiler_params=params(50),
        cost_estimate=pl.CostEstimate(flops=2_000_000_000, bytes_accessed=6_000_000, transcendentals=0),
        name="project",
    )(conv_own, conv_other, cot_own, cot_other, qkv_weight, out_weight)


def batches(depth):
    far = depth // 2
    near, rest = [(0, 0)], []
    for step in range(1, far):
        (near if step <= far // 2 else rest).extend((step, core) for core in range(CORES))
    rest.append((far, 0))
    return near, rest


def attention_kernel(depth, queries, grads, *refs):
    panels, rest = refs[:8], refs[8:]
    qkv_weight, att, gq, early, late, part, keys, values, panel, weight, sems, weight_sems = rest
    head = pl.program_id(0)
    core = lax.axis_index("core")

    def columns(at, kind):
        start = pl.multiple_of((kind * HEADS + core * OWN + at) * HEAD_DIM, HEAD_DIM)
        return pltpu.make_async_copy(
            qkv_weight.at[:, pl.ds(start, HEAD_DIM)],
            weight.at[at, :, pl.ds((kind - 1) * HEAD_DIM, HEAD_DIM)],
            weight_sems.at[at, kind - 1],
        )

    @pl.when(head == 0)
    def _():
        copies = fetch(stacked(panels, panel), sems)
        for at in range(OWN):
            for kind in (1, 2):
                columns(at, kind).start()
        for copy in copies:
            copy.wait()

    for kind in (1, 2):
        columns(head, kind).wait()
    both = mm(panel[...], weight[head]).astype(jnp.bfloat16)
    keys[...] = both[:, :HEAD_DIM]
    values[...] = both[:, HEAD_DIM:]
    query, grad = queries[...], grads[...]
    scores = mm(keys[...], query, NT)
    highest = jnp.max(scores, axis=0, keepdims=True)
    raised = jnp.exp2((scores - highest) * (SCALE * LOG2E))
    probs = raised * (1.0 / jnp.sum(raised, axis=0, keepdims=True))
    weights = probs.astype(jnp.bfloat16)
    attended = mm(values[...], weights, TN).astype(jnp.bfloat16)
    grad_t = grad.astype(jnp.float32).T
    delta = jnp.sum(grad_t * attended.astype(jnp.float32), axis=0, keepdims=True)
    dprob = mm(values[...], grad, NT)
    grad_scores = (probs * (dprob - delta)).astype(jnp.bfloat16)
    att[...] = attended.astype(jnp.float32).T.astype(jnp.bfloat16)
    gq[...] = (mm(keys[...], grad_scores, TN) * SCALE).T.astype(jnp.bfloat16)
    part[:, :HEAD_DIM] = (mm(grad_scores, query) * SCALE).astype(jnp.bfloat16)
    part[:, HEAD_DIM:] = mm(weights, grad).astype(jnp.bfloat16)

    piece = early.shape[3]
    sign = 2 * core - 1

    def store(out):
        at = 0
        for lane in range(CORES):
            for plane in range(PLANES):
                for batch in batches(depth):
                    for step, sender in batch:
                        steps = step * (1 - 2 * lane)
                        ahead = lax.rem(depth + sign * steps, depth)
                        out[ahead, plane, sender ^ lane] = part[at : at + piece, :]
                        at += piece

    @pl.when(head < OWN // 2)
    def _():
        store(early)

    @pl.when(head >= OWN // 2)
    def _():
        store(late)


def attention(queries, grads, panels, qkv_weight, depth):
    tokens = queries.shape[0]
    total = sum(block.shape[0] for block in panels)
    piece = total // depth // PLANES // CORES
    wide = 2 * HEAD_DIM
    head = pl.BlockSpec((tokens, HEAD_DIM), lambda h: (0, h))
    shape = (depth, PLANES, CORES, piece, wide)
    parts = jax.ShapeDtypeStruct(shape[:-1] + (HALF,), jnp.bfloat16)
    return pl.pallas_call(
        functools.partial(attention_kernel, depth),
        grid=(OWN,),
        in_specs=[head, head] + [HBM] * len(panels) + [HBM],
        out_specs=[
            head,
            head,
            pl.BlockSpec(shape, lambda h: (0, 0, 0, 0, jnp.minimum(h, OWN // 2 - 1))),
            pl.BlockSpec(shape, lambda h: (0, 0, 0, 0, jnp.maximum(h - OWN // 2, 0))),
            pl.BlockSpec((total, wide), lambda h: (0, h)),
        ],
        scratch_shapes=[
            pltpu.VMEM((total, HEAD_DIM), jnp.bfloat16),
            pltpu.VMEM((total, HEAD_DIM), jnp.bfloat16),
            pltpu.VMEM((total, D), jnp.bfloat16),
            pltpu.VMEM((OWN, D, wide), jnp.bfloat16),
            pltpu.SemaphoreType.DMA((len(panels),)),
            pltpu.SemaphoreType.DMA((OWN, 2)),
        ],
        out_shape=(
            jax.ShapeDtypeStruct((tokens, HALF), jnp.bfloat16),
            jax.ShapeDtypeStruct((tokens, HALF), jnp.bfloat16),
            parts,
            parts,
            jax.ShapeDtypeStruct((total, 2 * HALF), jnp.bfloat16),
        ),
        compiler_params=params(44),
        cost_estimate=pl.CostEstimate(flops=8_000_000_000, bytes_accessed=16_000_000, transcendentals=2_000_000),
        name="attention",
    )(queries, grads, *panels, qkv_weight)


def weights_kernel(depth, att, att_other, gq, conv_own, conv_other, cot_own, cot_other, part, *refs):
    panels, (sums, panel, sems) = refs[:8], refs[8:]
    core, plane = lax.axis_index("core"), lax.axis_index("y")
    rows = conv_own.shape[0]
    own, away = halves()
    size = D // depth // PLANES // CORES

    def store(value, first, cols):
        for at in range(0, value.shape[0], size):
            block = first + at // size
            other_core, other_plane = lax.rem(block + core, CORES), lax.rem(block // CORES + plane, PLANES)
            to = (block // (PLANES * CORES) * PLANES + other_plane) * CORES + other_core
            sums[pl.ds(pl.multiple_of(to * size, size), size), cols] = value[at : at + size].astype(jnp.bfloat16)

    step = pl.program_id(0)

    @pl.when(step == 0)
    def _():
        fetch(stacked(panels, panel), sems)
        queries = mm(conv_own[...], gq[:rows, :], TN) + mm(conv_other[...], gq[rows:, :], TN)
        store(queries, 0, slice(0, HALF))
        mine = mm(att[:rows, :], cot_own[:, own], TN) + mm(att[rows:, :], cot_other[:, own], TN)
        store(mine, core * (HALF // size), slice(HALF, D))
        other = mm(att_other[rows:, :], cot_own[:, own], TN) + mm(att_other[:rows, :], cot_other[:, own], TN)
        store(other, (1 - core) * (HALF // size), slice(HALF, D))

    @pl.when(step == 1)
    def _():
        for at, (source, target) in enumerate(stacked(panels, panel)):
            pltpu.make_async_copy(source, target, sems.at[at]).wait()
        store(mm(panel[...], part[...], TN), 0, slice(None))


def weights(depth, panels, *ins):
    total = sum(block.shape[0] for block in panels)
    return pl.pallas_call(
        functools.partial(weights_kernel, depth),
        grid=(2,),
        in_specs=[whole(item.shape) for item in ins] + [HBM] * len(panels),
        out_specs=pl.BlockSpec((D, D), lambda i: (0, 1 - i)),
        scratch_shapes=[pltpu.VMEM((total, D), jnp.bfloat16), pltpu.SemaphoreType.DMA((len(panels),))],
        out_shape=jax.ShapeDtypeStruct((D, 2 * D), jnp.bfloat16),
        compiler_params=params(45),
        cost_estimate=pl.CostEstimate(flops=4_000_000_000, bytes_accessed=12_000_000, transcendentals=0),
        name="weights",
    )(*ins, *panels)


def mixing_kernel(att, att_other, gq, gq_other, out_weight, qkv_weight, mixed, base, first, second, sems):
    core = lax.axis_index("core")
    rows = mixed.shape[0]
    own = pl.ds(pl.multiple_of(core * HALF, HALF), HALF)
    away = pl.ds(pl.multiple_of((1 - core) * HALF, HALF), HALF)
    copies = fetch(((out_weight, first), (qkv_weight.at[:, pl.ds(0, D)], second)), sems)
    copies[0].wait()
    blend = mm(att[:rows, :], first[own, :]) + mm(att_other[rows:, :], first[away, :])
    mixed[...] = blend.astype(jnp.bfloat16)
    copies[1].wait()
    base[...] = mm(gq[:rows, :], second[:, own], NT) + mm(gq_other[...], second[:, away], NT)


def mixing(att, att_other, gq, gq_other, out_weight, qkv_weight):
    rows = gq_other.shape[0]
    vmem = pl.BlockSpec(memory_space=pltpu.VMEM)
    return pl.pallas_call(
        mixing_kernel,
        in_specs=[vmem] * 4 + [HBM] * 2,
        out_shape=(
            jax.ShapeDtypeStruct((rows, D), jnp.bfloat16),
            jax.ShapeDtypeStruct((rows, D), jnp.float32),
        ),
        scratch_shapes=[
            pltpu.VMEM((D, D), jnp.bfloat16),
            pltpu.VMEM((D, D), jnp.bfloat16),
            pltpu.SemaphoreType.DMA((2,)),
        ],
        compiler_params=params(50),
        cost_estimate=pl.CostEstimate(flops=1_000_000_000, bytes_accessed=8_000_000, transcendentals=0),
        name="mixing",
    )(att, att_other, gq, gq_other, out_weight, qkv_weight)


def by_kind(block):
    pieces = [block[:, at : at + HEAD_DIM] for at in range(0, block.shape[1], HEAD_DIM)]
    return jnp.concatenate(pieces[0::2], axis=1), jnp.concatenate(pieces[1::2], axis=1)


def halves():
    core = lax.axis_index("core")
    return [pl.ds(pl.multiple_of(at * HALF, HALF), HALF) for at in (core, 1 - core)]


def tail_kernel(
    base, own, other, own_away, other_away, qkv_weight, frames, low, high, grad_out, taps, framed, total, weight, sems
):
    rows = frames.shape[0]
    copies = fetch([(qkv_weight.at[:, pl.ds(D * at, D)], weight.at[at - 1]) for at in (1, 2)], sems)
    framed[:EDGE] = low[...].astype(jnp.float32)
    framed[EDGE : EDGE + rows] = frames[...].astype(jnp.float32)
    framed[EDGE + rows :] = high[...].astype(jnp.float32)
    kinds = [by_kind(plus(own[...], own_away[...])), by_kind(plus(other[...], other_away[...]))]
    extra = None
    for kind in range(2):
        copies[kind].wait()
        for block, cols in zip(kinds, halves()):
            term = mm(block[kind], weight[kind, :, cols], NT)
            extra = term if extra is None else extra + term
    for chunk in range(D // HEAD_DIM):
        cols = slice(chunk * HEAD_DIM, (chunk + 1) * HEAD_DIM)
        total[chunk] = base[:, cols]
        at = (chunk, pl.ds(0, rows // STRIDE, stride=STRIDE), slice(None))
        total[at] = total[at] + extra[:, cols]
        grad = total[chunk].astype(jnp.bfloat16)
        grad_out[:, cols] = grad
        grad = grad.astype(jnp.float32)
        for tap in range(TAPS):
            start = EDGE - REACH + GAP * tap
            term = grad * framed[start : start + rows, cols]
            taps[tap : tap + 1, cols] = jnp.sum(term, axis=0, keepdims=True)
    taps[TAPS:, :] = jnp.zeros((taps.shape[0] - TAPS, D), jnp.float32)


def tail(base, panel_parts, qkv_weight, frames, low, high):
    rows = frames.shape[0]
    vmem = pl.BlockSpec(memory_space=pltpu.VMEM)
    return pl.pallas_call(
        tail_kernel,
        in_specs=[vmem] * 5 + [HBM] + [vmem] * 3,
        out_shape=(
            jax.ShapeDtypeStruct((rows, D), jnp.bfloat16),
            jax.ShapeDtypeStruct((8, D), jnp.float32),
        ),
        scratch_shapes=[
            pltpu.VMEM((rows + 2 * EDGE, D), jnp.float32),
            pltpu.VMEM((D // HEAD_DIM, rows, HEAD_DIM), jnp.float32),
            pltpu.VMEM((2, D, D), jnp.bfloat16),
            pltpu.SemaphoreType.DMA((2,)),
        ],
        compiler_params=params(50),
        cost_estimate=pl.CostEstimate(flops=20_000_000_000, bytes_accessed=8_000_000, transcendentals=0),
        name="tail",
    )(base, *panel_parts, qkv_weight, frames, low, high)


def finish_kernel(own, other, own_away, other_away, qkv_grad, out_grad):
    for here, away, cols in zip((own, other), (own_away, other_away), halves()):
        block = here[...].astype(jnp.float32) + away[...].astype(jnp.float32)
        keys, values = by_kind(block[:, :D])
        qkv_grad[:, cols] = block[:, D : D + HALF]
        qkv_grad[:, pl.ds(cols.start + D, HALF)] = keys
        qkv_grad[:, pl.ds(cols.start + 2 * D, HALF)] = values
        out_grad[:, cols] = block[:, D + HALF :]


def finish(parts):
    rows = parts[0].shape[0]
    return pl.pallas_call(
        finish_kernel,
        out_shape=(
            jax.ShapeDtypeStruct((rows, 3 * D), jnp.float32),
            jax.ShapeDtypeStruct((rows, D), jnp.float32),
        ),
        compiler_params=params(16),
        cost_estimate=pl.CostEstimate(flops=3_000_000_000, bytes_accessed=1_000_000, transcendentals=0),
        name="finish",
    )(*parts)


def back_kernel(grad, low, high, weight, out, framed):
    rows = grad.shape[0]
    framed[:EDGE] = low[...].astype(jnp.float32)
    framed[EDGE : EDGE + rows] = grad[...].astype(jnp.float32)
    framed[EDGE + rows :] = high[...].astype(jnp.float32)
    acc = None
    for tap in range(TAPS):
        start = EDGE + REACH - GAP * tap
        term = weight[tap : tap + 1, :] * framed[start : start + rows, :]
        acc = term if acc is None else acc + term
    out[...] = acc.astype(jnp.bfloat16)


def back(grad, low, high, weight):
    rows = grad.shape[0]
    return pl.pallas_call(
        back_kernel,
        out_shape=jax.ShapeDtypeStruct((rows, D), jnp.bfloat16),
        scratch_shapes=[pltpu.VMEM((rows + 2 * EDGE, D), jnp.float32)],
        compiler_params=params(16),
        name="back",
    )(grad, low, high, weight)


def swap(block, axis):
    return lax.ppermute(block, axis, SWAP)


def partners(own_plane, other_plane):
    count = own_plane.shape[0] // CORES
    both = [(PLANES * CORES - 1 - at, at) for at in range(PLANES * CORES)]
    return (
        swap(own_plane[count:], "core"),
        swap(other_plane[:count], "y"),
        lax.ppermute(other_plane[count:], ("y", "core"), both),
    )


def edges(block):
    count = lax.axis_size(TALL)
    up = [(i, i + 1) for i in range(count - 1)]
    down = [(i + 1, i) for i in range(count - 1)]
    return lax.ppermute(block[-EDGE:], TALL, up), lax.ppermute(block[:EDGE], TALL, down)


def ring_sums(parts, depth, beside):
    ahead = [(i, (i + 1) % depth) for i in range(depth)]
    behind = [(i, (i - 1) % depth) for i in range(depth)]
    far = depth // 2
    ups, downs = [part[far] for part in parts], [part[far + 1] for part in parts]
    done = []
    for step in range(1, far + 1):
        sent = ups[0]
        ups = [lax.ppermute(up, "z", ahead) for up in ups]
        if step < far:
            downs = [lax.ppermute(down, "z", behind) for down in downs]
        if step <= len(beside):
            result = beside[step - 1](sent)
            parts, result = lax.optimization_barrier((parts, result))
            done.append(result)
        if step < far:
            ups = [plus(up, part[far - step]) for up, part in zip(ups, parts)]
        if step < far - 1:
            downs = [plus(down, part[far + 1 + step]) for down, part in zip(downs, parts)]
    totals = [
        part[0].astype(jnp.float32) + up.astype(jnp.float32) + down.astype(jnp.float32)
        for part, up, down in zip(parts, ups, downs)
    ]
    return totals, done


def gather(own, depth, token):
    far = depth // 2
    routes = [(CORES * z, CORES * ((z + 1) % depth)) for z in range(depth)]
    routes += [(CORES * z + 1, CORES * ((z - 1) % depth) + 1) for z in range(depth)]
    near, rest = [own], []
    held = jnp.concatenate([own, swap(own, "core")], axis=0)
    for step in range(1, far + 1):
        held = lax.ppermute(held if step < far else held[: own.shape[0]], ("z", "core"), routes)
        (near if step <= far // 2 else rest).append(held)
    near = jnp.concatenate(near, axis=0)
    rest = jnp.concatenate(rest, axis=0)
    near_away, token = lax.optimization_barrier((swap(near, "y"), token))
    mine = [near, rest, near_away, swap(rest, "y")]
    return mine + [swap(block, "core") for block in mine], token


def plus(one, two):
    return (one.astype(jnp.float32) + two.astype(jnp.float32)).astype(jnp.bfloat16)


def shards(frames, conv_weight, qkv_weight, out_weight, cotangent):
    rows = frames.shape[0]
    depth = lax.axis_size("z")

    low, high = edges(frames)
    cot_other = swap(cotangent, "core")
    conv_own, conv_panel = conv(frames, low, high, conv_weight)
    conv_other = swap(conv_own, "core")
    queries, grads = project(conv_own, conv_other, cotangent, cot_other, qkv_weight, out_weight)
    panels, queries = gather(conv_panel, depth, queries)
    att, gq, early, late, part = attention(queries, grads, panels, qkv_weight, depth)

    att_other = swap(att, "core")
    gq_other = swap(gq[rows:], "core")

    totals, (sums, (mixed, base)) = ring_sums(
        (early, late),
        depth,
        (
            lambda sent: weights(
                depth, panels, att, att_other, gq, conv_own, conv_other, cotangent, cot_other, part
            ),
            lambda sent: mixing(
                att, att_other, gq, lax.optimization_barrier((gq_other, sent))[0], out_weight, qkv_weight
            ),
        ),
    )
    scattered = lax.psum_scatter(sums, "z", scatter_dimension=0, tiled=True)

    panel_sums = jnp.concatenate([total.astype(jnp.bfloat16) for total in totals], axis=-1)
    panel_sums = panel_sums.reshape(PLANES, -1, 2 * HALF)
    share = panel_sums.shape[1] // CORES
    panel_parts = (panel_sums[0, :share],) + partners(panel_sums[0], panel_sums[1])
    grad_conv, taps = tail(base, panel_parts, qkv_weight, frames, low, high)
    x_grad = back(grad_conv, *edges(grad_conv), conv_weight)

    spread = jnp.concatenate([taps, taps], axis=0)
    taps = taps + sum(partners(spread, spread))
    distance = 1
    while distance < depth:
        taps = taps + lax.ppermute(taps, "z", [(i, i ^ distance) for i in range(depth)])
        if distance == 1:
            scattered, x_grad, taps = lax.optimization_barrier((scattered, x_grad, taps))
        distance *= 2
    conv_weight_grad = taps[:TAPS]

    half = scattered.shape[0] // PLANES
    parts = (scattered[: half // CORES],) + partners(scattered[:half], scattered[half:])
    qkv_weight_grad, out_weight_grad = finish(parts)
    return (mixed, x_grad, qkv_weight_grad, out_weight_grad, conv_weight_grad)


def solution(mesh):
    clips, tall = mesh.devices.shape
    grid = Mesh(
        mesh.devices.reshape(clips, tall // (PLANES * CORES), PLANES, CORES), ("clip", "z", "y", "core")
    )
    rows = P(("clip",) + TALL, None)
    in_specs = (rows, P(), P(), P(), rows)
    out_specs = (rows, rows, rows, rows, P("clip", None))
    return jax.shard_map(shards, mesh=grid, in_specs=in_specs, out_specs=out_specs, check_vma=False)
```

```python
import functools

import jax
import jax.numpy as jnp
from jax import lax
from jax.experimental import pallas as pl
from jax.experimental.pallas import tpu as pltpu
from jax.sharding import Mesh
from jax.sharding import PartitionSpec as P

D = 1024
HEADS = 8
HEAD_DIM = 128
TAPS = 5
GAP = 2
STRIDE = 8
REACH = GAP * (TAPS // 2)
EDGE = 16
CORES = 2
PLANES = 2
OWN = HEADS // CORES
HALF = OWN * HEAD_DIM
SCALE = 1.0 / HEAD_DIM**0.5
LOG2E = 1.4426950408889634
TALL = ("z", "y", "core")
SWAP = [(0, 1), (1, 0)]

NN = (((1,), (0,)), ((), ()))
NT = (((1,), (1,)), ((), ()))
TN = (((0,), (0,)), ((), ()))


def mm(a, b, dims=NN):
    return lax.dot_general(a, b, dims, preferred_element_type=jnp.float32)


def params(mib):
    return pltpu.CompilerParams(vmem_limit_bytes=mib * 1024 * 1024)


HBM = pl.BlockSpec(memory_space=pltpu.HBM)


def fetch(pairs, sems):
    copies = [pltpu.make_async_copy(source, target, sems.at[at]) for at, (source, target) in enumerate(pairs)]
    for copy in copies:
        copy.start()
    return copies


def stacked(blocks, target):
    at, pairs = 0, []
    for block in blocks:
        pairs.append((block, target.at[at : at + block.shape[0]]))
        at += block.shape[0]
    return pairs


def whole(shape):
    return pl.BlockSpec(shape, lambda *_: (0,) * len(shape))


def conv_kernel(frames, low, high, weight, conv_out, conv_panel, framed, total):
    rows = frames.shape[0]
    framed[:EDGE] = low[...].astype(jnp.float32)
    framed[EDGE : EDGE + rows] = frames[...].astype(jnp.float32)
    framed[EDGE + rows :] = high[...].astype(jnp.float32)
    acc = None
    for tap in range(TAPS):
        start = EDGE - REACH + GAP * tap
        term = weight[tap : tap + 1, :] * framed[start : start + rows, :]
        acc = term if acc is None else acc + term
    conv_out[...] = acc.astype(jnp.bfloat16)
    for chunk in range(D // HEAD_DIM):
        cols = slice(chunk * HEAD_DIM, (chunk + 1) * HEAD_DIM)
        total[chunk] = acc[:, cols]
        picked = total[chunk, pl.ds(0, rows // STRIDE, stride=STRIDE), :]
        conv_panel[:, cols] = picked.astype(jnp.bfloat16)


def conv(frames, low, high, weight):
    rows = frames.shape[0]
    return pl.pallas_call(
        conv_kernel,
        out_shape=(
            jax.ShapeDtypeStruct((rows, D), jnp.bfloat16),
            jax.ShapeDtypeStruct((rows // STRIDE, D), jnp.bfloat16),
        ),
        scratch_shapes=[
            pltpu.VMEM((rows + 2 * EDGE, D), jnp.float32),
            pltpu.VMEM((D // HEAD_DIM, rows, HEAD_DIM), jnp.float32),
        ],
        compiler_params=params(16),
        name="conv",
    )(frames, low, high, weight)


def project_kernel(
    conv_own, conv_other, cot_own, cot_other, qkv_weight, out_weight, queries, grads, cot_rows, wide, tall, sems
):
    rows = conv_own.shape[0]
    core = lax.axis_index("core")
    start = pl.multiple_of(core * HALF, HALF)
    copies = fetch(
        (
            (qkv_weight.at[:, pl.ds(start, HALF)], wide),
            (out_weight.at[pl.ds(start, HALF), :], tall),
            (cot_own, cot_rows),
        ),
        sems,
    )
    copies[0].wait()
    queries[:rows, :] = mm(conv_own[...], wide[...]).astype(jnp.bfloat16)
    queries[rows:, :] = mm(conv_other[...], wide[...]).astype(jnp.bfloat16)
    copies[1].wait()
    grads[rows:, :] = mm(cot_other[...], tall[...], NT).astype(jnp.bfloat16)
    copies[2].wait()
    grads[:rows, :] = mm(cot_rows[...], tall[...], NT).astype(jnp.bfloat16)


def project(conv_own, conv_other, cot_own, cot_other, qkv_weight, out_weight):
    rows = conv_own.shape[0]
    vmem = pl.BlockSpec(memory_space=pltpu.VMEM)
    out = jax.ShapeDtypeStruct((2 * rows, HALF), jnp.bfloat16)
    return pl.pallas_call(
        project_kernel,
        in_specs=[vmem, vmem, HBM, vmem, HBM, HBM],
        out_shape=(out, out),
        scratch_shapes=[
            pltpu.VMEM((rows, D), jnp.bfloat16),
            pltpu.VMEM((D, HALF), jnp.bfloat16),
            pltpu.VMEM((HALF, D), jnp.bfloat16),
            pltpu.SemaphoreType.DMA((3,)),
        ],
        compiler_params=params(50),
        cost_estimate=pl.CostEstimate(flops=2_000_000_000, bytes_accessed=6_000_000, transcendentals=0),
        name="project",
    )(conv_own, conv_other, cot_own, cot_other, qkv_weight, out_weight)


def batches(depth):
    far = depth // 2
    near, rest = [(0, 0)], []
    for step in range(1, far):
        (near if step <= far // 2 else rest).extend((step, core) for core in range(CORES))
    rest.append((far, 0))
    return near, rest


def attention_kernel(depth, queries, grads, *refs):
    panels, rest = refs[:8], refs[8:]
    qkv_weight, att, gq, early, late, part, keys, values, panel, weight, sems, weight_sems = rest
    head = pl.program_id(0)
    core = lax.axis_index("core")

    def columns(at, kind):
        start = pl.multiple_of((kind * HEADS + core * OWN + at) * HEAD_DIM, HEAD_DIM)
        return pltpu.make_async_copy(
            qkv_weight.at[:, pl.ds(start, HEAD_DIM)],
            weight.at[at, :, pl.ds((kind - 1) * HEAD_DIM, HEAD_DIM)],
            weight_sems.at[at, kind - 1],
        )

    @pl.when(head == 0)
    def _():
        copies = fetch(stacked(panels, panel), sems)
        for at in range(OWN):
            for kind in (1, 2):
                columns(at, kind).start()
        for copy in copies:
            copy.wait()

    for kind in (1, 2):
        columns(head, kind).wait()
    both = mm(panel[...], weight[head]).astype(jnp.bfloat16)
    keys[...] = both[:, :HEAD_DIM]
    values[...] = both[:, HEAD_DIM:]
    query, grad = queries[...], grads[...]
    scores = mm(keys[...], query, NT)
    highest = jnp.max(scores, axis=0, keepdims=True)
    raised = jnp.exp2((scores - highest) * (SCALE * LOG2E))
    probs = raised * (1.0 / jnp.sum(raised, axis=0, keepdims=True))
    weights = probs.astype(jnp.bfloat16)
    attended = mm(values[...], weights, TN).astype(jnp.bfloat16)
    grad_t = grad.astype(jnp.float32).T
    delta = jnp.sum(grad_t * attended.astype(jnp.float32), axis=0, keepdims=True)
    dprob = mm(values[...], grad, NT)
    grad_scores = (probs * (dprob - delta)).astype(jnp.bfloat16)
    att[...] = attended.astype(jnp.float32).T.astype(jnp.bfloat16)
    gq[...] = (mm(keys[...], grad_scores, TN) * SCALE).T.astype(jnp.bfloat16)
    part[:, :HEAD_DIM] = (mm(grad_scores, query) * SCALE).astype(jnp.bfloat16)
    part[:, HEAD_DIM:] = mm(weights, grad).astype(jnp.bfloat16)

    piece = early.shape[3]
    sign = 2 * core - 1

    def store(out):
        at = 0
        for lane in range(CORES):
            for plane in range(PLANES):
                for batch in batches(depth):
                    for step, sender in batch:
                        steps = step * (1 - 2 * lane)
                        ahead = lax.rem(depth + sign * steps, depth)
                        out[ahead, plane, sender ^ lane] = part[at : at + piece, :]
                        at += piece

    @pl.when(head < OWN // 2)
    def _():
        store(early)

    @pl.when(head >= OWN // 2)
    def _():
        store(late)


def attention(queries, grads, panels, qkv_weight, depth):
    tokens = queries.shape[0]
    total = sum(block.shape[0] for block in panels)
    piece = total // depth // PLANES // CORES
    wide = 2 * HEAD_DIM
    head = pl.BlockSpec((tokens, HEAD_DIM), lambda h: (0, h))
    shape = (depth, PLANES, CORES, piece, wide)
    parts = jax.ShapeDtypeStruct(shape[:-1] + (HALF,), jnp.bfloat16)
    return pl.pallas_call(
        functools.partial(attention_kernel, depth),
        grid=(OWN,),
        in_specs=[head, head] + [HBM] * len(panels) + [HBM],
        out_specs=[
            head,
            head,
            pl.BlockSpec(shape, lambda h: (0, 0, 0, 0, jnp.minimum(h, OWN // 2 - 1))),
            pl.BlockSpec(shape, lambda h: (0, 0, 0, 0, jnp.maximum(h - OWN // 2, 0))),
            pl.BlockSpec((total, wide), lambda h: (0, h)),
        ],
        scratch_shapes=[
            pltpu.VMEM((total, HEAD_DIM), jnp.bfloat16),
            pltpu.VMEM((total, HEAD_DIM), jnp.bfloat16),
            pltpu.VMEM((total, D), jnp.bfloat16),
            pltpu.VMEM((OWN, D, wide), jnp.bfloat16),
            pltpu.SemaphoreType.DMA((len(panels),)),
            pltpu.SemaphoreType.DMA((OWN, 2)),
        ],
        out_shape=(
            jax.ShapeDtypeStruct((tokens, HALF), jnp.bfloat16),
            jax.ShapeDtypeStruct((tokens, HALF), jnp.bfloat16),
            parts,
            parts,
            jax.ShapeDtypeStruct((total, 2 * HALF), jnp.bfloat16),
        ),
        compiler_params=params(44),
        cost_estimate=pl.CostEstimate(flops=8_000_000_000, bytes_accessed=16_000_000, transcendentals=2_000_000),
        name="attention",
    )(queries, grads, *panels, qkv_weight)


def weights_kernel(att, att_other, gq, conv_own, conv_other, cot_own, cot_other, part, *refs):
    panels, (sums, panel, sems) = refs[:8], refs[8:]
    rows = conv_own.shape[0]
    own, away = halves()
    step = pl.program_id(0)

    @pl.when(step == 0)
    def _():
        fetch(stacked(panels, panel), sems)
        queries = mm(conv_own[...], gq[:rows, :], TN) + mm(conv_other[...], gq[rows:, :], TN)
        sums[:, :HALF] = queries.astype(jnp.bfloat16)
        mine = mm(att[:rows, :], cot_own[:, own], TN) + mm(att[rows:, :], cot_other[:, own], TN)
        sums[own, HALF:] = mine.astype(jnp.bfloat16)
        other = mm(att_other[rows:, :], cot_own[:, own], TN) + mm(att_other[:rows, :], cot_other[:, own], TN)
        sums[away, HALF:] = other.astype(jnp.bfloat16)

    @pl.when(step == 1)
    def _():
        for at, (source, target) in enumerate(stacked(panels, panel)):
            pltpu.make_async_copy(source, target, sems.at[at]).wait()
        sums[...] = mm(panel[...], part[...], TN).astype(jnp.bfloat16)


def weights(panels, *ins):
    total = sum(block.shape[0] for block in panels)
    return pl.pallas_call(
        weights_kernel,
        grid=(2,),
        in_specs=[whole(item.shape) for item in ins] + [HBM] * len(panels),
        out_specs=pl.BlockSpec((D, D), lambda i: (0, 1 - i)),
        scratch_shapes=[pltpu.VMEM((total, D), jnp.bfloat16), pltpu.SemaphoreType.DMA((len(panels),))],
        out_shape=jax.ShapeDtypeStruct((D, 2 * D), jnp.bfloat16),
        compiler_params=params(45),
        cost_estimate=pl.CostEstimate(flops=4_000_000_000, bytes_accessed=12_000_000, transcendentals=0),
        name="weights",
    )(*ins, *panels)


def mixing_kernel(att, att_other, gq, gq_other, out_weight, qkv_weight, mixed, base, first, second, sems):
    core = lax.axis_index("core")
    rows = mixed.shape[0]
    own = pl.ds(pl.multiple_of(core * HALF, HALF), HALF)
    away = pl.ds(pl.multiple_of((1 - core) * HALF, HALF), HALF)
    copies = fetch(((out_weight, first), (qkv_weight.at[:, pl.ds(0, D)], second)), sems)
    copies[0].wait()
    blend = mm(att[:rows, :], first[own, :]) + mm(att_other[rows:, :], first[away, :])
    mixed[...] = blend.astype(jnp.bfloat16)
    copies[1].wait()
    base[...] = mm(gq[:rows, :], second[:, own], NT) + mm(gq_other[...], second[:, away], NT)


def mixing(att, att_other, gq, gq_other, out_weight, qkv_weight):
    rows = gq_other.shape[0]
    vmem = pl.BlockSpec(memory_space=pltpu.VMEM)
    return pl.pallas_call(
        mixing_kernel,
        in_specs=[vmem] * 4 + [HBM] * 2,
        out_shape=(
            jax.ShapeDtypeStruct((rows, D), jnp.bfloat16),
            jax.ShapeDtypeStruct((rows, D), jnp.float32),
        ),
        scratch_shapes=[
            pltpu.VMEM((D, D), jnp.bfloat16),
            pltpu.VMEM((D, D), jnp.bfloat16),
            pltpu.SemaphoreType.DMA((2,)),
        ],
        compiler_params=params(50),
        cost_estimate=pl.CostEstimate(flops=1_000_000_000, bytes_accessed=8_000_000, transcendentals=0),
        name="mixing",
    )(att, att_other, gq, gq_other, out_weight, qkv_weight)


def by_kind(block):
    pieces = [block[:, at : at + HEAD_DIM] for at in range(0, block.shape[1], HEAD_DIM)]
    return jnp.concatenate(pieces[0::2], axis=1), jnp.concatenate(pieces[1::2], axis=1)


def halves():
    core = lax.axis_index("core")
    return [pl.ds(pl.multiple_of(at * HALF, HALF), HALF) for at in (core, 1 - core)]


def tail_kernel(
    base, own, other, own_away, other_away, qkv_weight, frames, low, high, grad_out, taps, framed, total, weight, sems
):
    rows = frames.shape[0]
    copies = fetch([(qkv_weight.at[:, pl.ds(D * at, D)], weight.at[at - 1]) for at in (1, 2)], sems)
    framed[:EDGE] = low[...].astype(jnp.float32)
    framed[EDGE : EDGE + rows] = frames[...].astype(jnp.float32)
    framed[EDGE + rows :] = high[...].astype(jnp.float32)
    kinds = [by_kind(plus(own[...], own_away[...])), by_kind(plus(other[...], other_away[...]))]
    extra = None
    for kind in range(2):
        copies[kind].wait()
        for block, cols in zip(kinds, halves()):
            term = mm(block[kind], weight[kind, :, cols], NT)
            extra = term if extra is None else extra + term
    for chunk in range(D // HEAD_DIM):
        cols = slice(chunk * HEAD_DIM, (chunk + 1) * HEAD_DIM)
        total[chunk] = base[:, cols]
        at = (chunk, pl.ds(0, rows // STRIDE, stride=STRIDE), slice(None))
        total[at] = total[at] + extra[:, cols]
        grad = total[chunk].astype(jnp.bfloat16)
        grad_out[:, cols] = grad
        grad = grad.astype(jnp.float32)
        for tap in range(TAPS):
            start = EDGE - REACH + GAP * tap
            term = grad * framed[start : start + rows, cols]
            taps[tap : tap + 1, cols] = jnp.sum(term, axis=0, keepdims=True)
    taps[TAPS:, :] = jnp.zeros((taps.shape[0] - TAPS, D), jnp.float32)


def tail(base, panel_parts, qkv_weight, frames, low, high):
    rows = frames.shape[0]
    vmem = pl.BlockSpec(memory_space=pltpu.VMEM)
    return pl.pallas_call(
        tail_kernel,
        in_specs=[vmem] * 5 + [HBM] + [vmem] * 3,
        out_shape=(
            jax.ShapeDtypeStruct((rows, D), jnp.bfloat16),
            jax.ShapeDtypeStruct((8, D), jnp.float32),
        ),
        scratch_shapes=[
            pltpu.VMEM((rows + 2 * EDGE, D), jnp.float32),
            pltpu.VMEM((D // HEAD_DIM, rows, HEAD_DIM), jnp.float32),
            pltpu.VMEM((2, D, D), jnp.bfloat16),
            pltpu.SemaphoreType.DMA((2,)),
        ],
        compiler_params=params(50),
        cost_estimate=pl.CostEstimate(flops=20_000_000_000, bytes_accessed=8_000_000, transcendentals=0),
        name="tail",
    )(base, *panel_parts, qkv_weight, frames, low, high)


def pick_kernel(block, own, core_block, plane_block, both_block):
    core, plane = lax.axis_index("core"), lax.axis_index("y")
    rows = own.shape[0]
    for out, at, there in (
        (own, plane, core),
        (core_block, plane, 1 - core),
        (plane_block, 1 - plane, core),
        (both_block, 1 - plane, 1 - core),
    ):
        out[...] = block[pl.ds(pl.multiple_of((at * CORES + there) * rows, rows), rows), :]


def pick(block):
    rows, columns = block.shape
    part = jax.ShapeDtypeStruct((rows // PLANES // CORES, columns), block.dtype)
    return pl.pallas_call(
        pick_kernel,
        out_shape=(part,) * (PLANES * CORES),
        compiler_params=params(16),
        cost_estimate=pl.CostEstimate(flops=0, bytes_accessed=1_000_000, transcendentals=0),
        name="pick",
    )(block)


def finish_kernel(own, other, own_away, other_away, qkv_grad, out_grad):
    for here, away, cols in zip((own, other), (own_away, other_away), halves()):
        block = here[...].astype(jnp.float32) + away[...].astype(jnp.float32)
        keys, values = by_kind(block[:, :D])
        qkv_grad[:, cols] = block[:, D : D + HALF]
        qkv_grad[:, pl.ds(cols.start + D, HALF)] = keys
        qkv_grad[:, pl.ds(cols.start + 2 * D, HALF)] = values
        out_grad[:, cols] = block[:, D + HALF :]


def finish(parts):
    rows = parts[0].shape[0]
    return pl.pallas_call(
        finish_kernel,
        out_shape=(
            jax.ShapeDtypeStruct((rows, 3 * D), jnp.float32),
            jax.ShapeDtypeStruct((rows, D), jnp.float32),
        ),
        compiler_params=params(16),
        cost_estimate=pl.CostEstimate(flops=3_000_000_000, bytes_accessed=1_000_000, transcendentals=0),
        name="finish",
    )(*parts)


def back_kernel(grad, low, high, weight, out, framed):
    rows = grad.shape[0]
    framed[:EDGE] = low[...].astype(jnp.float32)
    framed[EDGE : EDGE + rows] = grad[...].astype(jnp.float32)
    framed[EDGE + rows :] = high[...].astype(jnp.float32)
    acc = None
    for tap in range(TAPS):
        start = EDGE + REACH - GAP * tap
        term = weight[tap : tap + 1, :] * framed[start : start + rows, :]
        acc = term if acc is None else acc + term
    out[...] = acc.astype(jnp.bfloat16)


def back(grad, low, high, weight):
    rows = grad.shape[0]
    return pl.pallas_call(
        back_kernel,
        out_shape=jax.ShapeDtypeStruct((rows, D), jnp.bfloat16),
        scratch_shapes=[pltpu.VMEM((rows + 2 * EDGE, D), jnp.float32)],
        compiler_params=params(16),
        name="back",
    )(grad, low, high, weight)


def swap(block, axis):
    return lax.ppermute(block, axis, SWAP)


def partners(core_block, plane_block, both_block):
    both = [(PLANES * CORES - 1 - at, at) for at in range(PLANES * CORES)]
    return (
        swap(core_block, "core"),
        swap(plane_block, "y"),
        lax.ppermute(both_block, ("y", "core"), both),
    )


def doubling(depth):
    pairs = [(z, z ^ 1) for z in range(depth)]
    across = [(z, (z + 1) % depth if z % 2 else (z - 1) % depth) for z in range(depth)]
    far = [(z, (7 - z) % depth if z in (1, 2, 5, 6) else (3 - z) % depth) for z in range(depth)]
    return (pairs, across, far) if depth == 8 else (pairs, across)


def edges(block):
    count = lax.axis_size(TALL)
    up = [(i, i + 1) for i in range(count - 1)]
    down = [(i + 1, i) for i in range(count - 1)]
    return lax.ppermute(block[-EDGE:], TALL, up), lax.ppermute(block[:EDGE], TALL, down)


def ring_sums(parts, depth, beside):
    ahead = [(i, (i + 1) % depth) for i in range(depth)]
    behind = [(i, (i - 1) % depth) for i in range(depth)]
    far = depth // 2
    ups, downs = [part[far] for part in parts], [part[far + 1] for part in parts]
    done = []
    for step in range(1, far + 1):
        sent = ups[0]
        ups = [lax.ppermute(up, "z", ahead) for up in ups]
        if step < far:
            downs = [lax.ppermute(down, "z", behind) for down in downs]
        if step <= len(beside):
            result = beside[step - 1](sent)
            parts, result = lax.optimization_barrier((parts, result))
            done.append(result)
        if step < far:
            ups = [plus(up, part[far - step]) for up, part in zip(ups, parts)]
        if step < far - 1:
            downs = [plus(down, part[far + 1 + step]) for down, part in zip(downs, parts)]
    totals = [
        part[0].astype(jnp.float32) + up.astype(jnp.float32) + down.astype(jnp.float32)
        for part, up, down in zip(parts, ups, downs)
    ]
    return totals, done


def gather(own, depth, token):
    far = depth // 2
    routes = [(CORES * z, CORES * ((z + 1) % depth)) for z in range(depth)]
    routes += [(CORES * z + 1, CORES * ((z - 1) % depth) + 1) for z in range(depth)]
    near, rest = [own], []
    held = jnp.concatenate([own, swap(own, "core")], axis=0)
    for step in range(1, far + 1):
        held = lax.ppermute(held if step < far else held[: own.shape[0]], ("z", "core"), routes)
        (near if step <= far // 2 else rest).append(held)
    near = jnp.concatenate(near, axis=0)
    rest = jnp.concatenate(rest, axis=0)
    near_away, token = lax.optimization_barrier((swap(near, "y"), token))
    mine = [near, rest, near_away, swap(rest, "y")]
    return mine + [swap(block, "core") for block in mine], token


def plus(one, two):
    return (one.astype(jnp.float32) + two.astype(jnp.float32)).astype(jnp.bfloat16)


def shards(frames, conv_weight, qkv_weight, out_weight, cotangent):
    rows = frames.shape[0]
    depth = lax.axis_size("z")

    low, high = edges(frames)
    cot_other = swap(cotangent, "core")
    conv_own, conv_panel = conv(frames, low, high, conv_weight)
    conv_other = swap(conv_own, "core")
    queries, grads = project(conv_own, conv_other, cotangent, cot_other, qkv_weight, out_weight)
    panels, queries = gather(conv_panel, depth, queries)
    att, gq, early, late, part = attention(queries, grads, panels, qkv_weight, depth)

    att_other = swap(att, "core")
    gq_other = swap(gq[rows:], "core")

    totals, (sums, (mixed, base)) = ring_sums(
        (early, late),
        depth,
        (
            lambda sent: weights(
                panels, att, att_other, gq, conv_own, conv_other, cotangent, cot_other, part
            ),
            lambda sent: mixing(
                att, att_other, gq, lax.optimization_barrier((gq_other, sent))[0], out_weight, qkv_weight
            ),
        ),
    )
    scattered = lax.psum_scatter(sums, "z", scatter_dimension=0, tiled=True)

    panel_sums = jnp.concatenate([total.astype(jnp.bfloat16) for total in totals], axis=-1)
    panel_sums = panel_sums.reshape(PLANES, -1, 2 * HALF)
    share = panel_sums.shape[1] // CORES
    panel_parts = (panel_sums[0, :share],) + partners(
        panel_sums[0, share:], panel_sums[1, :share], panel_sums[1, share:]
    )
    grad_conv, taps = tail(base, panel_parts, qkv_weight, frames, low, high)
    x_grad = back(grad_conv, *edges(grad_conv), conv_weight)

    taps = taps + sum(partners(taps, taps, taps))
    for step, route in enumerate(doubling(depth)):
        taps = taps + lax.ppermute(taps, "z", route)
        if step == 1:
            scattered, x_grad, taps = lax.optimization_barrier((scattered, x_grad, taps))
    conv_weight_grad = taps[:TAPS]

    own, *others = pick(scattered)
    parts = (own,) + partners(*others)
    qkv_weight_grad, out_weight_grad = finish(parts)
    return (mixed, x_grad, qkv_weight_grad, out_weight_grad, conv_weight_grad)


def solution(mesh):
    clips, tall = mesh.devices.shape
    grid = Mesh(
        mesh.devices.reshape(clips, tall // (PLANES * CORES), PLANES, CORES), ("clip", "z", "y", "core")
    )
    rows = P(("clip",) + TALL, None)
    in_specs = (rows, P(), P(), P(), rows)
    out_specs = (rows, rows, rows, rows, P("clip", None))
    return jax.shard_map(shards, mesh=grid, in_specs=in_specs, out_specs=out_specs, check_vma=False)
```

```python
import functools

import jax
import jax.numpy as jnp
from jax import lax
from jax.experimental import pallas as pl
from jax.experimental.pallas import tpu as pltpu
from jax.sharding import Mesh
from jax.sharding import PartitionSpec as P

D = 1024
HEADS = 8
HEAD_DIM = 128
TAPS = 5
GAP = 2
STRIDE = 8
REACH = GAP * (TAPS // 2)
EDGE = 16
CORES = 2
PLANES = 2
OWN = HEADS // CORES
HALF = OWN * HEAD_DIM
SCALE = 1.0 / HEAD_DIM**0.5
LOG2E = 1.4426950408889634
TALL = ("z", "y", "core")
SWAP = [(0, 1), (1, 0)]

NN = (((1,), (0,)), ((), ()))
NT = (((1,), (1,)), ((), ()))
TN = (((0,), (0,)), ((), ()))


def mm(a, b, dims=NN):
    return lax.dot_general(a, b, dims, preferred_element_type=jnp.float32)


def params(mib):
    return pltpu.CompilerParams(vmem_limit_bytes=mib * 1024 * 1024)


HBM = pl.BlockSpec(memory_space=pltpu.HBM)


def fetch(pairs, sems):
    copies = [pltpu.make_async_copy(source, target, sems.at[at]) for at, (source, target) in enumerate(pairs)]
    for copy in copies:
        copy.start()
    return copies


def stacked(blocks, target):
    at, pairs = 0, []
    for block in blocks:
        pairs.append((block, target.at[at : at + block.shape[0]]))
        at += block.shape[0]
    return pairs


def whole(shape):
    return pl.BlockSpec(shape, lambda *_: (0,) * len(shape))


def conv_kernel(frames, low, high, weight, conv_out, conv_panel, framed, total):
    rows = frames.shape[0]
    framed[:EDGE] = low[...].astype(jnp.float32)
    framed[EDGE : EDGE + rows] = frames[...].astype(jnp.float32)
    framed[EDGE + rows :] = high[...].astype(jnp.float32)
    acc = None
    for tap in range(TAPS):
        start = EDGE - REACH + GAP * tap
        term = weight[tap : tap + 1, :] * framed[start : start + rows, :]
        acc = term if acc is None else acc + term
    conv_out[...] = acc.astype(jnp.bfloat16)
    for chunk in range(D // HEAD_DIM):
        cols = slice(chunk * HEAD_DIM, (chunk + 1) * HEAD_DIM)
        total[chunk] = acc[:, cols]
        picked = total[chunk, pl.ds(0, rows // STRIDE, stride=STRIDE), :]
        conv_panel[:, cols] = picked.astype(jnp.bfloat16)


def conv(frames, low, high, weight):
    rows = frames.shape[0]
    return pl.pallas_call(
        conv_kernel,
        out_shape=(
            jax.ShapeDtypeStruct((rows, D), jnp.bfloat16),
            jax.ShapeDtypeStruct((rows // STRIDE, D), jnp.bfloat16),
        ),
        scratch_shapes=[
            pltpu.VMEM((rows + 2 * EDGE, D), jnp.float32),
            pltpu.VMEM((D // HEAD_DIM, rows, HEAD_DIM), jnp.float32),
        ],
        compiler_params=params(16),
        name="conv",
    )(frames, low, high, weight)


def project_kernel(
    conv_own, conv_other, cot_own, cot_other, qkv_weight, out_weight, queries, grads, cot_rows, wide, tall, sems
):
    rows = conv_own.shape[0]
    core = lax.axis_index("core")
    start = pl.multiple_of(core * HALF, HALF)
    copies = fetch(
        (
            (qkv_weight.at[:, pl.ds(start, HALF)], wide),
            (out_weight.at[pl.ds(start, HALF), :], tall),
            (cot_own, cot_rows),
        ),
        sems,
    )
    copies[0].wait()
    queries[:rows, :] = mm(conv_own[...], wide[...]).astype(jnp.bfloat16)
    queries[rows:, :] = mm(conv_other[...], wide[...]).astype(jnp.bfloat16)
    copies[1].wait()
    grads[rows:, :] = mm(cot_other[...], tall[...], NT).astype(jnp.bfloat16)
    copies[2].wait()
    grads[:rows, :] = mm(cot_rows[...], tall[...], NT).astype(jnp.bfloat16)


def project(conv_own, conv_other, cot_own, cot_other, qkv_weight, out_weight):
    rows = conv_own.shape[0]
    vmem = pl.BlockSpec(memory_space=pltpu.VMEM)
    out = jax.ShapeDtypeStruct((2 * rows, HALF), jnp.bfloat16)
    return pl.pallas_call(
        project_kernel,
        in_specs=[vmem, vmem, HBM, vmem, HBM, HBM],
        out_shape=(out, out),
        scratch_shapes=[
            pltpu.VMEM((rows, D), jnp.bfloat16),
            pltpu.VMEM((D, HALF), jnp.bfloat16),
            pltpu.VMEM((HALF, D), jnp.bfloat16),
            pltpu.SemaphoreType.DMA((3,)),
        ],
        compiler_params=params(50),
        cost_estimate=pl.CostEstimate(flops=2_000_000_000, bytes_accessed=6_000_000, transcendentals=0),
        name="project",
    )(conv_own, conv_other, cot_own, cot_other, qkv_weight, out_weight)


def batches(depth):
    far = depth // 2
    near, rest = [(0, 0)], []
    for step in range(1, far):
        (near if step <= far // 2 else rest).extend((step, core) for core in range(CORES))
    rest.append((far, 0))
    return near, rest


def attention_kernel(depth, queries, grads, *refs):
    panels, rest = refs[:8], refs[8:]
    qkv_weight, att, gq, early, late, part, keys, values, panel, weight, sems, weight_sems = rest
    head = pl.program_id(0)
    core = lax.axis_index("core")

    def columns(at, kind):
        start = pl.multiple_of((kind * HEADS + core * OWN + at) * HEAD_DIM, HEAD_DIM)
        return pltpu.make_async_copy(
            qkv_weight.at[:, pl.ds(start, HEAD_DIM)],
            weight.at[at, :, pl.ds((kind - 1) * HEAD_DIM, HEAD_DIM)],
            weight_sems.at[at, kind - 1],
        )

    @pl.when(head == 0)
    def _():
        copies = fetch(stacked(panels, panel), sems)
        for at in range(OWN):
            for kind in (1, 2):
                columns(at, kind).start()
        for copy in copies:
            copy.wait()

    for kind in (1, 2):
        columns(head, kind).wait()
    both = mm(panel[...], weight[head]).astype(jnp.bfloat16)
    keys[...] = both[:, :HEAD_DIM]
    values[...] = both[:, HEAD_DIM:]
    query, grad = queries[...], grads[...]
    scores = mm(keys[...], query, NT)
    highest = jnp.max(scores, axis=0, keepdims=True)
    raised = jnp.exp2((scores - highest) * (SCALE * LOG2E))
    probs = raised * (1.0 / jnp.sum(raised, axis=0, keepdims=True))
    weights = probs.astype(jnp.bfloat16)
    attended = mm(values[...], weights, TN).astype(jnp.bfloat16)
    grad_t = grad.astype(jnp.float32).T
    delta = jnp.sum(grad_t * attended.astype(jnp.float32), axis=0, keepdims=True)
    dprob = mm(values[...], grad, NT)
    grad_scores = (probs * (dprob - delta)).astype(jnp.bfloat16)
    att[...] = attended.astype(jnp.float32).T.astype(jnp.bfloat16)
    gq[...] = (mm(keys[...], grad_scores, TN) * SCALE).T.astype(jnp.bfloat16)
    part[:, :HEAD_DIM] = (mm(grad_scores, query) * SCALE).astype(jnp.bfloat16)
    part[:, HEAD_DIM:] = mm(weights, grad).astype(jnp.bfloat16)

    piece = early.shape[3]
    sign = 2 * core - 1

    def store(out):
        at = 0
        for lane in range(CORES):
            for plane in range(PLANES):
                for batch in batches(depth):
                    for step, sender in batch:
                        steps = step * (1 - 2 * lane)
                        ahead = lax.rem(depth + sign * steps, depth)
                        out[ahead, plane, sender ^ lane] = part[at : at + piece, :]
                        at += piece

    @pl.when(head < OWN // 2)
    def _():
        store(early)

    @pl.when(head >= OWN // 2)
    def _():
        store(late)


def attention(queries, grads, panels, qkv_weight, depth):
    tokens = queries.shape[0]
    total = sum(block.shape[0] for block in panels)
    piece = total // depth // PLANES // CORES
    wide = 2 * HEAD_DIM
    head = pl.BlockSpec((tokens, HEAD_DIM), lambda h: (0, h))
    shape = (depth, PLANES, CORES, piece, wide)
    parts = jax.ShapeDtypeStruct(shape[:-1] + (HALF,), jnp.bfloat16)
    return pl.pallas_call(
        functools.partial(attention_kernel, depth),
        grid=(OWN,),
        in_specs=[head, head] + [HBM] * len(panels) + [HBM],
        out_specs=[
            head,
            head,
            pl.BlockSpec(shape, lambda h: (0, 0, 0, 0, jnp.minimum(h, OWN // 2 - 1))),
            pl.BlockSpec(shape, lambda h: (0, 0, 0, 0, jnp.maximum(h - OWN // 2, 0))),
            pl.BlockSpec((total, wide), lambda h: (0, h)),
        ],
        scratch_shapes=[
            pltpu.VMEM((total, HEAD_DIM), jnp.bfloat16),
            pltpu.VMEM((total, HEAD_DIM), jnp.bfloat16),
            pltpu.VMEM((total, D), jnp.bfloat16),
            pltpu.VMEM((OWN, D, wide), jnp.bfloat16),
            pltpu.SemaphoreType.DMA((len(panels),)),
            pltpu.SemaphoreType.DMA((OWN, 2)),
        ],
        out_shape=(
            jax.ShapeDtypeStruct((tokens, HALF), jnp.bfloat16),
            jax.ShapeDtypeStruct((tokens, HALF), jnp.bfloat16),
            parts,
            parts,
            jax.ShapeDtypeStruct((total, 2 * HALF), jnp.bfloat16),
        ),
        compiler_params=params(44),
        cost_estimate=pl.CostEstimate(flops=8_000_000_000, bytes_accessed=16_000_000, transcendentals=2_000_000),
        name="attention",
    )(queries, grads, *panels, qkv_weight)


def weights_kernel(depth, att, att_other, gq, conv_own, conv_other, cot_own, cot_other, part, *refs):
    panels, (sums, panel, sems) = refs[:8], refs[8:]
    core, plane = lax.axis_index("core"), lax.axis_index("y")
    rows = conv_own.shape[0]
    own, away = halves()
    size = D // depth // PLANES // CORES

    def store(value, first, cols):
        for at in range(0, value.shape[0], size):
            block = first + at // size
            other_core, other_plane = lax.rem(block + core, CORES), lax.rem(block // CORES + plane, PLANES)
            to = (block // (PLANES * CORES) * PLANES + other_plane) * CORES + other_core
            sums[pl.ds(pl.multiple_of(to * size, size), size), cols] = value[at : at + size].astype(jnp.bfloat16)

    @pl.when(pl.program_id(0) == 0)
    def _():
        for copy in fetch(stacked(panels, panel), sems):
            copy.wait()
        store(mm(panel[...], part[...], TN), 0, slice(None))

    @pl.when(pl.program_id(0) == 1)
    def _():
        queries = mm(conv_own[...], gq[:rows, :], TN) + mm(conv_other[...], gq[rows:, :], TN)
        store(queries, 0, slice(0, HALF))
        mine = mm(att[:rows, :], cot_own[:, own], TN) + mm(att[rows:, :], cot_other[:, own], TN)
        store(mine, core * (HALF // size), slice(HALF, D))
        other = mm(att_other[rows:, :], cot_own[:, own], TN) + mm(att_other[:rows, :], cot_other[:, own], TN)
        store(other, (1 - core) * (HALF // size), slice(HALF, D))


def weights(depth, panels, *ins):
    total = sum(block.shape[0] for block in panels)
    return pl.pallas_call(
        functools.partial(weights_kernel, depth),
        grid=(2,),
        in_specs=[whole(item.shape) for item in ins] + [HBM] * len(panels),
        out_specs=pl.BlockSpec((D, D), lambda i: (0, i)),
        scratch_shapes=[pltpu.VMEM((total, D), jnp.bfloat16), pltpu.SemaphoreType.DMA((len(panels),))],
        out_shape=jax.ShapeDtypeStruct((D, 2 * D), jnp.bfloat16),
        compiler_params=params(45),
        cost_estimate=pl.CostEstimate(flops=4_000_000_000, bytes_accessed=12_000_000, transcendentals=0),
        name="weights",
    )(*ins, *panels)


def mixing_kernel(att, att_other, gq, gq_other, out_weight, qkv_weight, mixed, base, first, second, sems):
    core = lax.axis_index("core")
    rows = mixed.shape[0]
    own = pl.ds(pl.multiple_of(core * HALF, HALF), HALF)
    away = pl.ds(pl.multiple_of((1 - core) * HALF, HALF), HALF)
    copies = fetch(((out_weight, first), (qkv_weight.at[:, pl.ds(0, D)], second)), sems)
    copies[0].wait()
    blend = mm(att[:rows, :], first[own, :]) + mm(att_other[rows:, :], first[away, :])
    mixed[...] = blend.astype(jnp.bfloat16)
    copies[1].wait()
    base[...] = mm(gq[:rows, :], second[:, own], NT) + mm(gq_other[...], second[:, away], NT)


def mixing(att, att_other, gq, gq_other, out_weight, qkv_weight):
    rows = gq_other.shape[0]
    vmem = pl.BlockSpec(memory_space=pltpu.VMEM)
    return pl.pallas_call(
        mixing_kernel,
        in_specs=[vmem] * 4 + [HBM] * 2,
        out_shape=(
            jax.ShapeDtypeStruct((rows, D), jnp.bfloat16),
            jax.ShapeDtypeStruct((rows, D), jnp.float32),
        ),
        scratch_shapes=[
            pltpu.VMEM((D, D), jnp.bfloat16),
            pltpu.VMEM((D, D), jnp.bfloat16),
            pltpu.SemaphoreType.DMA((2,)),
        ],
        compiler_params=params(50),
        cost_estimate=pl.CostEstimate(flops=1_000_000_000, bytes_accessed=8_000_000, transcendentals=0),
        name="mixing",
    )(att, att_other, gq, gq_other, out_weight, qkv_weight)


def by_kind(block):
    pieces = [block[:, at : at + HEAD_DIM] for at in range(0, block.shape[1], HEAD_DIM)]
    return jnp.concatenate(pieces[0::2], axis=1), jnp.concatenate(pieces[1::2], axis=1)


def halves():
    core = lax.axis_index("core")
    return [pl.ds(pl.multiple_of(at * HALF, HALF), HALF) for at in (core, 1 - core)]


def tail_kernel(
    base, own, other, own_away, other_away, qkv_weight, frames, low, high, grad_out, taps, framed, total, weight, sems
):
    rows = frames.shape[0]
    copies = fetch([(qkv_weight.at[:, pl.ds(D * at, D)], weight.at[at - 1]) for at in (1, 2)], sems)
    framed[:EDGE] = low[...].astype(jnp.float32)
    framed[EDGE : EDGE + rows] = frames[...].astype(jnp.float32)
    framed[EDGE + rows :] = high[...].astype(jnp.float32)
    kinds = [by_kind(plus(own[...], own_away[...])), by_kind(plus(other[...], other_away[...]))]
    extra = None
    for kind in range(2):
        copies[kind].wait()
        for block, cols in zip(kinds, halves()):
            term = mm(block[kind], weight[kind, :, cols], NT)
            extra = term if extra is None else extra + term
    for chunk in range(D // HEAD_DIM):
        cols = slice(chunk * HEAD_DIM, (chunk + 1) * HEAD_DIM)
        total[chunk] = base[:, cols]
        at = (chunk, pl.ds(0, rows // STRIDE, stride=STRIDE), slice(None))
        total[at] = total[at] + extra[:, cols]
        grad = total[chunk].astype(jnp.bfloat16)
        grad_out[:, cols] = grad
        grad = grad.astype(jnp.float32)
        for tap in range(TAPS):
            start = EDGE - REACH + GAP * tap
            term = grad * framed[start : start + rows, cols]
            taps[tap : tap + 1, cols] = jnp.sum(term, axis=0, keepdims=True)
    taps[TAPS:, :] = jnp.zeros((taps.shape[0] - TAPS, D), jnp.float32)


def tail(base, panel_parts, qkv_weight, frames, low, high):
    rows = frames.shape[0]
    vmem = pl.BlockSpec(memory_space=pltpu.VMEM)
    return pl.pallas_call(
        tail_kernel,
        in_specs=[vmem] * 5 + [HBM] + [vmem] * 3,
        out_shape=(
            jax.ShapeDtypeStruct((rows, D), jnp.bfloat16),
            jax.ShapeDtypeStruct((8, D), jnp.float32),
        ),
        scratch_shapes=[
            pltpu.VMEM((rows + 2 * EDGE, D), jnp.float32),
            pltpu.VMEM((D // HEAD_DIM, rows, HEAD_DIM), jnp.float32),
            pltpu.VMEM((2, D, D), jnp.bfloat16),
            pltpu.SemaphoreType.DMA((2,)),
        ],
        compiler_params=params(50),
        cost_estimate=pl.CostEstimate(flops=20_000_000_000, bytes_accessed=8_000_000, transcendentals=0),
        name="tail",
    )(base, *panel_parts, qkv_weight, frames, low, high)


def finish_kernel(own, other, qkv_grad, out_grad):
    for block, cols in zip((own, other), halves()):
        keys, values = by_kind(block[:, :D])
        qkv_grad[:, cols] = block[:, D : D + HALF]
        qkv_grad[:, pl.ds(cols.start + D, HALF)] = keys
        qkv_grad[:, pl.ds(cols.start + 2 * D, HALF)] = values
        out_grad[:, cols] = block[:, D + HALF :]


def finish(own, other):
    rows = own.shape[0]
    return pl.pallas_call(
        finish_kernel,
        out_shape=(
            jax.ShapeDtypeStruct((rows, 3 * D), jnp.float32),
            jax.ShapeDtypeStruct((rows, D), jnp.float32),
        ),
        compiler_params=params(16),
        cost_estimate=pl.CostEstimate(flops=3_000_000_000, bytes_accessed=1_000_000, transcendentals=0),
        name="finish",
    )(own, other)


def back_kernel(grad, low, high, weight, out, framed):
    rows = grad.shape[0]
    framed[:EDGE] = low[...].astype(jnp.float32)
    framed[EDGE : EDGE + rows] = grad[...].astype(jnp.float32)
    framed[EDGE + rows :] = high[...].astype(jnp.float32)
    acc = None
    for tap in range(TAPS):
        start = EDGE + REACH - GAP * tap
        term = weight[tap : tap + 1, :] * framed[start : start + rows, :]
        acc = term if acc is None else acc + term
    out[...] = acc.astype(jnp.bfloat16)


def back(grad, low, high, weight):
    rows = grad.shape[0]
    return pl.pallas_call(
        back_kernel,
        out_shape=jax.ShapeDtypeStruct((rows, D), jnp.bfloat16),
        scratch_shapes=[pltpu.VMEM((rows + 2 * EDGE, D), jnp.float32)],
        compiler_params=params(16),
        name="back",
    )(grad, low, high, weight)


def swap(block, axis):
    return lax.ppermute(block, axis, SWAP)


def partners(core_block, plane_block, both_block):
    both = [(PLANES * CORES - 1 - at, at) for at in range(PLANES * CORES)]
    return (
        swap(core_block, "core"),
        swap(plane_block, "y"),
        lax.ppermute(both_block, ("y", "core"), both),
    )


def doubling(depth):
    pairs = [(z, z ^ 1) for z in range(depth)]
    across = [(z, (z + 1) % depth if z % 2 else (z - 1) % depth) for z in range(depth)]
    far = [(z, (7 - z) % depth if z in (1, 2, 5, 6) else (3 - z) % depth) for z in range(depth)]
    return (pairs, across, far) if depth == 8 else (pairs, across)


def edges(block):
    count = lax.axis_size(TALL)
    up = [(i, i + 1) for i in range(count - 1)]
    down = [(i + 1, i) for i in range(count - 1)]
    return lax.ppermute(block[-EDGE:], TALL, up), lax.ppermute(block[:EDGE], TALL, down)


def ring_sums(parts, depth, beside):
    ahead = [(i, (i + 1) % depth) for i in range(depth)]
    behind = [(i, (i - 1) % depth) for i in range(depth)]
    far = depth // 2
    ups, downs = [part[far] for part in parts], [part[far + 1] for part in parts]
    done = []
    for step in range(1, far + 1):
        sent = ups[0]
        ups = [lax.ppermute(up, "z", ahead) for up in ups]
        if step < far:
            downs = [lax.ppermute(down, "z", behind) for down in downs]
        if step <= len(beside):
            result = beside[step - 1](sent)
            parts, result = lax.optimization_barrier((parts, result))
            done.append(result)
        if step < far:
            ups = [plus(up, part[far - step]) for up, part in zip(ups, parts)]
        if step < far - 1:
            downs = [plus(down, part[far + 1 + step]) for down, part in zip(downs, parts)]
    totals = [
        part[0].astype(jnp.float32) + up.astype(jnp.float32) + down.astype(jnp.float32)
        for part, up, down in zip(parts, ups, downs)
    ]
    return totals, done


def gather(own, depth, token):
    far = depth // 2
    routes = [(CORES * z, CORES * ((z + 1) % depth)) for z in range(depth)]
    routes += [(CORES * z + 1, CORES * ((z - 1) % depth) + 1) for z in range(depth)]
    near, rest = [own], []
    held = jnp.concatenate([own, swap(own, "core")], axis=0)
    for step in range(1, far + 1):
        held = lax.ppermute(held if step < far else held[: own.shape[0]], ("z", "core"), routes)
        (near if step <= far // 2 else rest).append(held)
    near = jnp.concatenate(near, axis=0)
    rest = jnp.concatenate(rest, axis=0)
    near_away, token = lax.optimization_barrier((swap(near, "y"), token))
    mine = [near, rest, near_away, swap(rest, "y")]
    return mine + [swap(block, "core") for block in mine], token


def plus(one, two):
    return (one.astype(jnp.float32) + two.astype(jnp.float32)).astype(jnp.bfloat16)


def shards(frames, conv_weight, qkv_weight, out_weight, cotangent):
    rows = frames.shape[0]
    depth = lax.axis_size("z")

    low, high = edges(frames)
    cot_other = swap(cotangent, "core")
    conv_own, conv_panel = conv(frames, low, high, conv_weight)
    conv_other = swap(conv_own, "core")
    queries, grads = project(conv_own, conv_other, cotangent, cot_other, qkv_weight, out_weight)
    panels, queries = gather(conv_panel, depth, queries)
    att, gq, early, late, part = attention(queries, grads, panels, qkv_weight, depth)

    att_other = swap(att, "core")
    gq_other = swap(gq[rows:], "core")

    totals, (sums, (mixed, base)) = ring_sums(
        (early, late),
        depth,
        (
            lambda sent: weights(
                depth, panels, att, att_other, gq, conv_own, conv_other, cotangent, cot_other, part
            ),
            lambda sent: mixing(
                att, att_other, gq, lax.optimization_barrier((gq_other, sent))[0], out_weight, qkv_weight
            ),
        ),
    )
    scattered = lax.psum_scatter(sums, "z", scatter_dimension=0, tiled=True)

    panel_sums = jnp.concatenate([total.astype(jnp.bfloat16) for total in totals], axis=-1)
    panel_sums = panel_sums.reshape(PLANES, -1, 2 * HALF)
    share = panel_sums.shape[1] // CORES
    panel_parts = (panel_sums[0, :share],) + partners(
        panel_sums[0, share:], panel_sums[1, :share], panel_sums[1, share:]
    )
    grad_conv, taps = tail(base, panel_parts, qkv_weight, frames, low, high)
    x_grad = back(grad_conv, *edges(grad_conv), conv_weight)

    taps = taps + swap(taps, "core")
    taps = taps + swap(taps, "y")
    scattered, x_grad, taps = lax.optimization_barrier((scattered, x_grad, taps))
    for route in doubling(depth):
        taps = taps + lax.ppermute(taps, "z", route)
    conv_weight_grad = taps[:TAPS]

    half = scattered.shape[0] // PLANES
    summed = scattered[:half].astype(jnp.float32) + swap(scattered[half:], "y").astype(jnp.float32)
    own, other = summed[: half // CORES], swap(summed[half // CORES :], "core")
    qkv_weight_grad, out_weight_grad = finish(own, other)
    return (mixed, x_grad, qkv_weight_grad, out_weight_grad, conv_weight_grad)


def solution(mesh):
    clips, tall = mesh.devices.shape
    grid = Mesh(
        mesh.devices.reshape(clips, tall // (PLANES * CORES), PLANES, CORES), ("clip", "z", "y", "core")
    )
    rows = P(("clip",) + TALL, None)
    in_specs = (rows, P(), P(), P(), rows)
    out_specs = (rows, rows, rows, rows, P("clip", None))
    return jax.shard_map(shards, mesh=grid, in_specs=in_specs, out_specs=out_specs, check_vma=False)
```
